128 devices in a mesh: group: 16 (over x, y), mp: 8 (over z, core).
Axes of the slice: x: 4, y: 4, z: 4, core: 2. Of those that a mesh axis runs over, the one named last changes fastest.
Arguments:
- node_features: bfloat16 [768, 262144], P('mp', 'group'), may hold values from -6 to 6
- target_nodes: int32 [16, 256], replicated, may hold values from 0 to 262143
- first_hop: int32 [16, 25, 256], replicated, may hold values from 0 to 262143
- live_counts: int32 [16], P('group'), may hold values from 64 to 256, as said below
- seed_links: int32 [16, 32, 15], P('group'), may hold values from 0 to 255, as said below
- seed_labels: int32 [16, 32], P('group'), may hold values from 0 to 152
- self_weight: bfloat16 [768, 1024], P('mp'), may hold values from -0.21875 to 0.21875
- neigh_weight: bfloat16 [768, 1024], P('mp'), may hold values from -0.21875 to 0.21875
- hidden_bias: float32 [1024], P('mp'), may hold values from -3 to 3
- class_self: bfloat16 [1024, 153], P('mp'), may hold values from -0.1875 to 0.1875
- class_neigh: bfloat16 [1024, 153], P('mp'), may hold values from -0.1875 to 0.1875
- class_bias: float32 [153], replicated, may hold values from -4 to 4
Outputs:
- hidden_layer: bfloat16 [4096, 1024], P('group', 'mp')
- grad_self: float32 [768, 1024], P('mp')
- grad_neigh: float32 [768, 1024], P('mp')
- grad_hbias: float32 [1024], P('mp')
- grad_cself: float32 [1024, 153], P('mp')
- grad_cneigh: float32 [1024, 153], P('mp')
- grad_cbias: float32 [153], replicated
- mean_loss: float32 [], replicated
The draws below stay inside these ranges and needn't reach their ends.
Inputs may be any that keep to these rules, and one draw needn't show every extreme that they name: live_counts[b] target slots of batch b are live; slots 0 to 31 are its seeds; slots at or beyond live_counts[b] are padding whose ids carry no meaning; some batch is full. seed_links[b, s, k] < live_counts[b].
All inputs are finite; a program needn't handle non-finite values.
Results may differ from the reference program's by a relative error of at most 0.0095.
Values sent between devices are 32-bit elements; how exact they have to be, the bound alone decides.
A program may use at most 128 MiB of HBM per device.

```python
import jax
import jax.numpy as jnp
from jax import lax

FEAT = 768
HIDDEN_SIZE = 1024
CLASSES = 153
FAN_ONE = 25
FAN_TWO = 15
TARGETS = 256
SEEDS = 32
BATCHES = 16
NODES = 262144


def shared_counts(key):
    lower_key, full_key = jax.random.split(key)
    lowest = max(SEEDS, TARGETS // 4)
    counts = jax.random.randint(lower_key, (BATCHES,), lowest, TARGETS + 1)
    full_batch = jax.random.randint(full_key, (), 0, BATCHES)
    return jnp.where(jnp.arange(BATCHES) == full_batch, TARGETS, counts).astype(jnp.int32)


def draw_live_counts(key, part):
    return shared_counts(key)


def draw_seed_links(key, part):
    counts = shared_counts(key)
    key = jax.random.fold_in(key, 7)
    entries = jax.random.randint(key, (BATCHES, SEEDS, FAN_TWO), 0, counts[:, None, None])
    entries = entries.at[:, SEEDS - 1, FAN_TWO - 1].set(counts - 1)
    return entries.astype(jnp.int32)


def place_ends(drawn, stream_key, smallest, top_value):
    spot = [jax.random.randint(jax.random.fold_in(stream_key, axis), (), 0, length) for axis, length in enumerate(drawn.shape)]
    longest = drawn.shape.index(max(drawn.shape))
    neighbour = spot[:longest] + [(spot[longest] + 1) % drawn.shape[longest]] + spot[longest + 1:]
    return drawn.at[tuple(spot)].set(smallest).at[tuple(neighbour)].set(top_value)


def block_scale(key, dims, shards, low, high):
    level = 1.0
    for axis_at, parts in shards:
        heights = jax.random.uniform(jax.random.fold_in(jax.random.fold_in(key, 6), axis_at), (parts,), jnp.float32, low / len(shards), high / len(shards))
        level = level * jnp.repeat(jnp.exp(heights), dims[axis_at] // parts).reshape((-1,) + (1,) * (len(dims) - 1 - axis_at))
    return level


def centred(stream_key, shape, scale, limit, cuts=(), kind=jnp.bfloat16):
    gain = block_scale(stream_key, shape, cuts, -0.22, 0.18) if cuts else 1.0
    drawn = jax.random.normal(stream_key, shape, jnp.float32) * scale * gain
    return jnp.minimum(jnp.maximum(drawn, -limit), limit).astype(kind)


def setup_inputs(seed: int = 0) -> dict:
    key_list = jax.random.split(jax.random.key(seed), 13)
    return {
        "node_features": centred(key_list[0], (FEAT, NODES), 1.0, 6.0, ((0, 8), (1, 16))),
        "target_nodes": place_ends(jax.random.randint(key_list[1], (BATCHES, TARGETS), 0, NODES), jax.random.fold_in(key_list[1], 1), 0, NODES - 1).astype(jnp.int32),
        "first_hop": place_ends(jax.random.randint(key_list[2], (BATCHES, FAN_ONE, TARGETS), 0, NODES), jax.random.fold_in(key_list[2], 1), 0, NODES - 1).astype(jnp.int32),
        "live_counts": draw_live_counts(jax.random.fold_in(key_list[12], 71), 0),
        "seed_links": draw_seed_links(jax.random.fold_in(key_list[12], 71), 0),
        "seed_labels": place_ends(jax.random.randint(key_list[5], (BATCHES, SEEDS), 0, CLASSES), jax.random.fold_in(key_list[5], 1), 0, CLASSES - 1).astype(jnp.int32),
        "self_weight": centred(key_list[6], (FEAT, HIDDEN_SIZE), FEAT ** -0.5, 0.21875, ((0, 8),)),
        "neigh_weight": centred(key_list[7], (FEAT, HIDDEN_SIZE), FEAT ** -0.5, 0.21875, ((0, 8),)),
        "hidden_bias": centred(key_list[8], (HIDDEN_SIZE,), 0.5, 3.0, ((0, 8),), jnp.float32),
        "class_self": centred(key_list[9], (HIDDEN_SIZE, CLASSES), HIDDEN_SIZE ** -0.5, 0.1875, ((0, 8),)),
        "class_neigh": centred(key_list[10], (HIDDEN_SIZE, CLASSES), HIDDEN_SIZE ** -0.5, 0.1875, ((0, 8),)),
        "class_bias": centred(key_list[11], (CLASSES,), 1.0, 4.0, (), jnp.float32),
    }


def reference(node_features, target_nodes, first_hop, live_counts, seed_links, seed_labels, self_weight, neigh_weight, hidden_bias, class_self, class_neigh, class_bias):
    high = lax.Precision.HIGHEST
    table = node_features.T
    self_rows = table[target_nodes].astype(jnp.float32)
    neigh_rows = jnp.sum(table[first_hop].astype(jnp.float32), axis=1) / FAN_ONE
    pre = (jnp.einsum("btf,fh->bth", self_rows, self_weight.astype(jnp.float32), precision=high)
           + jnp.einsum("btf,fh->bth", neigh_rows, neigh_weight.astype(jnp.float32), precision=high)
           + hidden_bias)
    live = jnp.arange(TARGETS, dtype=jnp.int32)[None, :] < live_counts[:, None]
    hidden_layer = jnp.where(live[:, :, None], jnp.maximum(pre, 0.0), 0.0).astype(jnp.bfloat16)
    active = hidden_layer.astype(jnp.float32)
    seed_self = active[:, :SEEDS]
    flat_links = seed_links.reshape(BATCHES, SEEDS * FAN_TWO)
    picked = jnp.take_along_axis(active, flat_links[:, :, None], axis=1)
    seed_neigh = jnp.sum(picked.reshape(BATCHES, SEEDS, FAN_TWO, HIDDEN_SIZE), axis=2) / FAN_TWO
    cself = class_self.astype(jnp.float32)
    cneigh = class_neigh.astype(jnp.float32)
    logits = (jnp.einsum("bsh,hc->bsc", seed_self, cself, precision=high)
              + jnp.einsum("bsh,hc->bsc", seed_neigh, cneigh, precision=high) + class_bias)
    log_total = jnp.log(jnp.sum(jnp.exp(logits), axis=-1, keepdims=True))
    onehot = (seed_labels[:, :, None] == jnp.arange(CLASSES, dtype=jnp.int32)[None, None, :]).astype(jnp.float32)
    losses = log_total[:, :, 0] - jnp.sum(onehot * logits, axis=-1)
    mean_loss = jnp.mean(losses)
    dlogit = jnp.exp(logits - log_total) - onehot
    grad_cbias = jnp.sum(dlogit, axis=(0, 1))
    grad_cself = jnp.einsum("bsh,bsc->hc", seed_self, dlogit, precision=high)
    grad_cneigh = jnp.einsum("bsh,bsc->hc", seed_neigh, dlogit, precision=high)
    back_self = jnp.einsum("bsc,hc->bsh", dlogit, cself, precision=high)
    back_neigh = jnp.einsum("bsc,hc->bsh", dlogit, cneigh, precision=high) / FAN_TWO
    spread = jnp.broadcast_to(back_neigh[:, :, None, :], (BATCHES, SEEDS, FAN_TWO, HIDDEN_SIZE)).reshape(BATCHES, SEEDS * FAN_TWO, HIDDEN_SIZE)
    grad_act = jnp.zeros((BATCHES, TARGETS, HIDDEN_SIZE), jnp.float32).at[:, :SEEDS].add(back_self)

    def scatter_rows(accum, where_to, values):
        return accum.at[where_to].add(values)

    grad_act = jax.vmap(scatter_rows)(grad_act, flat_links, spread)
    grad_pre = jnp.where(live[:, :, None] & (pre > 0), grad_act, 0.0)
    grad_hbias = jnp.sum(grad_pre, axis=(0, 1))
    grad_self = jnp.einsum("btf,bth->fh", self_rows, grad_pre, precision=high)
    grad_neigh = jnp.einsum("btf,bth->fh", neigh_rows, grad_pre, precision=high)
    return (hidden_layer.reshape(BATCHES * TARGETS, HIDDEN_SIZE), grad_self, grad_neigh, grad_hbias, grad_cself, grad_cneigh, grad_cbias, mean_loss)
```

```python
import functools
import jax
import jax.numpy as jnp
from jax import lax
from jax.experimental import pallas as pl
from jax.experimental.pallas import tpu as pltpu
from jax.sharding import PartitionSpec as P

UNROLL = 16

def gather_kernel(feat_ref, ids_ref, out_ref, table, acc, codes, first, counts, first_s, counts_s, extra_s, sems):
    nodes = feat_ref.shape[1]
    width = feat_ref.shape[0]
    chunks = ids_ref.shape[0]
    slots = acc.shape[0] - 8
    half = slots // 2
    per_half = half // 1024
    lane = lax.broadcasted_iota(jnp.int32, (8, 8, 128), 2)
    sub = lax.broadcasted_iota(jnp.int32, (8, 8, 128), 1)
    outer = lax.broadcasted_iota(jnp.int32, (8, 8, 128), 0)
    row_i = lax.broadcasted_iota(jnp.int32, (128, 128), 0)
    col_i = lax.broadcasted_iota(jnp.int32, (128, 128), 1)
    before = jnp.where(row_i < col_i, 1.0, 0.0).astype(jnp.bfloat16)
    ones = jnp.ones((128, 128), jnp.bfloat16)
    shift = (nodes - 1).bit_length()
    flag = 1 << (shift + 10)

    def compact(q, carry):
        local = ids_ref[pl.ds(q * 8, 8)]
        inside = (local >= 0) & (local < nodes)
        out_f = jnp.where(inside, 0.0, 1.0)
        out_b = out_f.reshape(64, 128).astype(jnp.bfloat16)
        pref = jnp.dot(out_b, before, preferred_element_type=jnp.float32).reshape(8, 8, 128)
        total = jnp.dot(out_b, ones, preferred_element_type=jnp.float32).reshape(8, 8, 128)
        scan = jnp.where(sub >= 1, pltpu.roll(total, 1, 1), 0.0)
        for step in (1, 2, 4):
            scan = scan + jnp.where(sub >= step, pltpu.roll(scan, step, 1), 0.0)
        moved = (pref + scan).astype(jnp.int32)
        counts[pl.ds(q * 8, 8), :] = 1024 - jnp.sum(total, axis=1).astype(jnp.int32)
        x = jnp.where(inside, flag | (moved << shift) | local, 0)
        for j in range(10):
            d = 1 << j
            if j < 7:
                y = pltpu.roll(x, 128 - d, 2)
                y = jnp.where(lane < 128 - d, y, pltpu.roll(y, 7, 1))
            else:
                y = pltpu.roll(x, 8 - d // 128, 1)
            bit = 1 << (shift + j)
            x = jnp.where((y & bit) != 0, y, jnp.where((x & bit) != 0, 0, x))
        chunk = q * 8 + outer
        slot = sub * 128 + lane + ((x >> shift) & 1023) + (chunk % per_half) * 1024
        slot = slot + jnp.where(chunk >= chunks - per_half, half, 0)
        code = jnp.where(x != 0, (slot << 15) | (x & (nodes - 1)), (slots << 15) | nodes)
        codes[pl.ds(q * 8, 8)] = code
        first[pl.ds(q * 8, 8), :] = codes[pl.ds(q * 8, 8), 0, :]
        return carry

    lax.fori_loop(0, chunks // 8, compact, 0)
    copy_first = pltpu.make_async_copy(first, first_s, sems.at[0])
    copy_counts = pltpu.make_async_copy(counts, counts_s, sems.at[1])
    copy_first.start()
    copy_counts.start()

    def turn(i, carry):
        at = pl.multiple_of(i * 128, 128)
        block = feat_ref[:, pl.ds(at, 128)].astype(jnp.float32)
        block = jnp.concatenate([block, jnp.zeros((128 - width, 128), jnp.float32)], axis=0)
        table[pl.ds(at, 128), :] = block.T
        return carry

    lax.fori_loop(0, nodes // 128, turn, 0, unroll=4)
    table[pl.ds(nodes, 8), :] = jnp.zeros((8, 128), jnp.float32)

    def clear(i, carry):
        acc[pl.ds(pl.multiple_of(i * 64, 64), 64), :] = jnp.zeros((64, 128), jnp.float32)
        return carry

    lax.fori_loop(0, slots // 64, clear, 0)
    acc[pl.ds(slots, 8), :] = jnp.zeros((8, 128), jnp.float32)
    copy_first.wait()
    copy_counts.wait()

    def add_rows(read, n):
        def group(i, carry):
            code = [read(i * UNROLL + u) for u in range(UNROLL)]
            at = [c >> 15 for c in code]
            rows = [table[pl.ds(c & 32767, 1), :] for c in code]
            olds = [acc[pl.ds(a, 1), :] for a in at]
            for a, old, row in zip(at, olds, rows):
                acc[pl.ds(a, 1), :] = old + row
            return carry

        lax.fori_loop(0, (n + UNROLL - 1) // UNROLL, group, 0)

    def chunk_rows(j, carry):
        n = counts_s[j, 0]
        add_rows(lambda i: first_s[j, i], jnp.minimum(n, 128))

        @pl.when(n > 128)
        def _():
            copy = pltpu.make_async_copy(codes.at[j], extra_s, sems.at[2])
            copy.start()
            copy.wait()

            def rest(r, inner):
                add_rows(lambda i: extra_s[r, i], jnp.minimum(n - r * 128, 128))
                return inner

            lax.fori_loop(1, (n + 127) // 128, rest, 0)

        return carry

    lax.fori_loop(0, chunks, chunk_rows, 0)

    lanes = lax.broadcasted_iota(jnp.int32, (64, 128), 1)

    def pack(i, carry):
        for s in range(2):
            base = (1 - s) * half + i * 256
            a, b, c, d = [acc[pl.ds(pl.multiple_of(base + n * 64, 64), 64), :] for n in range(4)]
            b, c, d = pltpu.roll(b, 96, 1), pltpu.roll(c, 64, 1), pltpu.roll(d, 32, 1)
            out_ref[i, pl.ds(s * 192, 64), :] = jnp.where(lanes < 96, a, b)
            out_ref[i, pl.ds(s * 192 + 64, 64), :] = jnp.where(lanes < 64, b, c)
            out_ref[i, pl.ds(s * 192 + 128, 64), :] = jnp.where(lanes < 32, c, d)
        return carry

    lax.fori_loop(0, half // 256, pack, 0)


def gather_rows(features, local_ids, batches):
    nodes = features.shape[1]
    chunks = local_ids.shape[0]
    return pl.pallas_call(
        gather_kernel,
        out_shape=jax.ShapeDtypeStruct((batches, 384, 128), jnp.float32),
        in_specs=[pl.BlockSpec(memory_space=pltpu.VMEM)] * 2,
        out_specs=pl.BlockSpec(memory_space=pltpu.VMEM),
        scratch_shapes=[
            pltpu.VMEM((nodes + 8, 128), jnp.float32),
            pltpu.VMEM((batches * 512 + 8, 128), jnp.float32),
            pltpu.VMEM((chunks, 8, 128), jnp.int32),
            pltpu.VMEM((chunks, 128), jnp.int32),
            pltpu.VMEM((chunks, 128), jnp.int32),
            pltpu.SMEM((chunks, 128), jnp.int32),
            pltpu.SMEM((chunks, 128), jnp.int32),
            pltpu.SMEM((8, 128), jnp.int32),
            pltpu.SemaphoreType.DMA((3,)),
        ],
        compiler_params=pltpu.CompilerParams(vmem_limit_bytes=48 * 1024 * 1024),
        name="gather_rows",
    )(features, local_ids)


def local_ids_of(target_nodes, first_hop, offset):
    ids = jnp.concatenate([jnp.moveaxis(first_hop, 1, 0), target_nodes[None]], axis=0) - offset
    return ids.reshape(-1, 8, 128)


MESH = pl.DeviceIdType.MESH
HIGH = lax.Precision.HIGHEST


def run_all(*routes):
    active = list(routes)
    while active:
        for route in list(active):
            try:
                next(route)
            except StopIteration:
                active.remove(route)


def ring_sum(blk, inb, ssem, rsem, base, i, right, left):
    after, before, across = lax.rem(i + 1, 4), lax.rem(i + 3, 4), lax.rem(i + 2, 4)

    def copy(src, k, device):
        return pltpu.make_async_remote_copy(
            src_ref=src,
            dst_ref=inb(k),
            send_sem=ssem.at[base + k],
            recv_sem=rsem.at[base + k],
            device_id=device,
            device_id_type=MESH,
        )

    c0 = copy(blk(across, 0), 0, right)
    c1 = copy(blk(across, 1), 1, left)
    c2 = copy(blk(after, 1), 2, right)
    c3 = copy(blk(before, 0), 3, left)
    c4 = copy(blk(after, 0), 4, right)
    c5 = copy(blk(before, 1), 5, left)
    for c in (c0, c1, c2, c3):
        c.start()
    yield
    c0.wait_recv()
    blk(after, 0)[...] = blk(after, 0)[...] + inb(0)[...]
    c4.start()
    c1.wait_recv()
    blk(before, 1)[...] = blk(before, 1)[...] + inb(1)[...]
    c5.start()
    yield
    c3.wait_recv()
    c2.wait_recv()
    blk(i, 0)[...] = blk(i, 0)[...] + inb(3)[...]
    blk(i, 1)[...] = blk(i, 1)[...] + inb(2)[...]
    yield
    c4.wait_recv()
    blk(i, 0)[...] = blk(i, 0)[...] + inb(4)[...]
    c5.wait_recv()
    blk(i, 1)[...] = blk(i, 1)[...] + inb(5)[...]
    for c in (c0, c1, c2, c3, c4, c5):
        c.wait_send()


def ring_gather(blk, part, ssem, rsem, base, i, right, left, landed=None):
    after, before, across = lax.rem(i + 1, 4), lax.rem(i + 3, 4), lax.rem(i + 2, 4)

    def copy(ref, k, device):
        return pltpu.make_async_remote_copy(
            src_ref=ref,
            dst_ref=ref,
            send_sem=ssem.at[base + k],
            recv_sem=rsem.at[base + k],
            device_id=device,
            device_id_type=MESH,
        )

    c0 = copy(blk(i), 0, right)
    c1 = copy(blk(i), 1, left)
    c0.start()
    c1.start()
    yield
    c0.wait_recv()
    c2 = copy(part(before, 0), 2, right)
    c2.start()
    c1.wait_recv()
    c3 = copy(part(after, 1), 3, left)
    c3.start()
    if landed is not None:
        landed(0, before)
        landed(1, after)
    yield
    c2.wait_recv()
    c3.wait_recv()
    if landed is not None:
        landed(2, across)
    for c in (c0, c1, c2, c3):
        c.wait_send()


def grid_sum(buf, rows, in_wide, in_thin, ssem, rsem, base, x, y, xs, ys):
    half = rows // 2
    quarter = half // 2

    def route(h):
        lo = h * half

        def wide(d, p):
            at = pl.ds(lo + p * quarter, quarter)
            return buf.at[d, :, at] if h == 0 else buf.at[:, d, at]

        def thin(d, p):
            at = pl.ds(lo + p * quarter, quarter)
            return buf.at[x, d, at] if h == 0 else buf.at[d, y, at]

        first, second = ((x,) + xs, (y,) + ys) if h == 0 else ((y,) + ys, (x,) + xs)
        yield from ring_sum(wide, lambda k: in_wide.at[h, k], ssem, rsem, base + h * 12, *first)
        yield from ring_sum(thin, lambda k: in_thin.at[h, k], ssem, rsem, base + h * 12 + 6, *second)

    return route(0), route(1)


def grid_gather(buf, rows, ssem, rsem, base, x, y, xs, ys):
    half = rows // 2
    quarter = half // 2

    def route(h):
        lo = h * half

        def thin_at(d, at):
            return buf.at[x, d, at] if h == 0 else buf.at[d, y, at]

        def wide_at(d, at):
            return buf.at[d, :, at] if h == 0 else buf.at[:, d, at]

        first, second = ((y,) + ys, (x,) + xs) if h == 0 else ((x,) + xs, (y,) + ys)
        for n, (at_of, ring) in enumerate(((thin_at, first), (wide_at, second))):
            yield from ring_gather(
                lambda d, at_of=at_of: at_of(d, pl.ds(lo, half)),
                lambda d, p, at_of=at_of: at_of(d, pl.ds(lo + p * quarter, quarter)),
                ssem,
                rsem,
                base + h * 8 + n * 4,
                *ring,
            )

    return route(0), route(1)


def unpack(ref, x, y, row, lane64):
    p = [ref[x, y, pl.ds(row + 64 * n, 64), :] for n in range(3)]
    b = jnp.where(lane64 < 32, pltpu.roll(p[0], 32, 1), pltpu.roll(p[1], 32, 1))
    c = jnp.where(lane64 < 64, pltpu.roll(p[1], 64, 1), pltpu.roll(p[2], 64, 1))
    d = pltpu.roll(p[2], 96, 1)
    out = [jnp.where(lane64 < 96, v, 0.0) for v in (p[0], b, c, d)]
    return jnp.concatenate(out, axis=0)


def split(v):
    hi = v.astype(jnp.bfloat16)
    return hi, (v - hi.astype(jnp.float32)).astype(jnp.bfloat16)


def dot(a, b):
    return jnp.dot(a, b, preferred_element_type=jnp.float32)


def high_dot(a, b, dims=((1,), (0,))):
    return lax.dot_general(a, b, (dims, ((), ())), precision=HIGH, preferred_element_type=jnp.float32)


def exchange_kernel(
    fan_one,
    fan_two,
    parts_ref,
    ws_ref,
    wn_ref,
    hb_ref,
    cs_ref,
    cn_ref,
    cb_ref,
    live_ref,
    links_ref,
    labels_ref,
    hidden_ref,
    grads_ref,
    extras_ref,
    parts,
    in_wide,
    in_thin,
    weights,
    pre_parts,
    in_core,
    in_z,
    cs_pad,
    cn_pad,
    logit_own,
    logit_core,
    logit_z,
    piece,
    terms,
    in_wide_t,
    in_thin_t,
    extras,
    in_wide_e,
    in_thin_e,
    local_sem,
    ssem,
    rsem,
):
    group = lax.axis_index("group")
    m = lax.axis_index("mp")
    x, y = lax.div(group, 4), lax.rem(group, 4)
    z, core = lax.div(m, 2), lax.rem(m, 2)

    def device(nx, ny, nz, nc):
        return (nx * 4 + ny, nz * 2 + nc)

    def up(i, n):
        return lax.rem(i + n, 4)

    xs = (device(up(x, 1), y, z, core), device(up(x, 3), y, z, core))
    ys = (device(x, up(y, 1), z, core), device(x, up(y, 3), z, core))
    zs = (device(x, y, up(z, 1), core), device(x, y, up(z, 3), core))
    opposite = device(x, y, up(z, 2), core)
    sibling = device(x, y, z, 1 - core)

    load = pltpu.make_async_copy(parts_ref, parts, local_sem)
    load.start()
    barrier = pltpu.get_barrier_semaphore()
    for near in xs + ys + zs + (opposite, sibling):
        pl.semaphore_signal(barrier, inc=1, device_id=near, device_id_type=MESH)
    pl.semaphore_wait(barrier, 8)
    load.wait()

    used = 0
    rows_sum = grid_sum(parts, 384, in_wide, in_thin, ssem, rsem, used, x, y, xs, ys)
    used += 24
    for route in rows_sum:
        next(route)

    width = ws_ref.shape[0]
    hidden_all = ws_ref.shape[1]
    targets = hidden_ref.shape[0]
    seeds = labels_ref.shape[0]
    classes = cs_ref.shape[1]
    weights[...] = jnp.zeros_like(weights)
    weights[0:width, :] = ws_ref[...]
    weights[128 : 128 + width, :] = wn_ref[...]
    weights[256 : 256 + width, :] = wn_ref[...]
    cs_pad[...] = jnp.zeros_like(cs_pad)
    cn_pad[...] = jnp.zeros_like(cn_pad)
    cs_pad[:, 0:classes] = cs_ref[...].astype(jnp.float32)
    cn_pad[:, 0:classes] = cn_ref[...].astype(jnp.float32)
    target_rows = lax.broadcasted_iota(jnp.int32, (targets, 128), 0)
    links_t = jnp.zeros((targets, 128), jnp.float32)
    for k in range(fan_two):
        links_t = links_t + jnp.where(target_rows == links_ref[k : k + 1, :], 1.0, 0.0)
    links_f = links_t.T[0:seeds]
    run_all(*rows_sum)

    lane64 = lax.broadcasted_iota(jnp.int32, (64, 128), 1)
    self_rows = unpack(parts, x, y, 0, lane64)
    neigh_rows = unpack(parts, x, y, 192, lane64) / fan_one
    neigh_hi, neigh_lo = split(neigh_rows)
    left_side = jnp.concatenate([self_rows.astype(jnp.bfloat16), neigh_hi, neigh_lo], axis=1)
    hid = hidden_ref.shape[1]
    for zz in range(4):
        for cc in range(2):
            at = (zz * 2 + cc) * hid
            pre_parts[zz, cc] = dot(left_side, weights[:, at : at + hid])

    def core_copy(src, dst, k):
        return pltpu.make_async_remote_copy(
            src_ref=src,
            dst_ref=dst,
            send_sem=ssem.at[k],
            recv_sem=rsem.at[k],
            device_id=sibling,
            device_id_type=MESH,
        )

    halves = core_copy(pre_parts.at[:, 1 - core], in_core, used)
    used += 1
    halves.start()
    self_t = self_rows.T[0:width]
    neigh_t = neigh_rows.T[0:width]
    neigh_t_hi, neigh_t_lo = split(neigh_t)
    rows_hi = jnp.concatenate([self_t.astype(jnp.bfloat16), neigh_t_hi], axis=0)
    halves.wait()
    for zz in range(4):
        pre_parts[zz, core] = pre_parts[zz, core] + in_core[zz]
    half_rows = targets // 2
    run_all(
        ring_sum(
            lambda d, p: pre_parts.at[d, core, pl.ds(p * half_rows, half_rows)],
            lambda k: in_z.at[k],
            ssem,
            rsem,
            used,
            z,
            *zs,
        )
    )
    used += 6
    pre = pre_parts[z, core] + hb_ref[...]
    alive = (target_rows < live_ref[0]) & (pre > 0.0)
    hidden = jnp.where(alive, pre, 0.0).astype(jnp.bfloat16)
    hidden_ref[...] = hidden
    active = hidden.astype(jnp.float32)
    seed_self = active[0:seeds]
    seed_neigh = dot(links_f.astype(jnp.bfloat16), hidden) / fan_two
    logit_own[...] = high_dot(seed_self, cs_pad[...]) + high_dot(seed_neigh, cn_pad[...])
    to_core = core_copy(logit_own, logit_core, used)
    used += 1
    to_core.start()
    to_core.wait()
    logit_z[z] = logit_own[...] + logit_core[...]
    sends = []
    for k, near in enumerate(zs + (opposite,)):
        sends.append(
            pltpu.make_async_remote_copy(
                src_ref=logit_z.at[z],
                dst_ref=logit_z.at[z],
                send_sem=ssem.at[used + k],
                recv_sem=rsem.at[used + k],
                device_id=near,
                device_id_type=MESH,
            )
        )
    used += 3
    for c in sends:
        c.start()
    extras[...] = jnp.zeros_like(extras)
    for c in sends:
        c.wait()
    logits = (logit_z[0] + logit_z[1]) + (logit_z[2] + logit_z[3]) + cb_ref[...]
    lanes = lax.broadcasted_iota(jnp.int32, logits.shape, 1)
    logits = jnp.where(lanes < classes, logits, -1e30)
    top = jnp.max(logits, axis=1, keepdims=True)
    log_total = jnp.log(jnp.sum(jnp.exp(logits - top), axis=1, keepdims=True)) + top
    onehot = jnp.where(lanes == labels_ref[...], 1.0, 0.0)
    losses = log_total - jnp.sum(onehot * logits, axis=1, keepdims=True)
    dlogit = jnp.exp(logits - log_total) - onehot
    back_self = high_dot(dlogit, cs_pad[...], ((1,), (1,)))
    back_neigh = high_dot(dlogit, cn_pad[...], ((1,), (1,))) / fan_two
    back_neigh = jnp.concatenate([back_neigh, jnp.zeros((128 - seeds, hid), jnp.float32)], axis=0)
    grad_act = high_dot(links_t, back_neigh)
    grad_act = grad_act + jnp.concatenate(
        [back_self, jnp.zeros((targets - seeds, hid), jnp.float32)], axis=0
    )
    grad_pre = jnp.where(alive, grad_act, 0.0)
    piece[z, core] = grad_pre

    to_sibling = [core_copy(piece.at[z, core], piece.at[z, core], used)]
    to_sibling[0].start()

    def landed(n, d):
        c = core_copy(piece.at[d, core], piece.at[d, core], base_core + 1 + n)
        c.start()
        to_sibling.append(c)

    base_core = used
    used += 4
    spread = ring_gather(
        lambda d: piece.at[d, core],
        lambda d, p: piece.at[d, core, pl.ds(p * half_rows, half_rows)],
        ssem,
        rsem,
        used,
        z,
        *zs,
        landed=landed,
    )
    used += 4
    next(spread)

    dlogit_t = dlogit.T[0:160]
    class_grads = jnp.concatenate(
        [high_dot(dlogit_t, seed_self), high_dot(dlogit_t, seed_neigh)], axis=0
    )
    for n in range(10):
        extras[n // 4, n % 4] = class_grads[n * 32 : n * 32 + 32]
    row_sum = jnp.sum(dlogit, axis=0, keepdims=True)
    extras[2, 2, 0:1] = jnp.sum(grad_pre, axis=0, keepdims=True)
    extras[2, 2, 1:2] = row_sum[:, 0:128]
    extras[2, 2, 2:3] = row_sum[:, 128:256]
    extras[2, 2, 3:4] = jnp.broadcast_to(jnp.sum(losses, axis=0, keepdims=True), (1, 128))
    extra_sum = grid_sum(extras, 32, in_wide_e, in_thin_e, ssem, rsem, used, x, y, xs, ys)
    used += 24
    run_all(spread, *extra_sum)
    extras_ref[x, y] = extras[x, y]
    extra_gather = grid_gather(extras_ref, 32, ssem, rsem, used, x, y, xs, ys)
    used += 16
    for route in extra_gather:
        next(route)
    for c in to_sibling:
        c.wait()
    for zz in range(4):
        for cc in range(2):
            g_hi, g_lo = split(piece[zz, cc])
            term = dot(rows_hi, g_hi) + dot(rows_hi, g_lo)
            terms[zz, 2 * cc] = term[0:width]
            terms[zz, 2 * cc + 1] = term[width : 2 * width] + dot(neigh_t_lo, g_hi)
    term_sum = grid_sum(terms, 96, in_wide_t, in_thin_t, ssem, rsem, used, x, y, xs, ys)
    used += 24
    run_all(*extra_gather, *term_sum)
    grads_ref[x, y] = terms[x, y]
    run_all(*grid_gather(grads_ref, 96, ssem, rsem, used, x, y, xs, ys))
    used += 16
    assert used <= SEMS


SEMS = 160


def body(
    node_features,
    target_nodes,
    first_hop,
    live_counts,
    seed_links,
    seed_labels,
    self_weight,
    neigh_weight,
    hidden_bias,
    class_self,
    class_neigh,
    class_bias,
):
    node_rows = node_features.shape[1]
    batches, targets = target_nodes.shape
    fan_one = first_hop.shape[1]
    seeds, fan_two = seed_links.shape[1:]
    hid = hidden_bias.shape[0]
    width, hidden_all = self_weight.shape
    classes = class_bias.shape[0]
    group = lax.axis_index("group")
    ids = local_ids_of(target_nodes, first_hop, group * node_rows)
    parts = gather_rows(node_features, ids, batches).reshape(4, 4, 384, 128)
    links = jnp.pad(seed_links[0].T, ((0, 1), (0, 128 - seeds)), constant_values=-1)
    labels = seed_labels[0][:, None]
    bias = jnp.pad(class_bias[None], ((0, 0), (0, 256 - classes)))
    f32, vmem = jnp.float32, pl.BlockSpec(memory_space=pltpu.VMEM)
    shapes = [
        ((4, 4, 384, 128), f32),
        ((2, 6, 4, 96, 128), f32),
        ((2, 6, 96, 128), f32),
        ((384, hidden_all), jnp.bfloat16),
        ((4, 2, targets, hid), f32),
        ((4, targets, hid), f32),
        ((6, targets // 2, hid), f32),
        ((hid, 256), f32),
        ((hid, 256), f32),
        ((seeds, 256), f32),
        ((seeds, 256), f32),
        ((4, seeds, 256), f32),
        ((4, 2, targets, hid), f32),
        ((4, 4, 96, 128), f32),
        ((2, 6, 4, 24, 128), f32),
        ((2, 6, 24, 128), f32),
        ((4, 4, 32, 128), f32),
        ((2, 6, 4, 8, 128), f32),
        ((2, 6, 8, 128), f32),
    ]
    hidden_layer, grads, extras = pl.pallas_call(
        functools.partial(exchange_kernel, fan_one, fan_two),
        out_shape=(
            jax.ShapeDtypeStruct((targets, hid), jnp.bfloat16),
            jax.ShapeDtypeStruct((4, 4, 96, 128), f32),
            jax.ShapeDtypeStruct((4, 4, 32, 128), f32),
        ),
        in_specs=[pl.BlockSpec(memory_space=pl.ANY)]
        + [vmem] * 6
        + [pl.BlockSpec(memory_space=pltpu.SMEM)]
        + [vmem] * 2,
        out_specs=(vmem, vmem, vmem),
        scratch_shapes=[pltpu.VMEM(shape, kind) for shape, kind in shapes]
        + [
            pltpu.SemaphoreType.DMA,
            pltpu.SemaphoreType.DMA((SEMS,)),
            pltpu.SemaphoreType.DMA((SEMS,)),
        ],
        compiler_params=pltpu.CompilerParams(
            collective_id=0, has_side_effects=True, vmem_limit_bytes=48 * 1024 * 1024
        ),
        name="exchange",
    )(
        parts,
        self_weight,
        neigh_weight,
        hidden_bias[None],
        class_self,
        class_neigh,
        bias,
        live_counts,
        links,
        labels,
    )
    pair = grads.reshape(8, 2, width, hid)
    rows = extras.reshape(-1, hid)
    both = jnp.moveaxis(pair, 0, 2).reshape(2, width, 8 * hid)
    last = rows[320:324]
    return (
        hidden_layer,
        both[0],
        both[1],
        last[0],
        rows[0:classes].T,
        rows[160 : 160 + classes].T,
        last[1:3].reshape(-1)[0:classes],
        last[3, 0] / (batches * seeds),
    )


def solution(mesh):
    in_specs = (
        P("mp", "group"),
        P(),
        P(),
        P("group"),
        P("group", None, None),
        P("group", None),
        P("mp", None),
        P("mp", None),
        P("mp"),
        P("mp", None),
        P("mp", None),
        P(),
    )
    out_specs = (
        P("group", "mp"),
        P("mp", None),
        P("mp", None),
        P("mp"),
        P("mp", None),
        P("mp", None),
        P(),
        P(),
    )
    return jax.shard_map(body, mesh=mesh, in_specs=in_specs, out_specs=out_specs, check_vma=False)
```

```python
import functools
import jax
import jax.numpy as jnp
from jax import lax
from jax.experimental import pallas as pl
from jax.experimental.pallas import tpu as pltpu
from jax.sharding import PartitionSpec as P

UNROLL = 16
TOP = 3
BLOCK = 4
TURNS = 18


def gather_kernel(offset_ref, feat_ref, targets_ref, hops_ref, out_ref, table, acc, ids, codes, counts, first_s, counts_s, extra_s, sems):
    width, nodes = feat_ref.shape
    lists, rows = ids.shape[:2]
    fan, batches, targets = hops_ref.shape
    used = fan + 1
    half = rows * 128
    slots = 2 * half
    cols = targets // 128
    for n in range(cols):
        at, wide = pl.ds(n * batches, batches), slice(n * 128, n * 128 + 128)
        ids[0:fan, at] = hops_ref[:, :, wide] - offset_ref[0]
        ids[fan, at] = targets_ref[:, wide] - offset_ref[0]
    ids[used:lists] = jnp.full((lists - used, rows, 128), -1, jnp.int32)
    lane = lax.broadcasted_iota(jnp.int32, (BLOCK, rows, 128), 2)
    sub = lax.broadcasted_iota(jnp.int32, (BLOCK, rows, 128), 1)
    outer = lax.broadcasted_iota(jnp.int32, (BLOCK, rows, 128), 0)
    row_i = lax.broadcasted_iota(jnp.int32, (128, 128), 0)
    col_i = lax.broadcasted_iota(jnp.int32, (128, 128), 1)
    before = jnp.where(row_i < col_i, 1.0, 0.0).astype(jnp.bfloat16)
    ones = jnp.ones((128, 128), jnp.bfloat16)
    row_r = lax.broadcasted_iota(jnp.int32, (BLOCK * rows, BLOCK * rows), 0)
    col_r = lax.broadcasted_iota(jnp.int32, (BLOCK * rows, BLOCK * rows), 1)
    same = (row_r // rows) == (col_r // rows)
    above = jnp.where(same & (col_r < row_r), 1.0, 0.0).astype(jnp.bfloat16)
    shift = (nodes - 1).bit_length()
    steps = (half - 1).bit_length()
    flag = 1 << (shift + steps)

    def turn(i):
        at = pl.multiple_of(i * 128, 128)
        part = feat_ref[:, pl.ds(at, 128)].astype(jnp.float32)
        part = jnp.concatenate([part, jnp.zeros((128 - width, 128), jnp.float32)], axis=0)
        table[pl.ds(at, 128), :] = part.T

    def compact(q, carry):
        local = ids[pl.ds(q * BLOCK, BLOCK)]
        inside = (local >= 0) & (local < nodes)
        out_b = jnp.where(inside, 0.0, 1.0).reshape(BLOCK * rows, 128).astype(jnp.bfloat16)
        pref = jnp.dot(out_b, before, preferred_element_type=jnp.float32)
        total = jnp.dot(out_b, ones, preferred_element_type=jnp.float32)
        scan = jnp.dot(above, total.astype(jnp.bfloat16), preferred_element_type=jnp.float32)
        moved = (pref + scan).reshape(BLOCK, rows, 128).astype(jnp.int32)
        total = total.reshape(BLOCK, rows, 128)
        for b in range(BLOCK):
            missing = jnp.sum(total[b], axis=0, keepdims=True)
            counts[pl.ds(q * BLOCK + b, 1), :] = (half - missing).astype(jnp.int32)
        x = jnp.where(inside, flag | (moved << shift) | local, 0)
        for j in range(steps):
            d = 1 << j
            if j < 7:
                y = pltpu.roll(x, 128 - d, 2)
                y = jnp.where(lane < 128 - d, y, pltpu.roll(y, rows - 1, 1))
            else:
                y = pltpu.roll(x, rows - d // 128, 1)
            bit = 1 << (shift + j)
            x = jnp.where((y & bit) != 0, y, jnp.where((x & bit) != 0, 0, x))
        place = sub * 128 + lane + ((x >> shift) & (half - 1))
        row = place >> 7
        slot = (row % batches) * targets + (row // batches) * 128 + (place & 127)
        slot = slot + jnp.where(q * BLOCK + outer == fan, half, 0)
        code = jnp.where(x != 0, (slot << 15) | (x & (nodes - 1)), (slots << 15) | nodes)
        codes[pl.ds(q * BLOCK, BLOCK)] = code
        for n in range(TURNS):
            turn(q * TURNS + n)
        return carry

    lax.fori_loop(0, lists // BLOCK, compact, 0)
    copy_counts = pltpu.make_async_copy(counts, counts_s, sems.at[0])
    copy_counts.start()
    copies = []
    for j in range(used):
        for r in range(TOP):
            n = j * TOP + r
            copy = pltpu.make_async_copy(codes.at[j, r], first_s.at[pl.ds(n * 128, 128)], sems.at[n + 2])
            copy.start()
            copies.append(copy)

    def turn_rest(i, carry):
        turn(i)
        return carry

    lax.fori_loop(lists // BLOCK * TURNS, nodes // 128, turn_rest, 0)
    table[pl.ds(nodes, 8), :] = jnp.zeros((8, 128), jnp.float32)

    def clear(i, carry):
        acc[pl.ds(pl.multiple_of(i * 128, 128), 128), :] = jnp.zeros((128, 128), jnp.float32)
        return carry

    lax.fori_loop(0, slots // 128, clear, 0)
    acc[pl.ds(slots, 8), :] = jnp.zeros((8, 128), jnp.float32)
    copy_counts.wait()
    for copy in copies:
        copy.wait()

    def add_group(ref, base):
        code = [ref[base + u] for u in range(UNROLL)]
        at = [c >> 15 for c in code]
        rows = [table[pl.ds(c & 32767, 1), :] for c in code]
        olds = [acc[pl.ds(a, 1), :] for a in at]
        for a, old, row in zip(at, olds, rows):
            acc[pl.ds(a, 1), :] = old + row

    span = TOP * 128

    def step(state):
        j, k = state
        add_group(first_s, j * span + k)
        k = k + UNROLL
        done = k >= jnp.minimum(counts_s[j, 0], span)
        return jnp.where(done, j + 1, j), jnp.where(done, 0, k)

    lax.while_loop(lambda state: state[0] < used, step, (0, 0))

    def rest(j, carry):
        n = counts_s[j, 0]

        @pl.when(n > span)
        def _():
            def one(r, inner):
                copy = pltpu.make_async_copy(codes.at[j, r], extra_s, sems.at[1])
                copy.start()
                copy.wait()

                def group(i, inner2):
                    add_group(extra_s, i * UNROLL)
                    return inner2

                return lax.fori_loop(0, 128 // UNROLL, group, inner)

            lax.fori_loop(TOP, (n + 127) // 128, one, 0)

        return carry

    lax.fori_loop(0, used, rest, 0)

    lanes = lax.broadcasted_iota(jnp.int32, (64, 128), 1)

    def pack(i, carry):
        for s in range(2):
            base = (1 - s) * half + i * 256
            a, b, c, d = [acc[pl.ds(pl.multiple_of(base + n * 64, 64), 64), :] for n in range(4)]
            b, c, d = pltpu.roll(b, 96, 1), pltpu.roll(c, 64, 1), pltpu.roll(d, 32, 1)
            out_ref[i, pl.ds(s * 192, 64), :] = jnp.where(lanes < 96, a, b)
            out_ref[i, pl.ds(s * 192 + 64, 64), :] = jnp.where(lanes < 64, b, c)
            out_ref[i, pl.ds(s * 192 + 128, 64), :] = jnp.where(lanes < 32, c, d)
        return carry

    lax.fori_loop(0, half // 256, pack, 0)


def gather_rows(features, target_nodes, first_hop, offset):
    nodes = features.shape[1]
    batches, targets = target_nodes.shape
    rows = batches * targets // 128
    lists = 28
    vmem = pl.BlockSpec(memory_space=pltpu.VMEM)
    return pl.pallas_call(
        gather_kernel,
        out_shape=jax.ShapeDtypeStruct((batches, 384, 128), jnp.float32),
        in_specs=[pl.BlockSpec(memory_space=pltpu.SMEM)] + [vmem] * 3,
        out_specs=vmem,
        scratch_shapes=[
            pltpu.VMEM((nodes + 8, 128), jnp.float32),
            pltpu.VMEM((batches * 512 + 8, 128), jnp.float32),
            pltpu.VMEM((lists, rows, 128), jnp.int32),
            pltpu.VMEM((lists, rows, 128), jnp.int32),
            pltpu.VMEM((lists + 4, 128), jnp.int32),
            pltpu.SMEM((lists * TOP * 128,), jnp.int32),
            pltpu.SMEM((lists + 4, 128), jnp.int32),
            pltpu.SMEM((128,), jnp.int32),
            pltpu.SemaphoreType.DMA((lists * TOP + 2,)),
        ],
        compiler_params=pltpu.CompilerParams(vmem_limit_bytes=48 * 1024 * 1024),
        name="gather_rows",
    )(offset, features, target_nodes, jnp.moveaxis(first_hop, 1, 0))


MESH = pl.DeviceIdType.MESH
HIGH = lax.Precision.HIGHEST


def run_all(*routes):
    active = list(routes)
    while active:
        for route in list(active):
            try:
                next(route)
            except StopIteration:
                active.remove(route)


def ring_sum(blk, inb, ssem, rsem, base, i, right, left):
    after, before, across = lax.rem(i + 1, 4), lax.rem(i + 3, 4), lax.rem(i + 2, 4)

    def copy(src, k, device):
        return pltpu.make_async_remote_copy(
            src_ref=src,
            dst_ref=inb(k),
            send_sem=ssem.at[base + k],
            recv_sem=rsem.at[base + k],
            device_id=device,
            device_id_type=MESH,
        )

    c0 = copy(blk(across, 0), 0, right)
    c1 = copy(blk(across, 1), 1, left)
    c2 = copy(blk(after, 1), 2, right)
    c3 = copy(blk(before, 0), 3, left)
    c4 = copy(blk(after, 0), 4, right)
    c5 = copy(blk(before, 1), 5, left)
    for c in (c0, c1, c2, c3):
        c.start()
    yield
    c0.wait_recv()
    blk(after, 0)[...] = blk(after, 0)[...] + inb(0)[...]
    c4.start()
    c1.wait_recv()
    blk(before, 1)[...] = blk(before, 1)[...] + inb(1)[...]
    c5.start()
    yield
    c3.wait_recv()
    c2.wait_recv()
    blk(i, 0)[...] = blk(i, 0)[...] + inb(3)[...]
    blk(i, 1)[...] = blk(i, 1)[...] + inb(2)[...]
    yield
    c4.wait_recv()
    blk(i, 0)[...] = blk(i, 0)[...] + inb(4)[...]
    c5.wait_recv()
    blk(i, 1)[...] = blk(i, 1)[...] + inb(5)[...]
    for c in (c0, c1, c2, c3, c4, c5):
        c.wait_send()


def grid_sum(buf, spans, in_wide, in_thin, ssem, rsem, base, x, y, xs, ys):
    def route(n, h, lo, half):
        def wide(d, p):
            at = pl.ds(lo + p * half, half)
            return buf.at[d, :, at] if h == 0 else buf.at[:, d, at]

        def thin(d, p):
            at = pl.ds(lo + p * half, half)
            return buf.at[x, d, at] if h == 0 else buf.at[d, y, at]

        first, second = ((x,) + xs, (y,) + ys) if h == 0 else ((y,) + ys, (x,) + xs)
        yield from ring_sum(wide, lambda k: in_wide.at[n, k], ssem, rsem, base + n * 12, *first)
        yield from ring_sum(thin, lambda k: in_thin.at[n, k], ssem, rsem, base + n * 12 + 6, *second)

    return [route(n, *span) for n, span in enumerate(spans)]


def grid_gather(buf, spans, ssem, rsem, base, x, y, device):
    def route(n, h, lo, rows):
        at = pl.ds(lo, rows)

        def near(dx, dy):
            return device(dx, dy) if h == 0 else device(dy, dx)

        def place(far, close):
            return buf.at[far, close, at] if h == 0 else buf.at[close, far, at]

        far, close = (x, y) if h == 0 else (y, x)
        started = []

        def send(ref, k, target):
            copy = pltpu.make_async_remote_copy(
                src_ref=ref,
                dst_ref=ref,
                send_sem=ssem.at[base + n * 15 + k],
                recv_sem=rsem.at[base + n * 15 + k],
                device_id=target,
                device_id_type=MESH,
            )
            copy.start()
            started.append(copy)

        for d in (1, 3, 2):
            send(place(far, close), d - 1, near(0, d))
        for d in (1, 3, 2):
            send(place(far, close), 2 + d, near(d, 0))
        firsts = list(started)
        for n2, d in enumerate((1, 3, 2)):
            yield
            firsts[n2].wait_recv()
            source = lax.rem(close + 4 - d, 4)
            for e in (1, 3, 2):
                send(place(far, source), 3 * d + 2 + e, near(e, 0))
        yield
        for copy in started[3:]:
            copy.wait_recv()
        for copy in started:
            copy.wait_send()

    return [route(n, *span) for n, span in enumerate(spans)]


def unpack(ref, x, y, row, lane64):
    p = [ref[x, y, pl.ds(row + 64 * n, 64), :] for n in range(3)]
    b = jnp.where(lane64 < 32, pltpu.roll(p[0], 32, 1), pltpu.roll(p[1], 32, 1))
    c = jnp.where(lane64 < 64, pltpu.roll(p[1], 64, 1), pltpu.roll(p[2], 64, 1))
    d = pltpu.roll(p[2], 96, 1)
    out = [jnp.where(lane64 < 96, v, 0.0) for v in (p[0], b, c, d)]
    return jnp.concatenate(out, axis=0)


def split(v):
    hi = v.astype(jnp.bfloat16)
    return hi, (v - hi.astype(jnp.float32)).astype(jnp.bfloat16)


def dot(a, b):
    return jnp.dot(a, b, preferred_element_type=jnp.float32)


def high_dot(a, b, dims=((1,), (0,))):
    return lax.dot_general(a, b, (dims, ((), ())), precision=HIGH, preferred_element_type=jnp.float32)


def exchange_kernel(
    fan_one,
    fan_two,
    parts_ref,
    ws_ref,
    wn_ref,
    hb_ref,
    cs_ref,
    cn_ref,
    cb_ref,
    live_ref,
    links_ref,
    labels_ref,
    hidden_ref,
    sums_ref,
    parts,
    in_wide,
    in_thin,
    weights,
    pre_parts,
    in_core,
    in_z,
    cs_pad,
    cn_pad,
    cb_pad,
    label_rows,
    link_pad,
    logit_own,
    logit_core,
    logit_z,
    piece,
    terms,
    in_terms,
    extras,
    in_extras,
    local_sem,
    ssem,
    rsem,
):
    group = lax.axis_index("group")
    m = lax.axis_index("mp")
    x, y = lax.div(group, 4), lax.rem(group, 4)
    z, core = lax.div(m, 2), lax.rem(m, 2)
    groups = in_terms.shape[0]

    def up(i, n):
        return lax.rem(i + n, 4)

    def grid_device(dx, dy):
        return (up(x, dx) * 4 + up(y, dy), m)

    def z_device(dz):
        return (group, up(z, dz) * 2 + core)

    xs = (grid_device(1, 0), grid_device(3, 0))
    ys = (grid_device(0, 1), grid_device(0, 3))
    zs = (z_device(1), z_device(3))
    opposite = z_device(2)
    sibling = (group, z * 2 + 1 - core)
    others = [(lax.rem(group + r, groups), m) for r in range(1, groups)]

    load = pltpu.make_async_copy(parts_ref, parts, local_sem)
    load.start()
    barrier = pltpu.get_barrier_semaphore()
    nears = others + list(zs) + [opposite, sibling]
    for near in nears:
        pl.semaphore_signal(barrier, inc=1, device_id=near, device_id_type=MESH)
    pl.semaphore_wait(barrier, len(nears))
    load.wait()

    used = 0
    spans = ((0, 0, 48), (1, 192, 48), (0, 96, 48), (1, 288, 48))
    rows_sum = grid_sum(parts, spans, in_wide, in_thin, ssem, rsem, used, x, y, xs, ys)
    used += 48
    for route in rows_sum:
        next(route)

    width = ws_ref.shape[0]
    targets, hid = hidden_ref.shape
    seeds = labels_ref.shape[1]
    classes = cs_ref.shape[0]
    weights[...] = jnp.zeros_like(weights)
    weights[0:width, :] = ws_ref[...]
    weights[128 : 128 + width, :] = wn_ref[...]
    weights[256 : 256 + width, :] = wn_ref[...]
    cs_pad[...] = jnp.zeros_like(cs_pad)
    cn_pad[...] = jnp.zeros_like(cn_pad)
    cb_pad[...] = jnp.zeros_like(cb_pad)
    cs_pad[0:classes, :] = cs_ref[...].astype(jnp.float32)
    cn_pad[0:classes, :] = cn_ref[...].astype(jnp.float32)
    cb_pad[:, 0:classes] = cb_ref[...]
    extras[...] = jnp.zeros_like(extras)
    for s in range(seeds):
        label_rows[s : s + 1, :] = jnp.full((1, 256), labels_ref[0, s], jnp.int32)
    seed_cols = lax.broadcasted_iota(jnp.int32, (targets, seeds), 0)
    counted = jnp.zeros((targets, seeds), jnp.float32)
    for k in range(fan_two):
        counted = counted + jnp.where(seed_cols == links_ref[k], 1.0, 0.0)
    link_pad[...] = jnp.zeros_like(link_pad)
    link_pad[:, 0:seeds] = counted
    links_t = link_pad[...]
    links_f = links_t.T[0:seeds]
    run_all(*rows_sum)

    lane64 = lax.broadcasted_iota(jnp.int32, (64, 128), 1)
    target_rows = lax.broadcasted_iota(jnp.int32, (targets, 128), 0)
    self_rows = unpack(parts, x, y, 0, lane64)
    neigh_rows = unpack(parts, x, y, 192, lane64) / fan_one
    neigh_hi, neigh_lo = split(neigh_rows)
    left_side = jnp.concatenate([self_rows.astype(jnp.bfloat16), neigh_hi, neigh_lo], axis=1)

    def block_of(zz, cc):
        at = pl.multiple_of((zz * 2 + cc) * hid, hid)
        pre_parts[zz, cc] = dot(left_side, weights[:, pl.ds(at, hid)])

    def core_copy(src, dst, k):
        return pltpu.make_async_remote_copy(
            src_ref=src,
            dst_ref=dst,
            send_sem=ssem.at[k],
            recv_sem=rsem.at[k],
            device_id=sibling,
            device_id_type=MESH,
        )

    half_rows = targets // 2

    def owner_sum(n, base):
        at = pl.ds(n * half_rows, half_rows)
        copy = core_copy(pre_parts.at[:, 1 - core, at], in_core.at[:, at], base)
        copy.start()
        yield
        copy.wait()
        for zz in range(4):
            pre_parts[zz, core, at] = pre_parts[zz, core, at] + in_core[zz, at]
        quarter = half_rows // 2
        yield from ring_sum(
            lambda d, p: pre_parts.at[d, core, pl.ds(n * half_rows + p * quarter, quarter)],
            lambda k: in_z.at[n, k],
            ssem,
            rsem,
            base + 1,
            z,
            *zs,
        )

    for zz in range(4):
        block_of(zz, 1 - core)
    owners = [owner_sum(n, used + 7 * n) for n in range(2)]
    used += 14
    for route in owners:
        next(route)
    for zz in range(4):
        block_of(zz, core)
    self_t = self_rows.T[0:width]
    neigh_t = neigh_rows.T[0:width]
    neigh_t_hi, neigh_t_lo = split(neigh_t)
    rows_hi = jnp.concatenate([self_t.astype(jnp.bfloat16), neigh_t_hi], axis=0)
    run_all(*owners)

    pre = pre_parts[z, core] + hb_ref[...]
    alive = (target_rows < live_ref[0]) & (pre > 0.0)
    hidden = jnp.where(alive, pre, 0.0).astype(jnp.bfloat16)
    hidden_ref[...] = hidden
    active = hidden.astype(jnp.float32)
    seed_self = active[0:seeds]
    seed_neigh = dot(links_f.astype(jnp.bfloat16), hidden) / fan_two
    rows_cols = ((1,), (1,))
    logit_own[...] = high_dot(seed_self, cs_pad[...], rows_cols) + high_dot(seed_neigh, cn_pad[...], rows_cols)
    to_core = core_copy(logit_own, logit_core, used)
    used += 1
    to_core.start()
    to_core.wait()
    logit_z[z] = logit_own[...] + logit_core[...]

    def z_sends(ref, base):
        copies = []
        for k, near in enumerate(zs + (opposite,)):
            copies.append(
                pltpu.make_async_remote_copy(
                    src_ref=ref,
                    dst_ref=ref,
                    send_sem=ssem.at[base + k],
                    recv_sem=rsem.at[base + k],
                    device_id=near,
                    device_id_type=MESH,
                )
            )
            copies[-1].start()
        return copies

    sends = z_sends(logit_z.at[z], used)
    used += 3
    for c in sends:
        c.wait()
    logits = (logit_z[0] + logit_z[1]) + (logit_z[2] + logit_z[3]) + cb_pad[...]
    lanes = lax.broadcasted_iota(jnp.int32, logits.shape, 1)
    logits = jnp.where(lanes < classes, logits, -1e30)
    top = jnp.max(logits, axis=1, keepdims=True)
    log_total = jnp.log(jnp.sum(jnp.exp(logits - top), axis=1, keepdims=True)) + top
    onehot = jnp.where(lanes == label_rows[...], 1.0, 0.0)
    losses = log_total - jnp.sum(onehot * logits, axis=1, keepdims=True)
    dlogit = jnp.exp(logits - log_total) - onehot
    back_self = high_dot(dlogit, cs_pad[...])
    back_neigh = high_dot(dlogit, cn_pad[...]) / fan_two
    back_neigh = jnp.concatenate([back_neigh, jnp.zeros((128 - seeds, hid), jnp.float32)], axis=0)
    grad_act = high_dot(links_t, back_neigh)
    grad_act = grad_act + jnp.concatenate(
        [back_self, jnp.zeros((targets - seeds, hid), jnp.float32)], axis=0
    )
    grad_pre = jnp.where(alive, grad_act, 0.0)
    piece[0, 0] = grad_pre

    def piece_send(slot, target, k):
        copy = pltpu.make_async_remote_copy(
            src_ref=piece.at[0, 0],
            dst_ref=piece.at[slot, 0],
            send_sem=ssem.at[used + k],
            recv_sem=rsem.at[used + k],
            device_id=target,
            device_id_type=MESH,
        )
        copy.start()
        return copy

    spread = [piece_send(1, zs[0], 0), piece_send(3, zs[1], 1), piece_send(2, opposite, 2)]
    used += 3
    core_base = used
    used += 4
    to_sibling = [core_copy(piece.at[0, 0], piece.at[0, 1], core_base)]
    to_sibling[0].start()

    dlogit_t = dlogit.T[0:160]
    class_grads = jnp.concatenate(
        [high_dot(dlogit_t, seed_self), high_dot(dlogit_t, seed_neigh)], axis=0
    )
    per = extras.shape[1]
    for n in range(0, 320, 8):
        extras[n // per, n % per : n % per + 8] = class_grads[n : n + 8]
    row_sum = jnp.sum(dlogit, axis=0, keepdims=True)
    lines = (
        jnp.sum(grad_pre, axis=0, keepdims=True),
        row_sum[:, 0:128],
        row_sum[:, 128:256],
        jnp.broadcast_to(jnp.sum(losses, axis=0, keepdims=True), (1, 128)),
    )
    for n, line in enumerate(lines):
        extras[320 // per, 320 % per + n : 320 % per + n + 1] = line
    extra_sends = []
    for r in range(1, groups):
        copy = pltpu.make_async_remote_copy(
            src_ref=extras.at[lax.rem(group + r, groups)],
            dst_ref=in_extras.at[r],
            send_sem=ssem.at[used + r - 1],
            recv_sem=rsem.at[used + r - 1],
            device_id=others[r - 1],
            device_id_type=MESH,
        )
        copy.start()
        extra_sends.append(copy)
    used += groups - 1

    term_base = used
    used += groups

    def term_copy(k, dest, k_recv):
        return pltpu.make_async_remote_copy(
            src_ref=terms.at[k],
            dst_ref=in_terms.at[group],
            send_sem=ssem.at[term_base + k],
            recv_sem=rsem.at[term_base + k_recv],
            device_id=(dest, m),
            device_id_type=MESH,
        )

    dests = {}

    def block_terms(step, n, across):
        zz = lax.rem(z + 4 - n, 4)
        cc = 1 - core if across else core
        g_hi, g_lo = split(piece[n, across])
        term = dot(rows_hi, g_hi) + dot(rows_hi, g_lo)
        terms[2 * step] = term[0:width]
        terms[2 * step + 1] = term[width : 2 * width] + dot(neigh_t_lo, g_hi)
        for s in range(2):
            k = 2 * step + s
            dests[k] = dest = zz * 4 + cc * 2 + s

            @pl.when(dest != group)
            def _():
                term_copy(k, dest, group).start()

            @pl.when(dest == group)
            def _():
                in_terms[group] = terms[k]

    def forward(n):
        copy = core_copy(piece.at[n, 0], piece.at[n, 1], core_base + n)
        copy.start()
        to_sibling.append(copy)

    block_terms(0, 0, 0)
    to_sibling[0].wait_recv()
    block_terms(1, 0, 1)
    spread[0].wait_recv()
    forward(1)
    block_terms(2, 1, 0)
    spread[1].wait_recv()
    forward(3)
    block_terms(3, 3, 0)
    to_sibling[1].wait_recv()
    block_terms(4, 1, 1)
    to_sibling[2].wait_recv()
    block_terms(5, 3, 1)
    spread[2].wait_recv()
    forward(2)
    block_terms(6, 2, 0)
    to_sibling[3].wait_recv()
    block_terms(7, 2, 1)

    for copy in extra_sends:
        copy.wait_recv()
    total = extras[group]
    for r in range(1, groups):
        total = total + in_extras[r]
    sums_ref[x, y, width : width + per] = total
    for source in range(groups):

        @pl.when(source != group)
        def _():
            pltpu.make_async_remote_copy(
                src_ref=terms.at[0],
                dst_ref=in_terms.at[source],
                send_sem=ssem.at[term_base],
                recv_sem=rsem.at[term_base + source],
                device_id=(source, m),
                device_id_type=MESH,
            ).wait_recv()

    total = in_terms[0]
    for source in range(1, groups):
        total = total + in_terms[source]
    sums_ref[x, y, 0:width] = total
    spans = ((0, 0, 56), (1, 56, 64))
    last = grid_gather(sums_ref, spans, ssem, rsem, used, x, y, grid_device)
    used += 30
    for route in last:
        next(route)
    for copy in spread + to_sibling + extra_sends:
        copy.wait_send()
    for k in range(groups):
        dest = dests[k]

        @pl.when(dest != group)
        def _():
            term_copy(k, dest, group).wait_send()

    run_all(*last)
    assert used <= SEMS


SEMS = 144


def finish_kernel(scale, hidden_ref, sums_ref, *outs):
    hidden_out, self_out, neigh_out, hb_out, cs_out, cn_out, cb_out, loss_out, lines = outs
    width = self_out.shape[0]
    hid = hidden_ref.shape[1]
    groups, rows = sums_ref.shape[:2]
    per = rows - width
    hidden_out[...] = hidden_ref[...]
    for n in range(groups):
        out = neigh_out if n % 2 else self_out
        at = n // 2 * hid
        out[:, at : at + hid] = sums_ref[n, 0:width, :]
        lines[n * per : n * per + per, :] = sums_ref[n, width:rows, :]
    classes = cs_out.shape[0]
    cs_out[...] = lines[0:classes, :]
    cn_out[...] = lines[160 : 160 + classes, :]
    hb_out[...] = lines[320:321, :]
    cb_out[:, 0:128] = lines[321:322, :]
    cb_out[:, 128:classes] = lines[322:323, 0 : classes - 128]
    loss_out[...] = lines[323:324, :] * scale


def body(
    node_features,
    target_nodes,
    first_hop,
    live_counts,
    seed_links,
    seed_labels,
    self_weight,
    neigh_weight,
    hidden_bias,
    class_self,
    class_neigh,
    class_bias,
):
    node_rows = node_features.shape[1]
    batches, targets = target_nodes.shape
    fan_one = first_hop.shape[1]
    seeds, fan_two = seed_links.shape[1:]
    hid = hidden_bias.shape[0]
    width, hidden_all = self_weight.shape
    classes = class_bias.shape[0]
    offset = (lax.axis_index("group") * node_rows).astype(jnp.int32)[None]
    parts = gather_rows(node_features, target_nodes, first_hop, offset).reshape(4, 4, 384, 128)
    f32, vmem = jnp.float32, pl.BlockSpec(memory_space=pltpu.VMEM)
    smem = pl.BlockSpec(memory_space=pltpu.SMEM)
    shapes = [
        ((4, 4, 384, 128), f32),
        ((4, 6, 4, 48, 128), f32),
        ((4, 6, 48, 128), f32),
        ((384, hidden_all), jnp.bfloat16),
        ((4, 2, targets, hid), f32),
        ((4, targets, hid), f32),
        ((2, 6, targets // 4, hid), f32),
        ((256, hid), f32),
        ((256, hid), f32),
        ((1, 256), f32),
        ((seeds, 256), jnp.int32),
        ((targets, 128), f32),
        ((seeds, 256), f32),
        ((seeds, 256), f32),
        ((4, seeds, 256), f32),
        ((4, 2, targets, hid), f32),
        ((16, width, 128), f32),
        ((16, width, 128), f32),
        ((16, 24, 128), f32),
        ((16, 24, 128), f32),
    ]
    hidden_layer, sums = pl.pallas_call(
        functools.partial(exchange_kernel, fan_one, fan_two),
        out_shape=(
            jax.ShapeDtypeStruct((targets, hid), jnp.bfloat16),
            jax.ShapeDtypeStruct((4, 4, width + 24, 128), f32),
        ),
        in_specs=[pl.BlockSpec(memory_space=pl.ANY)] + [vmem] * 6 + [smem, vmem, smem],
        out_specs=(vmem, vmem),
        scratch_shapes=[pltpu.VMEM(shape, kind) for shape, kind in shapes]
        + [
            pltpu.SemaphoreType.DMA,
            pltpu.SemaphoreType.DMA((SEMS,)),
            pltpu.SemaphoreType.DMA((SEMS,)),
        ],
        compiler_params=pltpu.CompilerParams(
            collective_id=0, has_side_effects=True, vmem_limit_bytes=48 * 1024 * 1024
        ),
        name="exchange",
    )(
        parts,
        self_weight,
        neigh_weight,
        hidden_bias[None],
        class_self.T,
        class_neigh.T,
        class_bias[None],
        live_counts,
        jnp.transpose(seed_links, (2, 0, 1)),
        seed_labels,
    )
    outs = pl.pallas_call(
        functools.partial(finish_kernel, 1.0 / (batches * seeds)),
        out_shape=(
            jax.ShapeDtypeStruct((targets, hid), jnp.bfloat16),
            jax.ShapeDtypeStruct((width, hidden_all), f32),
            jax.ShapeDtypeStruct((width, hidden_all), f32),
            jax.ShapeDtypeStruct((1, hid), f32),
            jax.ShapeDtypeStruct((classes, hid), f32),
            jax.ShapeDtypeStruct((classes, hid), f32),
            jax.ShapeDtypeStruct((1, classes), f32),
            jax.ShapeDtypeStruct((1, 128), f32),
        ),
        in_specs=[vmem] * 2,
        out_specs=(vmem,) * 8,
        scratch_shapes=[pltpu.VMEM((16 * 24, 128), f32)],
        name="finish",
    )(hidden_layer, sums.reshape(16, width + 24, 128))
    return (
        outs[0],
        outs[1],
        outs[2],
        outs[3][0],
        outs[4].T,
        outs[5].T,
        outs[6][0],
        outs[7][0, 0],
    )


def solution(mesh):
    in_specs = (
        P("mp", "group"),
        P(),
        P(),
        P("group"),
        P("group", None, None),
        P("group", None),
        P("mp", None),
        P("mp", None),
        P("mp"),
        P("mp", None),
        P("mp", None),
        P(),
    )
    out_specs = (
        P("group", "mp"),
        P("mp", None),
        P("mp", None),
        P("mp"),
        P("mp", None),
        P("mp", None),
        P(),
        P(),
    )
    return jax.shard_map(body, mesh=mesh, in_specs=in_specs, out_specs=out_specs, check_vma=False)
```

```python
import functools
import jax
import jax.numpy as jnp
from jax import lax
from jax.experimental import pallas as pl
from jax.experimental.pallas import tpu as pltpu
from jax.sharding import PartitionSpec as P

UNROLL = 16
TOP = 3
BLOCK = 4
TURNS = 18


def gather_kernel(offset_ref, feat_hbm, targets_hbm, hops_hbm, out_ref, feat_ref, targets_ref, hops_ref, table, acc, ids, codes, counts, first_s, counts_s, extra_s, sems, load_sems):
    loads = [
        pltpu.make_async_copy(src, dst, load_sems.at[n])
        for n, (src, dst) in enumerate(((hops_hbm, hops_ref), (targets_hbm, targets_ref), (feat_hbm, feat_ref)))
    ]
    for load in loads:
        load.start()
    width, nodes = feat_ref.shape
    lists, rows = ids.shape[:2]
    fan, batches, targets = hops_ref.shape
    used = fan + 1
    half = rows * 128
    slots = 2 * half
    cols = targets // 128
    loads[0].wait()
    loads[1].wait()
    for n in range(cols):
        at, wide = pl.ds(n * batches, batches), slice(n * 128, n * 128 + 128)
        ids[0:fan, at] = hops_ref[:, :, wide] - offset_ref[0]
        ids[fan, at] = targets_ref[:, wide] - offset_ref[0]
    ids[used:lists] = jnp.full((lists - used, rows, 128), -1, jnp.int32)
    lane = lax.broadcasted_iota(jnp.int32, (BLOCK, rows, 128), 2)
    sub = lax.broadcasted_iota(jnp.int32, (BLOCK, rows, 128), 1)
    outer = lax.broadcasted_iota(jnp.int32, (BLOCK, rows, 128), 0)
    row_i = lax.broadcasted_iota(jnp.int32, (128, 128), 0)
    col_i = lax.broadcasted_iota(jnp.int32, (128, 128), 1)
    before = jnp.where(row_i < col_i, 1.0, 0.0).astype(jnp.bfloat16)
    ones = jnp.ones((128, 128), jnp.bfloat16)
    row_r = lax.broadcasted_iota(jnp.int32, (BLOCK * rows, BLOCK * rows), 0)
    col_r = lax.broadcasted_iota(jnp.int32, (BLOCK * rows, BLOCK * rows), 1)
    same = (row_r // rows) == (col_r // rows)
    above = jnp.where(same & (col_r < row_r), 1.0, 0.0).astype(jnp.bfloat16)
    shift = (nodes - 1).bit_length()
    steps = (half - 1).bit_length()
    flag = 1 << (shift + steps)

    def turn(i):
        at = pl.multiple_of(i * 128, 128)
        part = feat_ref[:, pl.ds(at, 128)].astype(jnp.float32)
        part = jnp.concatenate([part, jnp.zeros((128 - width, 128), jnp.float32)], axis=0)
        table[pl.ds(at, 128), :] = part.T

    def compact(q, carry):
        local = ids[pl.ds(q * BLOCK, BLOCK)]
        inside = (local >= 0) & (local < nodes)
        out_b = jnp.where(inside, 0.0, 1.0).reshape(BLOCK * rows, 128).astype(jnp.bfloat16)
        pref = jnp.dot(out_b, before, preferred_element_type=jnp.float32)
        total = jnp.dot(out_b, ones, preferred_element_type=jnp.float32)
        scan = jnp.dot(above, total.astype(jnp.bfloat16), preferred_element_type=jnp.float32)
        moved = (pref + scan).reshape(BLOCK, rows, 128).astype(jnp.int32)
        total = total.reshape(BLOCK, rows, 128)
        for b in range(BLOCK):
            missing = jnp.sum(total[b], axis=0, keepdims=True)
            counts[pl.ds(q * BLOCK + b, 1), :] = (half - missing).astype(jnp.int32)
        x = jnp.where(inside, flag | (moved << shift) | local, 0)
        for j in range(steps):
            d = 1 << j
            if j < 7:
                y = pltpu.roll(x, 128 - d, 2)
                y = jnp.where(lane < 128 - d, y, pltpu.roll(y, rows - 1, 1))
            else:
                y = pltpu.roll(x, rows - d // 128, 1)
            bit = 1 << (shift + j)
            x = jnp.where((y & bit) != 0, y, jnp.where((x & bit) != 0, 0, x))
        place = sub * 128 + lane + ((x >> shift) & (half - 1))
        row = place >> 7
        slot = (row % batches) * targets + (row // batches) * 128 + (place & 127)
        slot = slot + jnp.where(q * BLOCK + outer == fan, half, 0)
        code = jnp.where(x != 0, (slot << 15) | (x & (nodes - 1)), (slots << 15) | nodes)
        codes[pl.ds(q * BLOCK, BLOCK)] = code
        for n in range(TURNS):
            turn(q * TURNS + n)
        return carry

    loads[2].wait()
    lax.fori_loop(0, lists // BLOCK, compact, 0)
    copy_counts = pltpu.make_async_copy(counts, counts_s, sems.at[0])
    copy_counts.start()
    copies = []
    for j in range(used):
        for r in range(TOP):
            n = j * TOP + r
            copy = pltpu.make_async_copy(codes.at[j, r], first_s.at[pl.ds(n * 128, 128)], sems.at[n + 2])
            copy.start()
            copies.append(copy)

    def turn_rest(i, carry):
        turn(i)
        return carry

    lax.fori_loop(lists // BLOCK * TURNS, nodes // 128, turn_rest, 0)
    table[pl.ds(nodes, 8), :] = jnp.zeros((8, 128), jnp.float32)

    def clear(i, carry):
        acc[pl.ds(pl.multiple_of(i * 128, 128), 128), :] = jnp.zeros((128, 128), jnp.float32)
        return carry

    lax.fori_loop(0, slots // 128, clear, 0)
    acc[pl.ds(slots, 8), :] = jnp.zeros((8, 128), jnp.float32)
    copy_counts.wait()
    for copy in copies:
        copy.wait()

    def add_group(ref, base):
        code = [ref[base + u] for u in range(UNROLL)]
        at = [c >> 15 for c in code]
        rows = [table[pl.ds(c & 32767, 1), :] for c in code]
        olds = [acc[pl.ds(a, 1), :] for a in at]
        for a, old, row in zip(at, olds, rows):
            acc[pl.ds(a, 1), :] = old + row

    span = TOP * 128

    def step(state):
        j, k = state
        add_group(first_s, j * span + k)
        k = k + UNROLL
        done = k >= jnp.minimum(counts_s[j, 0], span)
        return jnp.where(done, j + 1, j), jnp.where(done, 0, k)

    lax.while_loop(lambda state: state[0] < used, step, (0, 0))

    def rest(j, carry):
        n = counts_s[j, 0]

        @pl.when(n > span)
        def _():
            def one(r, inner):
                copy = pltpu.make_async_copy(codes.at[j, r], extra_s, sems.at[1])
                copy.start()
                copy.wait()

                def group(i, inner2):
                    add_group(extra_s, i * UNROLL)
                    return inner2

                return lax.fori_loop(0, 128 // UNROLL, group, inner)

            lax.fori_loop(TOP, (n + 127) // 128, one, 0)

        return carry

    lax.fori_loop(0, used, rest, 0)

    lanes = lax.broadcasted_iota(jnp.int32, (32, 128), 1)

    def pack(i, carry):
        for s in range(2):
            for n in range(2):
                base = (1 - s) * half + i * 256 + n * 128
                a, b, c, d = [acc[pl.ds(pl.multiple_of(base + k * 32, 32), 32), :] for k in range(4)]
                b, c, d = pltpu.roll(b, 96, 1), pltpu.roll(c, 64, 1), pltpu.roll(d, 32, 1)
                row = s * 192 + n * 96
                out_ref[i, pl.ds(row, 32), :] = jnp.where(lanes < 96, a, b)
                out_ref[i, pl.ds(row + 32, 32), :] = jnp.where(lanes < 64, b, c)
                out_ref[i, pl.ds(row + 64, 32), :] = jnp.where(lanes < 32, c, d)
        return carry

    lax.fori_loop(0, half // 256, pack, 0)


def gather_rows(features, target_nodes, first_hop, offset):
    nodes = features.shape[1]
    batches, targets = target_nodes.shape
    rows = batches * targets // 128
    lists = 28
    hbm = pl.BlockSpec(memory_space=pltpu.HBM)
    hops = jnp.moveaxis(first_hop, 1, 0)
    return pl.pallas_call(
        gather_kernel,
        out_shape=jax.ShapeDtypeStruct((batches, 384, 128), jnp.float32),
        in_specs=[pl.BlockSpec(memory_space=pltpu.SMEM)] + [hbm] * 3,
        out_specs=pl.BlockSpec(memory_space=pltpu.VMEM),
        scratch_shapes=[
            pltpu.VMEM(features.shape, features.dtype),
            pltpu.VMEM(target_nodes.shape, jnp.int32),
            pltpu.VMEM(hops.shape, jnp.int32),
            pltpu.VMEM((nodes + 8, 128), jnp.float32),
            pltpu.VMEM((batches * 512 + 8, 128), jnp.float32),
            pltpu.VMEM((lists, rows, 128), jnp.int32),
            pltpu.VMEM((lists, rows, 128), jnp.int32),
            pltpu.VMEM((lists + 4, 128), jnp.int32),
            pltpu.SMEM((lists * TOP * 128,), jnp.int32),
            pltpu.SMEM((lists + 4, 128), jnp.int32),
            pltpu.SMEM((128,), jnp.int32),
            pltpu.SemaphoreType.DMA((lists * TOP + 2,)),
            pltpu.SemaphoreType.DMA((3,)),
        ],
        compiler_params=pltpu.CompilerParams(vmem_limit_bytes=48 * 1024 * 1024),
        name="gather_rows",
    )(offset, features, target_nodes, hops)


MESH = pl.DeviceIdType.MESH
HIGH = lax.Precision.HIGHEST


def run_all(*routes):
    active = list(routes)
    while active:
        for route in list(active):
            try:
                next(route)
            except StopIteration:
                active.remove(route)


def ring_sum(blk, inb, ssem, rsem, base, i, right, left):
    after, before, across = lax.rem(i + 1, 4), lax.rem(i + 3, 4), lax.rem(i + 2, 4)

    def copy(src, k, device):
        return pltpu.make_async_remote_copy(
            src_ref=src,
            dst_ref=inb(k),
            send_sem=ssem.at[base + k],
            recv_sem=rsem.at[base + k],
            device_id=device,
            device_id_type=MESH,
        )

    c0 = copy(blk(across, 0), 0, right)
    c1 = copy(blk(across, 1), 1, left)
    c2 = copy(blk(after, 1), 2, right)
    c3 = copy(blk(before, 0), 3, left)
    c4 = copy(blk(after, 0), 4, right)
    c5 = copy(blk(before, 1), 5, left)
    for c in (c0, c1, c2, c3):
        c.start()
    yield
    c0.wait_recv()
    blk(after, 0)[...] = blk(after, 0)[...] + inb(0)[...]
    c4.start()
    c1.wait_recv()
    blk(before, 1)[...] = blk(before, 1)[...] + inb(1)[...]
    c5.start()
    yield
    c3.wait_recv()
    c2.wait_recv()
    blk(i, 0)[...] = blk(i, 0)[...] + inb(3)[...]
    blk(i, 1)[...] = blk(i, 1)[...] + inb(2)[...]
    yield
    c4.wait_recv()
    blk(i, 0)[...] = blk(i, 0)[...] + inb(4)[...]
    c5.wait_recv()
    blk(i, 1)[...] = blk(i, 1)[...] + inb(5)[...]
    for c in (c0, c1, c2, c3, c4, c5):
        c.wait_send()


def grid_sum(buf, spans, in_wide, in_thin, ssem, rsem, base, x, y, xs, ys):
    def route(h, n, lo, half):
        def wide(d, p):
            at = pl.ds(lo + p * half, half)
            return buf.at[d, :, at] if h == 0 else buf.at[:, d, at]

        def thin(d, p):
            at = pl.ds(lo + p * half, half)
            return buf.at[x, d, at] if h == 0 else buf.at[d, y, at]

        first, second = ((x,) + xs, (y,) + ys) if h == 0 else ((y,) + ys, (x,) + xs)
        yield from ring_sum(wide, lambda k: in_wide.at[n, k], ssem, rsem, base + n * 12, *first)
        yield from ring_sum(thin, lambda k: in_thin.at[n, k], ssem, rsem, base + n * 12 + 6, *second)

    return [route(*span) for span in spans]


def together(routes):
    active = list(routes)
    while active:
        for route in list(active):
            try:
                next(route)
            except StopIteration:
                active.remove(route)
        yield


def grid_gather(buf, spans, ssem, rsem, base, x, y, device):
    def route(n, h, lo, rows):
        at = pl.ds(lo, rows)

        def near(dx, dy):
            return device(dx, dy) if h == 0 else device(dy, dx)

        def place(far, close):
            return buf.at[far, close, at] if h == 0 else buf.at[close, far, at]

        far, close = (x, y) if h == 0 else (y, x)
        started = []

        def send(ref, k, target):
            copy = pltpu.make_async_remote_copy(
                src_ref=ref,
                dst_ref=ref,
                send_sem=ssem.at[base + n * 15 + k],
                recv_sem=rsem.at[base + n * 15 + k],
                device_id=target,
                device_id_type=MESH,
            )
            copy.start()
            started.append(copy)

        for d in (1, 3, 2):
            send(place(far, close), d - 1, near(0, d))
        for d in (1, 3, 2):
            send(place(far, close), 2 + d, near(d, 0))
        firsts = list(started)
        for n2, d in enumerate((1, 3, 2)):
            yield
            firsts[n2].wait_recv()
            source = lax.rem(close + 4 - d, 4)
            for e in (1, 3, 2):
                send(place(far, source), 3 * d + 2 + e, near(e, 0))
        yield
        for copy in started[3:]:
            copy.wait_recv()
        for copy in started:
            copy.wait_send()

    return [route(n, *span) for n, span in enumerate(spans)]


def unpack(ref, x, y, row):
    lane = lax.broadcasted_iota(jnp.int32, (32, 128), 1)
    p = [ref[x, y, pl.ds(row + 32 * n, 32), :] for n in range(3)]
    b = jnp.where(lane < 32, pltpu.roll(p[0], 32, 1), pltpu.roll(p[1], 32, 1))
    c = jnp.where(lane < 64, pltpu.roll(p[1], 64, 1), pltpu.roll(p[2], 64, 1))
    d = pltpu.roll(p[2], 96, 1)
    out = [jnp.where(lane < 96, v, 0.0) for v in (p[0], b, c, d)]
    return jnp.concatenate(out, axis=0)


def split(v):
    hi = v.astype(jnp.bfloat16)
    return hi, (v - hi.astype(jnp.float32)).astype(jnp.bfloat16)


def dot(a, b):
    return jnp.dot(a, b, preferred_element_type=jnp.float32)


def high_dot(a, b, dims=((1,), (0,))):
    return lax.dot_general(a, b, (dims, ((), ())), precision=HIGH, preferred_element_type=jnp.float32)


def exchange_kernel(
    fan_one,
    fan_two,
    parts_ref,
    ws_ref,
    wn_ref,
    hb_ref,
    cs_ref,
    cn_ref,
    cb_ref,
    live_ref,
    links_ref,
    labels_ref,
    hidden_ref,
    sums_ref,
    parts,
    in_wide,
    in_thin,
    weights,
    pre_parts,
    in_core,
    in_z,
    classes_all,
    self_all,
    neigh_all,
    cb_pad,
    label_rows,
    link_pad,
    logit_own,
    logit_core,
    logit_z,
    piece,
    terms,
    in_terms,
    extras,
    in_extras,
    local_sem,
    ssem,
    rsem,
):
    group = lax.axis_index("group")
    m = lax.axis_index("mp")
    x, y = lax.div(group, 4), lax.rem(group, 4)
    z, core = lax.div(m, 2), lax.rem(m, 2)
    groups = in_terms.shape[0]

    def up(i, n):
        return lax.rem(i + n, 4)

    def grid_device(dx, dy):
        return (up(x, dx) * 4 + up(y, dy), m)

    def z_device(dz):
        return (group, up(z, dz) * 2 + core)

    xs = (grid_device(1, 0), grid_device(3, 0))
    ys = (grid_device(0, 1), grid_device(0, 3))
    zs = (z_device(1), z_device(3))
    opposite = z_device(2)
    sibling = (group, z * 2 + 1 - core)
    others = [(lax.rem(group + r, groups), m) for r in range(1, groups)]

    load = pltpu.make_async_copy(parts_ref, parts, local_sem)
    load.start()
    barrier = pltpu.get_barrier_semaphore()
    nears = others + list(zs) + [opposite, sibling]
    for near in nears:
        pl.semaphore_signal(barrier, inc=1, device_id=near, device_id_type=MESH)
    pl.semaphore_wait(barrier, len(nears))
    load.wait()

    def core_copy(src, dst, k):
        return pltpu.make_async_remote_copy(
            src_ref=src,
            dst_ref=dst,
            send_sem=ssem.at[k],
            recv_sem=rsem.at[k],
            device_id=sibling,
            device_id_type=MESH,
        )

    def spread(ref_of, base):
        started = []
        for k, (slot, near) in enumerate(((1, zs[0]), (3, zs[1]), (2, opposite))):
            started.append(
                pltpu.make_async_remote_copy(
                    src_ref=ref_of(0, 0),
                    dst_ref=ref_of(slot, 0),
                    send_sem=ssem.at[base + k],
                    recv_sem=rsem.at[base + k],
                    device_id=near,
                    device_id_type=MESH,
                )
            )
        started.append(core_copy(ref_of(0, 0), ref_of(0, 1), base + 3))
        for copy in started:
            copy.start()
        yield (0, 0)
        started[3].wait_recv()
        yield (0, 1)
        for k, slot in enumerate((1, 3)):
            started[k].wait_recv()
            started.append(core_copy(ref_of(slot, 0), ref_of(slot, 1), base + 3 + slot))
            started[-1].start()
            yield (slot, 0)
        for k, slot in enumerate((1, 3)):
            started[4 + k].wait_recv()
            yield (slot, 1)
        started[2].wait_recv()
        started.append(core_copy(ref_of(2, 0), ref_of(2, 1), base + 5))
        started[-1].start()
        yield (2, 0)
        started[6].wait_recv()
        yield (2, 1)
        for copy in started:
            copy.wait_send()

    used = 0
    width = ws_ref.shape[0]
    targets, hid = hidden_ref.shape
    half_rows = targets // 2
    seeds = labels_ref.shape[1]
    classes = cs_ref.shape[0]

    def half_route(n, base):
        spans = ((0, 2 * n, n * 96, 48), (1, 2 * n + 1, 192 + n * 96, 48))
        yield from together(grid_sum(parts, spans, in_wide, in_thin, ssem, rsem, 0, x, y, xs, ys))
        at = pl.ds(n * half_rows, half_rows)
        own_self = unpack(parts, x, y, n * 96)
        own_neigh = unpack(parts, x, y, 192 + n * 96) / fan_one
        self_all[at, :] = own_self
        neigh_all[at, :] = own_neigh
        neigh_hi, neigh_lo = split(own_neigh)
        left_side = jnp.concatenate([own_self.astype(jnp.bfloat16), neigh_hi, neigh_lo], axis=1)

        def block_of(zz, cc):
            cols = pl.multiple_of((zz * 2 + cc) * hid, hid)
            pre_parts[zz, cc, at] = dot(left_side, weights[:, pl.ds(cols, hid)])

        for zz in range(4):
            block_of(zz, 1 - core)
        copy = core_copy(pre_parts.at[:, 1 - core, at], in_core.at[:, at], base)
        copy.start()
        for zz in range(4):
            block_of(zz, core)
        yield
        copy.wait()
        for zz in range(4):
            pre_parts[zz, core, at] = pre_parts[zz, core, at] + in_core[zz, at]
        quarter = half_rows // 2
        yield from ring_sum(
            lambda d, p: pre_parts.at[d, core, pl.ds(n * half_rows + p * quarter, quarter)],
            lambda k: in_z.at[n, k],
            ssem,
            rsem,
            base + 1,
            z,
            *zs,
        )

    used += 48
    owners = [half_route(n, used + 7 * n) for n in range(2)]
    used += 14
    next(owners[0])

    sent = 160
    for n in range(4):
        for a in range(2):
            for kind in range(2):
                classes_all[n, a, kind, sent:256, :] = jnp.zeros((256 - sent, hid), jnp.float32)
    for kind in range(2):
        classes_all[0, 0, kind, 0:sent, :] = jnp.zeros((sent, hid), jnp.float32)
    classes_all[0, 0, 0, 0:classes, :] = cs_ref[...].astype(jnp.float32)
    classes_all[0, 0, 1, 0:classes, :] = cn_ref[...].astype(jnp.float32)
    class_spread = spread(lambda n, a: classes_all.at[n, a, :, pl.ds(0, sent)], used)
    used += 7
    next(class_spread)
    weights[...] = jnp.zeros_like(weights)
    weights[0:width, :] = ws_ref[...]
    weights[128 : 128 + width, :] = wn_ref[...]
    weights[256 : 256 + width, :] = wn_ref[...]
    next(owners[0])
    next(owners[1])
    cb_pad[...] = jnp.zeros_like(cb_pad)
    cb_pad[:, 0:classes] = cb_ref[...]
    extras[...] = jnp.zeros_like(extras)
    for s in range(seeds):
        label_rows[s : s + 1, :] = jnp.full((1, 256), labels_ref[0, s], jnp.int32)
    seed_cols = lax.broadcasted_iota(jnp.int32, (targets, seeds), 0)
    counted = jnp.zeros((targets, seeds), jnp.float32)
    for k in range(fan_two):
        counted = counted + jnp.where(seed_cols == links_ref[k], 1.0, 0.0)
    link_pad[...] = jnp.zeros_like(link_pad)
    link_pad[:, 0:seeds] = counted
    links_t = link_pad[...]
    links_f = links_t.T[0:seeds].astype(jnp.bfloat16)
    links_b = links_t.astype(jnp.bfloat16)
    target_rows = lax.broadcasted_iota(jnp.int32, (targets, 128), 0)

    def later(route, rounds):
        for _ in range(rounds):
            yield
        yield from route

    run_all(*owners, later(class_spread, 4))

    pre = pre_parts[z, core] + hb_ref[...]
    piece[0, 0] = pre
    alive = (target_rows < live_ref[0]) & (pre > 0.0)
    hidden = jnp.where(alive, pre, 0.0).astype(jnp.bfloat16)
    hidden_ref[...] = hidden
    active = hidden.astype(jnp.float32)
    seed_self = active[0:seeds]
    seed_neigh = dot(links_f, hidden) / fan_two
    rows_cols = ((1,), (1,))
    own_self = high_dot(seed_self, classes_all[0, 0, 0], rows_cols)
    logit_own[...] = own_self + high_dot(seed_neigh, classes_all[0, 0, 1], rows_cols)
    to_core = core_copy(logit_own, logit_core, used)
    used += 1
    to_core.start()
    to_core.wait()
    logit_z[z] = logit_own[...] + logit_core[...]

    def z_sends(ref, base):
        copies = []
        for k, near in enumerate(zs + (opposite,)):
            copies.append(
                pltpu.make_async_remote_copy(
                    src_ref=ref,
                    dst_ref=ref,
                    send_sem=ssem.at[base + k],
                    recv_sem=rsem.at[base + k],
                    device_id=near,
                    device_id_type=MESH,
                )
            )
            copies[-1].start()
        return copies

    sends = z_sends(logit_z.at[z], used)
    used += 3
    pre_spread = spread(lambda n, a: piece.at[n, a], used)
    used += 7
    next(pre_spread)
    self_t = self_all[...].T[0:width].astype(jnp.bfloat16)
    neigh_t_hi, neigh_t_lo = split(neigh_all[...].T[0:width])
    rows_hi = jnp.concatenate([self_t, neigh_t_hi], axis=0)
    for c in sends:
        c.wait()
    logits = (logit_z[0] + logit_z[1]) + (logit_z[2] + logit_z[3]) + cb_pad[...]
    lanes = lax.broadcasted_iota(jnp.int32, logits.shape, 1)
    logits = jnp.where(lanes < classes, logits, -1e30)
    top = jnp.max(logits, axis=1, keepdims=True)
    log_total = jnp.log(jnp.sum(jnp.exp(logits - top), axis=1, keepdims=True)) + top
    onehot = jnp.where(lanes == label_rows[...], 1.0, 0.0)
    losses = log_total - jnp.sum(onehot * logits, axis=1, keepdims=True)
    dlogit = jnp.exp(logits - log_total) - onehot
    dlogit_hi, dlogit_lo = split(dlogit)

    def back(n, across, kind):
        side = classes_all[n, across, kind].astype(jnp.bfloat16)
        return dot(dlogit_hi, side) + dot(dlogit_lo, side)

    def grad_of(n, across):
        low = jnp.zeros((128 - seeds, hid), jnp.float32)
        neigh_hi, neigh_lo = split(jnp.concatenate([back(n, across, 1) / fan_two, low], axis=0))
        top_rows = jnp.concatenate([back(n, across, 0), jnp.zeros((targets - seeds, hid), jnp.float32)], axis=0)
        act = dot(links_b, neigh_hi) + dot(links_b, neigh_lo) + top_rows
        on = (target_rows < live_ref[0]) & (piece[n, across] > 0.0)
        return jnp.where(on, act, 0.0)

    term_base = used
    used += groups

    def term_copy(k, dest, k_recv):
        return pltpu.make_async_remote_copy(
            src_ref=terms.at[k],
            dst_ref=in_terms.at[group],
            send_sem=ssem.at[term_base + k],
            recv_sem=rsem.at[term_base + k_recv],
            device_id=(dest, m),
            device_id_type=MESH,
        )

    dests = {}

    hidden_line = []

    def block_terms(step, n, across):
        zz = lax.rem(z + 4 - n, 4)
        cc = 1 - core if across else core
        grad_pre = grad_of(n, across)
        if step == 0:
            hidden_line.append(jnp.sum(grad_pre, axis=0, keepdims=True))
        g_hi, g_lo = split(grad_pre)
        term = dot(rows_hi, g_hi) + dot(rows_hi, g_lo)
        terms[2 * step] = term[0:width]
        terms[2 * step + 1] = term[width : 2 * width] + dot(neigh_t_lo, g_hi)
        for s in range(2):
            k = 2 * step + s
            dests[k] = dest = zz * 4 + cc * 2 + s

            @pl.when(dest != group)
            def _():
                term_copy(k, dest, group).start()

            @pl.when(dest == group)
            def _():
                in_terms[group] = terms[k]

    block_terms(0, 0, 0)
    block_terms(1, *next(pre_spread))

    dlogit_t = dlogit.T[0:sent]
    class_grads = jnp.concatenate(
        [high_dot(dlogit_t, seed_self), high_dot(dlogit_t, seed_neigh)], axis=0
    )
    per = extras.shape[1]
    for n in range(0, 320, 8):
        extras[n // per, n % per : n % per + 8] = class_grads[n : n + 8]
    row_sum = jnp.sum(dlogit, axis=0, keepdims=True)
    lines = (
        hidden_line[0],
        row_sum[:, 0:128],
        row_sum[:, 128:256],
        jnp.broadcast_to(jnp.sum(losses, axis=0, keepdims=True), (1, 128)),
    )
    for n, line in enumerate(lines):
        extras[320 // per, 320 % per + n : 320 % per + n + 1] = line
    extra_sends = []
    for r in range(1, groups):
        copy = pltpu.make_async_remote_copy(
            src_ref=extras.at[lax.rem(group + r, groups)],
            dst_ref=in_extras.at[r],
            send_sem=ssem.at[used + r - 1],
            recv_sem=rsem.at[used + r - 1],
            device_id=others[r - 1],
            device_id_type=MESH,
        )
        copy.start()
        extra_sends.append(copy)
    used += groups - 1

    for step in range(2, groups // 2):
        block_terms(step, *next(pre_spread))
    run_all(pre_spread)

    for copy in extra_sends:
        copy.wait_recv()
    total = extras[group]
    for r in range(1, groups):
        total = total + in_extras[r]
    sums_ref[x, y, width : width + per] = total
    for source in range(groups):

        @pl.when(source != group)
        def _():
            pltpu.make_async_remote_copy(
                src_ref=terms.at[0],
                dst_ref=in_terms.at[source],
                send_sem=ssem.at[term_base],
                recv_sem=rsem.at[term_base + source],
                device_id=(source, m),
                device_id_type=MESH,
            ).wait_recv()

    total = in_terms[0]
    for source in range(1, groups):
        total = total + in_terms[source]
    sums_ref[x, y, 0:width] = total
    spans = ((0, 0, 56), (1, 56, 64))
    last = grid_gather(sums_ref, spans, ssem, rsem, used, x, y, grid_device)
    used += 30
    for route in last:
        next(route)
    for copy in extra_sends:
        copy.wait_send()
    for k in range(groups):
        dest = dests[k]

        @pl.when(dest != group)
        def _():
            term_copy(k, dest, group).wait_send()

    run_all(*last)
    assert used <= SEMS


SEMS = 160


def finish_kernel(scale, hidden_ref, sums_ref, *outs):
    hidden_out, self_out, neigh_out, hb_out, cs_out, cn_out, cb_out, loss_out, lines = outs
    width = self_out.shape[0]
    hid = hidden_ref.shape[1]
    groups, rows = sums_ref.shape[:2]
    per = rows - width
    hidden_out[...] = hidden_ref[...]
    for n in range(groups):
        out = neigh_out if n % 2 else self_out
        at = n // 2 * hid
        out[:, at : at + hid] = sums_ref[n, 0:width, :]
        lines[n * per : n * per + per, :] = sums_ref[n, width:rows, :]
    classes = cs_out.shape[0]
    cs_out[...] = lines[0:classes, :]
    cn_out[...] = lines[160 : 160 + classes, :]
    hb_out[...] = lines[320:321, :]
    cb_out[:, 0:128] = lines[321:322, :]
    cb_out[:, 128:classes] = lines[322:323, 0 : classes - 128]
    loss_out[...] = lines[323:324, :] * scale


def body(
    node_features,
    target_nodes,
    first_hop,
    live_counts,
    seed_links,
    seed_labels,
    self_weight,
    neigh_weight,
    hidden_bias,
    class_self,
    class_neigh,
    class_bias,
):
    node_rows = node_features.shape[1]
    batches, targets = target_nodes.shape
    fan_one = first_hop.shape[1]
    seeds, fan_two = seed_links.shape[1:]
    hid = hidden_bias.shape[0]
    width, hidden_all = self_weight.shape
    classes = class_bias.shape[0]
    offset = (lax.axis_index("group") * node_rows).astype(jnp.int32)[None]
    parts = gather_rows(node_features, target_nodes, first_hop, offset).reshape(4, 4, 384, 128)
    f32, vmem = jnp.float32, pl.BlockSpec(memory_space=pltpu.VMEM)
    smem = pl.BlockSpec(memory_space=pltpu.SMEM)
    shapes = [
        ((4, 4, 384, 128), f32),
        ((4, 6, 4, 48, 128), f32),
        ((4, 6, 48, 128), f32),
        ((384, hidden_all), jnp.bfloat16),
        ((4, 2, targets, hid), f32),
        ((4, targets, hid), f32),
        ((2, 6, targets // 4, hid), f32),
        ((4, 2, 2, 256, hid), f32),
        ((targets, 128), f32),
        ((targets, 128), f32),
        ((1, 256), f32),
        ((seeds, 256), jnp.int32),
        ((targets, 128), f32),
        ((seeds, 256), f32),
        ((seeds, 256), f32),
        ((4, seeds, 256), f32),
        ((4, 2, targets, hid), f32),
        ((16, width, 128), f32),
        ((16, width, 128), f32),
        ((16, 24, 128), f32),
        ((16, 24, 128), f32),
    ]
    hidden_layer, sums = pl.pallas_call(
        functools.partial(exchange_kernel, fan_one, fan_two),
        out_shape=(
            jax.ShapeDtypeStruct((targets, hid), jnp.bfloat16),
            jax.ShapeDtypeStruct((4, 4, width + 24, 128), f32),
        ),
        in_specs=[pl.BlockSpec(memory_space=pl.ANY)] + [vmem] * 6 + [smem, vmem, smem],
        out_specs=(vmem, vmem),
        scratch_shapes=[pltpu.VMEM(shape, kind) for shape, kind in shapes]
        + [
            pltpu.SemaphoreType.DMA,
            pltpu.SemaphoreType.DMA((SEMS,)),
            pltpu.SemaphoreType.DMA((SEMS,)),
        ],
        compiler_params=pltpu.CompilerParams(
            collective_id=0, has_side_effects=True, vmem_limit_bytes=48 * 1024 * 1024
        ),
        name="exchange",
    )(
        parts,
        self_weight,
        neigh_weight,
        hidden_bias[None],
        class_self.T,
        class_neigh.T,
        class_bias[None],
        live_counts,
        jnp.transpose(seed_links, (2, 0, 1)),
        seed_labels,
    )
    outs = pl.pallas_call(
        functools.partial(finish_kernel, 1.0 / (batches * seeds)),
        out_shape=(
            jax.ShapeDtypeStruct((targets, hid), jnp.bfloat16),
            jax.ShapeDtypeStruct((width, hidden_all), f32),
            jax.ShapeDtypeStruct((width, hidden_all), f32),
            jax.ShapeDtypeStruct((1, hid), f32),
            jax.ShapeDtypeStruct((classes, hid), f32),
            jax.ShapeDtypeStruct((classes, hid), f32),
            jax.ShapeDtypeStruct((1, classes), f32),
            jax.ShapeDtypeStruct((1, 128), f32),
        ),
        in_specs=[vmem] * 2,
        out_specs=(vmem,) * 8,
        scratch_shapes=[pltpu.VMEM((16 * 24, 128), f32)],
        name="finish",
    )(hidden_layer, sums.reshape(16, width + 24, 128))
    return (
        outs[0],
        outs[1],
        outs[2],
        outs[3][0],
        outs[4].T,
        outs[5].T,
        outs[6][0],
        outs[7][0, 0],
    )


def solution(mesh):
    in_specs = (
        P("mp", "group"),
        P(),
        P(),
        P("group"),
        P("group", None, None),
        P("group", None),
        P("mp", None),
        P("mp", None),
        P("mp"),
        P("mp", None),
        P("mp", None),
        P(),
    )
    out_specs = (
        P("group", "mp"),
        P("mp", None),
        P("mp", None),
        P("mp"),
        P("mp", None),
        P("mp", None),
        P(),
        P(),
    )
    return jax.shard_map(body, mesh=mesh, in_specs=in_specs, out_specs=out_specs, check_vma=False)
```

```python
import functools
import jax
import jax.numpy as jnp
from jax import lax
from jax.experimental import pallas as pl
from jax.experimental.pallas import tpu as pltpu
from jax.sharding import PartitionSpec as P

UNROLL = 16
TOP = 3
BLOCK = 4
TURNS = 18


def gather_kernel(offset_ref, feat_hbm, targets_hbm, hops_hbm, out_ref, feat_ref, targets_ref, hops_ref, table, acc, ids, codes, counts, first_s, counts_s, extra_s, sems, load_sems):
    loads = [
        pltpu.make_async_copy(src, dst, load_sems.at[n])
        for n, (src, dst) in enumerate(((hops_hbm, hops_ref), (targets_hbm, targets_ref), (feat_hbm, feat_ref)))
    ]
    for load in loads:
        load.start()
    width, nodes = feat_ref.shape
    lists, rows = ids.shape[:2]
    fan, batches, targets = hops_ref.shape
    used = fan + 1
    half = rows * 128
    slots = 2 * half
    cols = targets // 128
    loads[0].wait()
    loads[1].wait()
    for n in range(cols):
        at, wide = pl.ds(n * batches, batches), slice(n * 128, n * 128 + 128)
        ids[0:fan, at] = hops_ref[:, :, wide] - offset_ref[0]
        ids[fan, at] = targets_ref[:, wide] - offset_ref[0]
    ids[used:lists] = jnp.full((lists - used, rows, 128), -1, jnp.int32)
    lane = lax.broadcasted_iota(jnp.int32, (BLOCK, rows, 128), 2)
    sub = lax.broadcasted_iota(jnp.int32, (BLOCK, rows, 128), 1)
    outer = lax.broadcasted_iota(jnp.int32, (BLOCK, rows, 128), 0)
    row_i = lax.broadcasted_iota(jnp.int32, (128, 128), 0)
    col_i = lax.broadcasted_iota(jnp.int32, (128, 128), 1)
    before = jnp.where(row_i < col_i, 1.0, 0.0).astype(jnp.bfloat16)
    ones = jnp.ones((128, 128), jnp.bfloat16)
    row_r = lax.broadcasted_iota(jnp.int32, (BLOCK * rows, BLOCK * rows), 0)
    col_r = lax.broadcasted_iota(jnp.int32, (BLOCK * rows, BLOCK * rows), 1)
    same = (row_r // rows) == (col_r // rows)
    above = jnp.where(same & (col_r < row_r), 1.0, 0.0).astype(jnp.bfloat16)
    shift = (nodes - 1).bit_length()
    steps = (half - 1).bit_length()
    flag = 1 << (shift + steps)

    def turn(i):
        at = pl.multiple_of(i * 128, 128)
        part = feat_ref[:, pl.ds(at, 128)].astype(jnp.float32)
        part = jnp.concatenate([part, jnp.zeros((128 - width, 128), jnp.float32)], axis=0)
        table[pl.ds(at, 128), :] = part.T

    def compact(q, carry):
        local = ids[pl.ds(q * BLOCK, BLOCK)]
        inside = (local >= 0) & (local < nodes)
        out_b = jnp.where(inside, 0.0, 1.0).reshape(BLOCK * rows, 128).astype(jnp.bfloat16)
        pref = jnp.dot(out_b, before, preferred_element_type=jnp.float32)
        total = jnp.dot(out_b, ones, preferred_element_type=jnp.float32)
        scan = jnp.dot(above, total.astype(jnp.bfloat16), preferred_element_type=jnp.float32)
        moved = (pref + scan).reshape(BLOCK, rows, 128).astype(jnp.int32)
        total = total.reshape(BLOCK, rows, 128)
        for b in range(BLOCK):
            missing = jnp.sum(total[b], axis=0, keepdims=True)
            counts[pl.ds(q * BLOCK + b, 1), :] = (half - missing).astype(jnp.int32)
        x = jnp.where(inside, flag | (moved << shift) | local, 0)
        for j in range(steps):
            d = 1 << j
            if j < 7:
                y = pltpu.roll(x, 128 - d, 2)
                y = jnp.where(lane < 128 - d, y, pltpu.roll(y, rows - 1, 1))
            else:
                y = pltpu.roll(x, rows - d // 128, 1)
            bit = 1 << (shift + j)
            x = jnp.where((y & bit) != 0, y, jnp.where((x & bit) != 0, 0, x))
        place = sub * 128 + lane + ((x >> shift) & (half - 1))
        row = place >> 7
        slot = (row % batches) * targets + (row // batches) * 128 + (place & 127)
        slot = slot + jnp.where(q * BLOCK + outer == fan, half, 0)
        code = jnp.where(x != 0, (slot << 15) | (x & (nodes - 1)), (slots << 15) | nodes)
        codes[pl.ds(q * BLOCK, BLOCK)] = code
        for n in range(TURNS):
            turn(q * TURNS + n)
        return carry

    loads[2].wait()
    lax.fori_loop(0, lists // BLOCK, compact, 0)
    copy_counts = pltpu.make_async_copy(counts, counts_s, sems.at[0])
    copy_counts.start()
    copies = []
    for j in range(used):
        for r in range(TOP):
            n = j * TOP + r
            copy = pltpu.make_async_copy(codes.at[j, r], first_s.at[pl.ds(n * 128, 128)], sems.at[n + 2])
            copy.start()
            copies.append(copy)

    def turn_rest(i, carry):
        turn(i)
        return carry

    lax.fori_loop(lists // BLOCK * TURNS, nodes // 128, turn_rest, 0)
    table[pl.ds(nodes, 8), :] = jnp.zeros((8, 128), jnp.float32)

    def clear(i, carry):
        acc[pl.ds(pl.multiple_of(i * 128, 128), 128), :] = jnp.zeros((128, 128), jnp.float32)
        return carry

    lax.fori_loop(0, slots // 128, clear, 0)
    acc[pl.ds(slots, 8), :] = jnp.zeros((8, 128), jnp.float32)
    copy_counts.wait()
    for copy in copies:
        copy.wait()

    def add_group(ref, base):
        code = [ref[base + u] for u in range(UNROLL)]
        at = [c >> 15 for c in code]
        rows = [table[pl.ds(c & 32767, 1), :] for c in code]
        olds = [acc[pl.ds(a, 1), :] for a in at]
        for a, old, row in zip(at, olds, rows):
            acc[pl.ds(a, 1), :] = old + row

    span = TOP * 128

    def step(state):
        j, k = state
        add_group(first_s, j * span + k)
        k = k + UNROLL
        done = k >= jnp.minimum(counts_s[j, 0], span)
        return jnp.where(done, j + 1, j), jnp.where(done, 0, k)

    lax.while_loop(lambda state: state[0] < used, step, (0, 0))

    def rest(j, carry):
        n = counts_s[j, 0]

        @pl.when(n > span)
        def _():
            def one(r, inner):
                copy = pltpu.make_async_copy(codes.at[j, r], extra_s, sems.at[1])
                copy.start()
                copy.wait()

                def group(i, inner2):
                    add_group(extra_s, i * UNROLL)
                    return inner2

                return lax.fori_loop(0, 128 // UNROLL, group, inner)

            lax.fori_loop(TOP, (n + 127) // 128, one, 0)

        return carry

    lax.fori_loop(0, used, rest, 0)

    lanes = lax.broadcasted_iota(jnp.int32, (32, 128), 1)

    def pack(i, carry):
        for s in range(2):
            for n in range(2):
                base = (1 - s) * half + i * 256 + n * 128
                a, b, c, d = [acc[pl.ds(pl.multiple_of(base + k * 32, 32), 32), :] for k in range(4)]
                b, c, d = pltpu.roll(b, 96, 1), pltpu.roll(c, 64, 1), pltpu.roll(d, 32, 1)
                row = s * 192 + n * 96
                out_ref[i, pl.ds(row, 32), :] = jnp.where(lanes < 96, a, b)
                out_ref[i, pl.ds(row + 32, 32), :] = jnp.where(lanes < 64, b, c)
                out_ref[i, pl.ds(row + 64, 32), :] = jnp.where(lanes < 32, c, d)
        return carry

    lax.fori_loop(0, half // 256, pack, 0)


def gather_rows(features, target_nodes, first_hop, offset):
    nodes = features.shape[1]
    batches, targets = target_nodes.shape
    rows = batches * targets // 128
    lists = 28
    hbm = pl.BlockSpec(memory_space=pltpu.HBM)
    hops = jnp.moveaxis(first_hop, 1, 0)
    return pl.pallas_call(
        gather_kernel,
        out_shape=jax.ShapeDtypeStruct((batches, 384, 128), jnp.float32),
        in_specs=[pl.BlockSpec(memory_space=pltpu.SMEM)] + [hbm] * 3,
        out_specs=pl.BlockSpec(memory_space=pltpu.VMEM),
        scratch_shapes=[
            pltpu.VMEM(features.shape, features.dtype),
            pltpu.VMEM(target_nodes.shape, jnp.int32),
            pltpu.VMEM(hops.shape, jnp.int32),
            pltpu.VMEM((nodes + 8, 128), jnp.float32),
            pltpu.VMEM((batches * 512 + 8, 128), jnp.float32),
            pltpu.VMEM((lists, rows, 128), jnp.int32),
            pltpu.VMEM((lists, rows, 128), jnp.int32),
            pltpu.VMEM((lists + 4, 128), jnp.int32),
            pltpu.SMEM((lists * TOP * 128,), jnp.int32),
            pltpu.SMEM((lists + 4, 128), jnp.int32),
            pltpu.SMEM((128,), jnp.int32),
            pltpu.SemaphoreType.DMA((lists * TOP + 2,)),
            pltpu.SemaphoreType.DMA((3,)),
        ],
        compiler_params=pltpu.CompilerParams(vmem_limit_bytes=48 * 1024 * 1024),
        name="gather_rows",
    )(offset, features, target_nodes, hops)


MESH = pl.DeviceIdType.MESH
HIGH = lax.Precision.HIGHEST


def run_all(*routes):
    active = list(routes)
    while active:
        for route in list(active):
            try:
                next(route)
            except StopIteration:
                active.remove(route)


def ring_sum(blk, inb, ssem, rsem, base, i, right, left):
    after, before, across = lax.rem(i + 1, 4), lax.rem(i + 3, 4), lax.rem(i + 2, 4)

    def copy(src, k, device):
        return pltpu.make_async_remote_copy(
            src_ref=src,
            dst_ref=inb(k),
            send_sem=ssem.at[base + k],
            recv_sem=rsem.at[base + k],
            device_id=device,
            device_id_type=MESH,
        )

    c0 = copy(blk(across, 0), 0, right)
    c1 = copy(blk(across, 1), 1, left)
    c2 = copy(blk(after, 1), 2, right)
    c3 = copy(blk(before, 0), 3, left)
    c4 = copy(blk(after, 0), 4, right)
    c5 = copy(blk(before, 1), 5, left)
    for c in (c0, c1, c2, c3):
        c.start()
    yield
    c0.wait_recv()
    blk(after, 0)[...] = blk(after, 0)[...] + inb(0)[...]
    c4.start()
    c1.wait_recv()
    blk(before, 1)[...] = blk(before, 1)[...] + inb(1)[...]
    c5.start()
    yield
    c3.wait_recv()
    c2.wait_recv()
    blk(i, 0)[...] = blk(i, 0)[...] + inb(3)[...]
    blk(i, 1)[...] = blk(i, 1)[...] + inb(2)[...]
    yield
    c4.wait_recv()
    blk(i, 0)[...] = blk(i, 0)[...] + inb(4)[...]
    c5.wait_recv()
    blk(i, 1)[...] = blk(i, 1)[...] + inb(5)[...]
    for c in (c0, c1, c2, c3, c4, c5):
        c.wait_send()


def grid_sum(buf, spans, in_wide, in_thin, ssem, rsem, base, x, y, xs, ys, device):
    def route(h, n, lo, half):
        def wide(d, p):
            at = pl.ds(lo + p * half, half)
            return buf.at[d, :, at] if h == 0 else buf.at[:, d, at]

        def thin(d):
            at = pl.ds(lo, 2 * half)
            return buf.at[x, d, at] if h == 0 else buf.at[d, y, at]

        first = (x,) + xs if h == 0 else (y,) + ys
        yield from ring_sum(wide, lambda k: in_wide.at[n, k], ssem, rsem, base + n * 9, *first)
        i = y if h == 0 else x
        copies = []
        for k, step in enumerate((1, 3, 2)):
            copies.append(
                pltpu.make_async_remote_copy(
                    src_ref=thin(lax.rem(i + step, 4)),
                    dst_ref=in_thin.at[n, k],
                    send_sem=ssem.at[base + n * 9 + 6 + k],
                    recv_sem=rsem.at[base + n * 9 + 6 + k],
                    device_id=device(0, step) if h == 0 else device(step, 0),
                    device_id_type=MESH,
                )
            )
            copies[-1].start()
        yield
        for k, copy in enumerate(copies):
            copy.wait_recv()
            thin(i)[...] = thin(i)[...] + in_thin[n, k]
        for copy in copies:
            copy.wait_send()

    return [route(*span) for span in spans]


def together(routes):
    active = list(routes)
    while active:
        for route in list(active):
            try:
                next(route)
            except StopIteration:
                active.remove(route)
        yield


def grid_gather(buf, spans, ssem, rsem, base, x, y, device):
    def route(n, h, lo, rows):
        at = pl.ds(lo, rows)

        def near(dx, dy):
            return device(dx, dy) if h == 0 else device(dy, dx)

        def place(far, close):
            return buf.at[far, close, at] if h == 0 else buf.at[close, far, at]

        far, close = (x, y) if h == 0 else (y, x)
        started = []

        def send(ref, k, target):
            copy = pltpu.make_async_remote_copy(
                src_ref=ref,
                dst_ref=ref,
                send_sem=ssem.at[base + n * 15 + k],
                recv_sem=rsem.at[base + n * 15 + k],
                device_id=target,
                device_id_type=MESH,
            )
            copy.start()
            started.append(copy)

        for d in (1, 3, 2):
            send(place(far, close), d - 1, near(0, d))
        for d in (1, 3, 2):
            send(place(far, close), 2 + d, near(d, 0))
        firsts = list(started)
        for n2, d in enumerate((1, 3, 2)):
            yield
            firsts[n2].wait_recv()
            source = lax.rem(close + 4 - d, 4)
            for e in (1, 3, 2):
                send(place(far, source), 3 * d + 2 + e, near(e, 0))
        yield
        for copy in started[3:]:
            copy.wait_recv()
        for copy in started:
            copy.wait_send()

    return [route(n, *span) for n, span in enumerate(spans)]


def unpack(ref, x, y, row):
    lane = lax.broadcasted_iota(jnp.int32, (32, 128), 1)
    p = [ref[x, y, pl.ds(row + 32 * n, 32), :] for n in range(3)]
    b = jnp.where(lane < 32, pltpu.roll(p[0], 32, 1), pltpu.roll(p[1], 32, 1))
    c = jnp.where(lane < 64, pltpu.roll(p[1], 64, 1), pltpu.roll(p[2], 64, 1))
    d = pltpu.roll(p[2], 96, 1)
    out = [jnp.where(lane < 96, v, 0.0) for v in (p[0], b, c, d)]
    return jnp.concatenate(out, axis=0)


def split(v):
    hi = v.astype(jnp.bfloat16)
    return hi, (v - hi.astype(jnp.float32)).astype(jnp.bfloat16)


def dot(a, b):
    return jnp.dot(a, b, preferred_element_type=jnp.float32)


def high_dot(a, b, dims=((1,), (0,))):
    return lax.dot_general(a, b, (dims, ((), ())), precision=HIGH, preferred_element_type=jnp.float32)


def exchange_kernel(
    fan_one,
    fan_two,
    parts_ref,
    ws_ref,
    wn_ref,
    hb_ref,
    cs_ref,
    cn_ref,
    cb_ref,
    live_ref,
    links_ref,
    labels_ref,
    hidden_ref,
    sums_ref,
    parts,
    in_wide,
    in_thin,
    weights,
    pre_parts,
    in_core,
    in_z,
    classes_all,
    self_all,
    neigh_all,
    cb_pad,
    acts,
    label_rows,
    link_pad,
    logit_own,
    logit_core,
    logit_z,
    piece,
    terms,
    in_terms,
    extras,
    in_extras,
    local_sem,
    ssem,
    rsem,
):
    group = lax.axis_index("group")
    m = lax.axis_index("mp")
    x, y = lax.div(group, 4), lax.rem(group, 4)
    z, core = lax.div(m, 2), lax.rem(m, 2)
    groups = in_terms.shape[0]

    def up(i, n):
        return lax.rem(i + n, 4)

    def grid_device(dx, dy):
        return (up(x, dx) * 4 + up(y, dy), m)

    def z_device(dz):
        return (group, up(z, dz) * 2 + core)

    xs = (grid_device(1, 0), grid_device(3, 0))
    ys = (grid_device(0, 1), grid_device(0, 3))
    zs = (z_device(1), z_device(3))
    opposite = z_device(2)
    sibling = (group, z * 2 + 1 - core)
    others = [(lax.rem(group + r, groups), m) for r in range(1, groups)]

    load = pltpu.make_async_copy(parts_ref, parts, local_sem)
    load.start()
    barrier = pltpu.get_barrier_semaphore()
    nears = others + list(zs) + [opposite, sibling]
    for near in nears:
        pl.semaphore_signal(barrier, inc=1, device_id=near, device_id_type=MESH)
    pl.semaphore_wait(barrier, len(nears))
    load.wait()

    def core_copy(src, dst, k):
        return pltpu.make_async_remote_copy(
            src_ref=src,
            dst_ref=dst,
            send_sem=ssem.at[k],
            recv_sem=rsem.at[k],
            device_id=sibling,
            device_id_type=MESH,
        )

    def spread(ref_of, base):
        started = []
        for k, (slot, near) in enumerate(((1, zs[0]), (3, zs[1]), (2, opposite))):
            started.append(
                pltpu.make_async_remote_copy(
                    src_ref=ref_of(0, 0),
                    dst_ref=ref_of(slot, 0),
                    send_sem=ssem.at[base + k],
                    recv_sem=rsem.at[base + k],
                    device_id=near,
                    device_id_type=MESH,
                )
            )
        started.append(core_copy(ref_of(0, 0), ref_of(0, 1), base + 3))
        for k in (0, 1, 3):
            started[k].start()
        yield (0, 0)
        started[2].start()
        yield (0, 0)
        started[3].wait_recv()
        yield (0, 1)
        for k, slot in enumerate((1, 3)):
            started[k].wait_recv()
            started.append(core_copy(ref_of(slot, 0), ref_of(slot, 1), base + 3 + slot))
            started[-1].start()
            yield (slot, 0)
        for k, slot in enumerate((1, 3)):
            started[4 + k].wait_recv()
            yield (slot, 1)
        started[2].wait_recv()
        started.append(core_copy(ref_of(2, 0), ref_of(2, 1), base + 5))
        started[-1].start()
        yield (2, 0)
        started[6].wait_recv()
        yield (2, 1)
        for copy in started:
            copy.wait_send()

    used = 0
    width = ws_ref.shape[0]
    targets, hid = hidden_ref.shape
    half_rows = targets // 2
    seeds = labels_ref.shape[1]
    classes = cs_ref.shape[0]

    def half_route(n, base):
        spans = ((0, 2 * n, n * 96, 48), (1, 2 * n + 1, 192 + n * 96, 48))
        yield from together(grid_sum(parts, spans, in_wide, in_thin, ssem, rsem, 0, x, y, xs, ys, grid_device))
        at = pl.ds(n * half_rows, half_rows)
        own_self = unpack(parts, x, y, n * 96)
        own_neigh = unpack(parts, x, y, 192 + n * 96) / fan_one
        self_all[at, :] = own_self
        neigh_all[at, :] = own_neigh
        neigh_hi, neigh_lo = split(own_neigh)
        left_side = jnp.concatenate([own_self.astype(jnp.bfloat16), neigh_hi, neigh_lo], axis=1)

        def block_of(zz, cc):
            cols = pl.multiple_of((zz * 2 + cc) * hid, hid)
            pre_parts[zz, cc, at] = dot(left_side, weights[:, pl.ds(cols, hid)])

        for zz in range(4):
            block_of(zz, 1 - core)
        copy = core_copy(pre_parts.at[:, 1 - core, at], in_core.at[:, at], base)
        copy.start()
        for zz in range(4):
            block_of(zz, core)
        yield
        copy.wait()
        for zz in range(4):
            pre_parts[zz, core, at] = pre_parts[zz, core, at] + in_core[zz, at]
        quarter = half_rows // 2
        yield from ring_sum(
            lambda d, p: pre_parts.at[d, core, pl.ds(n * half_rows + p * quarter, quarter)],
            lambda k: in_z.at[n, k],
            ssem,
            rsem,
            base + 1,
            z,
            *zs,
        )

    used += 36
    owners = [half_route(n, used + 7 * n) for n in range(2)]
    used += 14
    next(owners[0])
    next(owners[1])

    sent = 160
    classes_all[:, sent:256, :] = jnp.zeros((2, 256 - sent, 8 * hid), jnp.float32)
    classes_all[:, 0:sent, 0:hid] = jnp.zeros((2, sent, hid), jnp.float32)
    classes_all[0, 0:classes, 0:hid] = cs_ref[...].astype(jnp.float32)
    classes_all[1, 0:classes, 0:hid] = cn_ref[...].astype(jnp.float32)
    class_spread = spread(
        lambda n, a: classes_all.at[:, pl.ds(0, sent), pl.ds((n * 2 + a) * hid, hid)], used
    )
    used += 7
    next(class_spread)
    next(class_spread)
    weights[...] = jnp.zeros_like(weights)
    weights[0:width, :] = ws_ref[...]
    weights[128 : 128 + width, :] = wn_ref[...]
    weights[256 : 256 + width, :] = wn_ref[...]
    cb_pad[...] = jnp.zeros_like(cb_pad)
    cb_pad[:, 0:classes] = cb_ref[...]
    extras[...] = jnp.zeros_like(extras)
    for s in range(seeds):
        label_rows[s : s + 1, :] = jnp.full((1, 256), labels_ref[0, s], jnp.int32)
    seed_cols = lax.broadcasted_iota(jnp.int32, (targets, seeds), 0)
    counted = jnp.zeros((targets, seeds), jnp.float32)
    for k in range(fan_two):
        counted = counted + jnp.where(seed_cols == links_ref[k], 1.0, 0.0)
    link_pad[...] = jnp.zeros_like(link_pad)
    link_pad[:, 0:seeds] = counted
    links_t = link_pad[...]
    links_f = links_t.T[0:seeds].astype(jnp.bfloat16)
    links_b = links_t.astype(jnp.bfloat16)
    target_rows = lax.broadcasted_iota(jnp.int32, (targets, 128), 0)

    run_all(*owners)

    pre = pre_parts[z, core] + hb_ref[...]
    piece[0, 0] = pre
    pre_spread = spread(lambda n, a: piece.at[n, a], used)
    used += 7
    next(pre_spread)
    alive = (target_rows < live_ref[0]) & (pre > 0.0)
    hidden = jnp.where(alive, pre, 0.0).astype(jnp.bfloat16)
    hidden_ref[...] = hidden
    active = hidden.astype(jnp.float32)
    seed_self = active[0:seeds]
    seed_neigh = dot(links_f, hidden) / fan_two
    rows_cols = ((1,), (1,))
    own_self = high_dot(seed_self, classes_all[0, :, 0:hid], rows_cols)
    logit_own[...] = own_self + high_dot(seed_neigh, classes_all[1, :, 0:hid], rows_cols)
    to_core = core_copy(logit_own, logit_core, used)
    used += 1
    to_core.start()
    to_core.wait()
    logit_z[z] = logit_own[...] + logit_core[...]

    def z_sends(ref, base):
        copies = []
        for k, near in enumerate(zs + (opposite,)):
            copies.append(
                pltpu.make_async_remote_copy(
                    src_ref=ref,
                    dst_ref=ref,
                    send_sem=ssem.at[base + k],
                    recv_sem=rsem.at[base + k],
                    device_id=near,
                    device_id_type=MESH,
                )
            )
            copies[-1].start()
        return copies

    sends = z_sends(logit_z.at[z], used)
    used += 3
    next(pre_spread)
    run_all(class_spread)
    self_t = self_all[...].T[0:width].astype(jnp.bfloat16)
    neigh_t_hi, neigh_t_lo = split(neigh_all[...].T[0:width])
    rows_three = jnp.concatenate([self_t, neigh_t_hi, neigh_t_lo], axis=0)
    for c in sends:
        c.wait()
    logits = (logit_z[0] + logit_z[1]) + (logit_z[2] + logit_z[3]) + cb_pad[...]
    lanes = lax.broadcasted_iota(jnp.int32, logits.shape, 1)
    logits = jnp.where(lanes < classes, logits, -1e30)
    top = jnp.max(logits, axis=1, keepdims=True)
    log_total = jnp.log(jnp.sum(jnp.exp(logits - top), axis=1, keepdims=True)) + top
    onehot = jnp.where(lanes == label_rows[...], 1.0, 0.0)
    losses = log_total - jnp.sum(onehot * logits, axis=1, keepdims=True)
    dlogit = jnp.exp(logits - log_total) - onehot
    dlogit_two = jnp.concatenate(split(dlogit), axis=0)

    def back(kind):
        both = dot(dlogit_two, classes_all[kind].astype(jnp.bfloat16))
        return both[0:seeds] + both[seeds : 2 * seeds]

    back_neigh = jnp.concatenate(
        [back(1) / fan_two, jnp.zeros((128 - seeds, 8 * hid), jnp.float32)], axis=0
    )
    links_two = jnp.concatenate([links_b, links_b], axis=1)
    acts[...] = dot(links_two, jnp.concatenate(split(back_neigh), axis=0))
    acts[0:seeds, :] = acts[0:seeds, :] + back(0)
    live_rows = target_rows < live_ref[0]

    def grad_of(n, across):
        at = (n * 2 + across) * hid
        return jnp.where(live_rows & (piece[n, across] > 0.0), acts[:, at : at + hid], 0.0)

    term_base = used
    used += groups

    def term_copy(k, dest, k_recv):
        return pltpu.make_async_remote_copy(
            src_ref=terms.at[k],
            dst_ref=in_terms.at[group],
            send_sem=ssem.at[term_base + k],
            recv_sem=rsem.at[term_base + k_recv],
            device_id=(dest, m),
            device_id_type=MESH,
        )

    dests = {}

    hidden_line = []

    def block_terms(step, n, across):
        zz = lax.rem(z + 4 - n, 4)
        cc = 1 - core if across else core
        grad_pre = grad_of(n, across)
        if step == 0:
            hidden_line.append(jnp.sum(grad_pre, axis=0, keepdims=True))
        term = dot(rows_three, jnp.concatenate(split(grad_pre), axis=1))
        terms[2 * step] = term[0:width, 0:hid] + term[0:width, hid : 2 * hid]
        neigh_term = term[width : 2 * width, 0:hid] + term[width : 2 * width, hid : 2 * hid]
        terms[2 * step + 1] = neigh_term + term[2 * width : 3 * width, 0:hid]
        for s in range(2):
            k = 2 * step + s
            dests[k] = dest = zz * 4 + cc * 2 + s

            @pl.when(dest != group)
            def _():
                term_copy(k, dest, group).start()

            @pl.when(dest == group)
            def _():
                in_terms[group] = terms[k]

    block_terms(0, 0, 0)
    block_terms(1, *next(pre_spread))

    dlogit_t = dlogit.T[0:sent]
    class_grads = jnp.concatenate(
        [high_dot(dlogit_t, seed_self), high_dot(dlogit_t, seed_neigh)], axis=0
    )
    per = extras.shape[1]
    for n in range(0, 320, 8):
        extras[n // per, n % per : n % per + 8] = class_grads[n : n + 8]
    row_sum = jnp.sum(dlogit, axis=0, keepdims=True)
    lines = (
        hidden_line[0],
        row_sum[:, 0:128],
        row_sum[:, 128:256],
        jnp.broadcast_to(jnp.sum(losses, axis=0, keepdims=True), (1, 128)),
    )
    for n, line in enumerate(lines):
        extras[320 // per, 320 % per + n : 320 % per + n + 1] = line
    extra_sends = []
    for r in range(1, groups):
        copy = pltpu.make_async_remote_copy(
            src_ref=extras.at[lax.rem(group + r, groups)],
            dst_ref=in_extras.at[r],
            send_sem=ssem.at[used + r - 1],
            recv_sem=rsem.at[used + r - 1],
            device_id=others[r - 1],
            device_id_type=MESH,
        )
        copy.start()
        extra_sends.append(copy)
    used += groups - 1

    for step in range(2, groups // 2):
        block_terms(step, *next(pre_spread))
    run_all(pre_spread)

    for copy in extra_sends:
        copy.wait_recv()
    total = extras[group]
    for r in range(1, groups):
        total = total + in_extras[r]
    sums_ref[x, y, width : width + per] = total
    for source in range(groups):

        @pl.when(source != group)
        def _():
            pltpu.make_async_remote_copy(
                src_ref=terms.at[0],
                dst_ref=in_terms.at[source],
                send_sem=ssem.at[term_base],
                recv_sem=rsem.at[term_base + source],
                device_id=(source, m),
                device_id_type=MESH,
            ).wait_recv()

    total = in_terms[0]
    for source in range(1, groups):
        total = total + in_terms[source]
    sums_ref[x, y, 0:width] = total
    spans = ((0, 0, 56), (1, 56, 64))
    last = grid_gather(sums_ref, spans, ssem, rsem, used, x, y, grid_device)
    used += 30
    for route in last:
        next(route)
    for copy in extra_sends:
        copy.wait_send()
    for k in range(groups):
        dest = dests[k]

        @pl.when(dest != group)
        def _():
            term_copy(k, dest, group).wait_send()

    run_all(*last)
    assert used <= SEMS


SEMS = 160


def finish_kernel(scale, hidden_ref, sums_ref, *outs):
    hidden_out, self_out, neigh_out, hb_out, cs_out, cn_out, cb_out, loss_out, lines = outs
    width = self_out.shape[0]
    hid = hidden_ref.shape[1]
    groups, rows = sums_ref.shape[:2]
    per = rows - width
    hidden_out[...] = hidden_ref[...]
    for n in range(groups):
        out = neigh_out if n % 2 else self_out
        at = n // 2 * hid
        out[:, at : at + hid] = sums_ref[n, 0:width, :]
        lines[n * per : n * per + per, :] = sums_ref[n, width:rows, :]
    classes = cs_out.shape[0]
    cs_out[...] = lines[0:classes, :]
    cn_out[...] = lines[160 : 160 + classes, :]
    hb_out[...] = lines[320:321, :]
    cb_out[:, 0:128] = lines[321:322, :]
    cb_out[:, 128:classes] = lines[322:323, 0 : classes - 128]
    loss_out[...] = lines[323:324, :] * scale


def body(
    node_features,
    target_nodes,
    first_hop,
    live_counts,
    seed_links,
    seed_labels,
    self_weight,
    neigh_weight,
    hidden_bias,
    class_self,
    class_neigh,
    class_bias,
):
    node_rows = node_features.shape[1]
    batches, targets = target_nodes.shape
    fan_one = first_hop.shape[1]
    seeds, fan_two = seed_links.shape[1:]
    hid = hidden_bias.shape[0]
    width, hidden_all = self_weight.shape
    classes = class_bias.shape[0]
    offset = (lax.axis_index("group") * node_rows).astype(jnp.int32)[None]
    parts = gather_rows(node_features, target_nodes, first_hop, offset).reshape(4, 4, 384, 128)
    f32, vmem = jnp.float32, pl.BlockSpec(memory_space=pltpu.VMEM)
    smem = pl.BlockSpec(memory_space=pltpu.SMEM)
    shapes = [
        ((4, 4, 384, 128), f32),
        ((4, 6, 4, 48, 128), f32),
        ((4, 3, 96, 128), f32),
        ((384, hidden_all), jnp.bfloat16),
        ((4, 2, targets, hid), f32),
        ((4, targets, hid), f32),
        ((2, 6, targets // 4, hid), f32),
        ((2, 256, 8 * hid), f32),
        ((targets, 128), f32),
        ((targets, 128), f32),
        ((1, 256), f32),
        ((targets, 8 * hid), f32),
        ((seeds, 256), jnp.int32),
        ((targets, 128), f32),
        ((seeds, 256), f32),
        ((seeds, 256), f32),
        ((4, seeds, 256), f32),
        ((4, 2, targets, hid), f32),
        ((16, width, 128), f32),
        ((16, width, 128), f32),
        ((16, 24, 128), f32),
        ((16, 24, 128), f32),
    ]
    hidden_layer, sums = pl.pallas_call(
        functools.partial(exchange_kernel, fan_one, fan_two),
        out_shape=(
            jax.ShapeDtypeStruct((targets, hid), jnp.bfloat16),
            jax.ShapeDtypeStruct((4, 4, width + 24, 128), f32),
        ),
        in_specs=[pl.BlockSpec(memory_space=pl.ANY)] + [vmem] * 6 + [smem, vmem, smem],
        out_specs=(vmem, vmem),
        scratch_shapes=[pltpu.VMEM(shape, kind) for shape, kind in shapes]
        + [
            pltpu.SemaphoreType.DMA,
            pltpu.SemaphoreType.DMA((SEMS,)),
            pltpu.SemaphoreType.DMA((SEMS,)),
        ],
        compiler_params=pltpu.CompilerParams(
            collective_id=0, has_side_effects=True, vmem_limit_bytes=48 * 1024 * 1024
        ),
        name="exchange",
    )(
        parts,
        self_weight,
        neigh_weight,
        hidden_bias[None],
        class_self.T,
        class_neigh.T,
        class_bias[None],
        live_counts,
        jnp.transpose(seed_links, (2, 0, 1)),
        seed_labels,
    )
    outs = pl.pallas_call(
        functools.partial(finish_kernel, 1.0 / (batches * seeds)),
        out_shape=(
            jax.ShapeDtypeStruct((targets, hid), jnp.bfloat16),
            jax.ShapeDtypeStruct((width, hidden_all), f32),
            jax.ShapeDtypeStruct((width, hidden_all), f32),
            jax.ShapeDtypeStruct((1, hid), f32),
            jax.ShapeDtypeStruct((classes, hid), f32),
            jax.ShapeDtypeStruct((classes, hid), f32),
            jax.ShapeDtypeStruct((1, classes), f32),
            jax.ShapeDtypeStruct((1, 128), f32),
        ),
        in_specs=[vmem] * 2,
        out_specs=(vmem,) * 8,
        scratch_shapes=[pltpu.VMEM((16 * 24, 128), f32)],
        name="finish",
    )(hidden_layer, sums.reshape(16, width + 24, 128))
    return (
        outs[0],
        outs[1],
        outs[2],
        outs[3][0],
        outs[4].T,
        outs[5].T,
        outs[6][0],
        outs[7][0, 0],
    )


def solution(mesh):
    in_specs = (
        P("mp", "group"),
        P(),
        P(),
        P("group"),
        P("group", None, None),
        P("group", None),
        P("mp", None),
        P("mp", None),
        P("mp"),
        P("mp", None),
        P("mp", None),
        P(),
    )
    out_specs = (
        P("group", "mp"),
        P("mp", None),
        P("mp", None),
        P("mp"),
        P("mp", None),
        P("mp", None),
        P(),
        P(),
    )
    return jax.shard_map(body, mesh=mesh, in_specs=in_specs, out_specs=out_specs, check_vma=False)
```

```python
import functools
import jax
import jax.numpy as jnp
from jax import lax
from jax.experimental import pallas as pl
from jax.experimental.pallas import tpu as pltpu
from jax.sharding import PartitionSpec as P

UNROLL = 16
TOP = 3
BLOCK = 14
TURNS = 64


def gather_kernel(offset_ref, feat_hbm, targets_hbm, hops_hbm, out_ref, feat_ref, targets_ref, hops_ref, table, acc, ids, codes, counts, first_s, counts_s, extra_s, sems, load_sems):
    loads = [
        pltpu.make_async_copy(src, dst, load_sems.at[n])
        for n, (src, dst) in enumerate(((hops_hbm, hops_ref), (targets_hbm, targets_ref), (feat_hbm, feat_ref)))
    ]
    for load in loads:
        load.start()
    width, nodes = feat_ref.shape
    lists, rows = ids.shape[:2]
    fan, batches, targets = hops_ref.shape
    used = fan + 1
    half = rows * 128
    slots = 2 * half
    cols = targets // 128
    loads[0].wait()
    loads[1].wait()
    for n in range(cols):
        at, wide = pl.ds(n * batches, batches), slice(n * 128, n * 128 + 128)
        ids[0:fan, at] = hops_ref[:, :, wide] - offset_ref[0]
        ids[fan, at] = targets_ref[:, wide] - offset_ref[0]
    ids[used:lists] = jnp.full((lists - used, rows, 128), -1, jnp.int32)
    lane = lax.broadcasted_iota(jnp.int32, (BLOCK, rows, 128), 2)
    sub = lax.broadcasted_iota(jnp.int32, (BLOCK, rows, 128), 1)
    outer = lax.broadcasted_iota(jnp.int32, (BLOCK, rows, 128), 0)
    row_i = lax.broadcasted_iota(jnp.int32, (128, 128), 0)
    col_i = lax.broadcasted_iota(jnp.int32, (128, 128), 1)
    before = jnp.where(row_i < col_i, 1.0, 0.0).astype(jnp.bfloat16)
    ones = jnp.ones((128, 128), jnp.bfloat16)
    row_r = lax.broadcasted_iota(jnp.int32, (BLOCK * rows, BLOCK * rows), 0)
    col_r = lax.broadcasted_iota(jnp.int32, (BLOCK * rows, BLOCK * rows), 1)
    same = (row_r // rows) == (col_r // rows)
    above = jnp.where(same & (col_r < row_r), 1.0, 0.0).astype(jnp.bfloat16)
    shift = (nodes - 1).bit_length()
    steps = (half - 1).bit_length()
    flag = 1 << (shift + steps)

    def turn(i):
        at = pl.multiple_of(i * 128, 128)
        part = feat_ref[:, pl.ds(at, 128)].astype(jnp.float32)
        part = jnp.concatenate([part, jnp.zeros((128 - width, 128), jnp.float32)], axis=0)
        table[pl.ds(at, 128), :] = part.T

    def compact(q, carry):
        local = ids[pl.ds(q * BLOCK, BLOCK)]
        inside = (local >= 0) & (local < nodes)
        out_b = jnp.where(inside, 0.0, 1.0).reshape(BLOCK * rows, 128).astype(jnp.bfloat16)
        pref = jnp.dot(out_b, before, preferred_element_type=jnp.float32)
        total = jnp.dot(out_b, ones, preferred_element_type=jnp.float32)
        scan = jnp.dot(above, total.astype(jnp.bfloat16), preferred_element_type=jnp.float32)
        moved = (pref + scan).reshape(BLOCK, rows, 128).astype(jnp.int32)
        total = total.reshape(BLOCK, rows, 128)
        for b in range(BLOCK):
            missing = jnp.sum(total[b], axis=0, keepdims=True)
            counts[pl.ds(q * BLOCK + b, 1), :] = (half - missing).astype(jnp.int32)
        x = jnp.where(inside, flag | (moved << shift) | local, 0)
        for j in range(steps):
            d = 1 << j
            if j < 7:
                y = pltpu.roll(x, 128 - d, 2)
                y = jnp.where(lane < 128 - d, y, pltpu.roll(y, rows - 1, 1))
            else:
                y = pltpu.roll(x, rows - d // 128, 1)
            bit = 1 << (shift + j)
            x = jnp.where((y & bit) != 0, y, jnp.where((x & bit) != 0, 0, x))
        place = sub * 128 + lane + ((x >> shift) & (half - 1))
        row = place >> 7
        slot = (row % batches) * targets + (row // batches) * 128 + (place & 127)
        slot = slot + jnp.where(q * BLOCK + outer == fan, half, 0)
        code = jnp.where(x != 0, (slot << 15) | (x & (nodes - 1)), (slots << 15) | nodes)
        codes[pl.ds(q * BLOCK, BLOCK)] = code
        for n in range(TURNS):
            turn(q * TURNS + n)
        return carry

    loads[2].wait()
    lax.fori_loop(0, lists // BLOCK, compact, 0)
    copy_counts = pltpu.make_async_copy(counts, counts_s, sems.at[0])
    copy_counts.start()
    copies = []
    for j in range(used):
        for r in range(TOP):
            n = j * TOP + r
            copy = pltpu.make_async_copy(codes.at[j, r], first_s.at[pl.ds(n * 128, 128)], sems.at[n + 2])
            copy.start()
            copies.append(copy)

    def turn_rest(i, carry):
        turn(i)
        return carry

    lax.fori_loop(lists // BLOCK * TURNS, nodes // 128, turn_rest, 0)
    table[pl.ds(nodes, 8), :] = jnp.zeros((8, 128), jnp.float32)

    def clear(i, carry):
        acc[pl.ds(pl.multiple_of(i * 128, 128), 128), :] = jnp.zeros((128, 128), jnp.float32)
        return carry

    lax.fori_loop(0, slots // 128, clear, 0)
    acc[pl.ds(slots, 8), :] = jnp.zeros((8, 128), jnp.float32)
    copy_counts.wait()
    for copy in copies:
        copy.wait()

    def add_group(ref, base):
        code = [ref[base + u] for u in range(UNROLL)]
        at = [c >> 15 for c in code]
        rows = [table[pl.ds(c & 32767, 1), :] for c in code]
        olds = [acc[pl.ds(a, 1), :] for a in at]
        for a, old, row in zip(at, olds, rows):
            acc[pl.ds(a, 1), :] = old + row

    span = TOP * 128

    def step(state):
        j, k = state
        add_group(first_s, j * span + k)
        k = k + UNROLL
        done = k >= jnp.minimum(counts_s[j, 0], span)
        return jnp.where(done, j + 1, j), jnp.where(done, 0, k)

    lax.while_loop(lambda state: state[0] < used, step, (0, 0))

    def rest(j, carry):
        n = counts_s[j, 0]

        @pl.when(n > span)
        def _():
            def one(r, inner):
                copy = pltpu.make_async_copy(codes.at[j, r], extra_s, sems.at[1])
                copy.start()
                copy.wait()

                def group(i, inner2):
                    add_group(extra_s, i * UNROLL)
                    return inner2

                return lax.fori_loop(0, 128 // UNROLL, group, inner)

            lax.fori_loop(TOP, (n + 127) // 128, one, 0)

        return carry

    lax.fori_loop(0, used, rest, 0)

    lanes = lax.broadcasted_iota(jnp.int32, (32, 128), 1)

    def pack(i, carry):
        for s in range(2):
            for n in range(2):
                base = (1 - s) * half + i * 256 + n * 128
                a, b, c, d = [acc[pl.ds(pl.multiple_of(base + k * 32, 32), 32), :] for k in range(4)]
                b, c, d = pltpu.roll(b, 96, 1), pltpu.roll(c, 64, 1), pltpu.roll(d, 32, 1)
                row = s * 192 + n * 96
                out_ref[i, pl.ds(row, 32), :] = jnp.where(lanes < 96, a, b)
                out_ref[i, pl.ds(row + 32, 32), :] = jnp.where(lanes < 64, b, c)
                out_ref[i, pl.ds(row + 64, 32), :] = jnp.where(lanes < 32, c, d)
        return carry

    lax.fori_loop(0, half // 256, pack, 0)


def gather_rows(features, target_nodes, first_hop, offset):
    nodes = features.shape[1]
    batches, targets = target_nodes.shape
    rows = batches * targets // 128
    lists = 28
    hbm = pl.BlockSpec(memory_space=pltpu.HBM)
    hops = jnp.moveaxis(first_hop, 1, 0)
    return pl.pallas_call(
        gather_kernel,
        out_shape=jax.ShapeDtypeStruct((batches, 384, 128), jnp.float32),
        in_specs=[pl.BlockSpec(memory_space=pltpu.SMEM)] + [hbm] * 3,
        out_specs=pl.BlockSpec(memory_space=pltpu.VMEM),
        scratch_shapes=[
            pltpu.VMEM(features.shape, features.dtype),
            pltpu.VMEM(target_nodes.shape, jnp.int32),
            pltpu.VMEM(hops.shape, jnp.int32),
            pltpu.VMEM((nodes + 8, 128), jnp.float32),
            pltpu.VMEM((batches * 512 + 8, 128), jnp.float32),
            pltpu.VMEM((lists, rows, 128), jnp.int32),
            pltpu.VMEM((lists, rows, 128), jnp.int32),
            pltpu.VMEM((lists + 4, 128), jnp.int32),
            pltpu.SMEM((lists * TOP * 128,), jnp.int32),
            pltpu.SMEM((lists + 4, 128), jnp.int32),
            pltpu.SMEM((128,), jnp.int32),
            pltpu.SemaphoreType.DMA((lists * TOP + 2,)),
            pltpu.SemaphoreType.DMA((3,)),
        ],
        compiler_params=pltpu.CompilerParams(vmem_limit_bytes=48 * 1024 * 1024),
        name="gather_rows",
    )(offset, features, target_nodes, hops)


MESH = pl.DeviceIdType.MESH
HIGH = lax.Precision.HIGHEST


def run_all(*routes):
    active = list(routes)
    while active:
        for route in list(active):
            try:
                next(route)
            except StopIteration:
                active.remove(route)


def ring_sum(blk, inb, ssem, rsem, base, i, right, left):
    after, before, across = lax.rem(i + 1, 4), lax.rem(i + 3, 4), lax.rem(i + 2, 4)

    def copy(src, k, device):
        return pltpu.make_async_remote_copy(
            src_ref=src,
            dst_ref=inb(k),
            send_sem=ssem.at[base + k],
            recv_sem=rsem.at[base + k],
            device_id=device,
            device_id_type=MESH,
        )

    c0 = copy(blk(across, 0), 0, right)
    c1 = copy(blk(across, 1), 1, left)
    c2 = copy(blk(after, 1), 2, right)
    c3 = copy(blk(before, 0), 3, left)
    c4 = copy(blk(after, 0), 4, right)
    c5 = copy(blk(before, 1), 5, left)
    for c in (c0, c1, c2, c3):
        c.start()
    yield
    c0.wait_recv()
    blk(after, 0)[...] = blk(after, 0)[...] + inb(0)[...]
    c4.start()
    c1.wait_recv()
    blk(before, 1)[...] = blk(before, 1)[...] + inb(1)[...]
    c5.start()
    yield
    c3.wait_recv()
    c2.wait_recv()
    blk(i, 0)[...] = blk(i, 0)[...] + inb(3)[...]
    blk(i, 1)[...] = blk(i, 1)[...] + inb(2)[...]
    yield
    c4.wait_recv()
    blk(i, 0)[...] = blk(i, 0)[...] + inb(4)[...]
    c5.wait_recv()
    blk(i, 1)[...] = blk(i, 1)[...] + inb(5)[...]
    for c in (c0, c1, c2, c3, c4, c5):
        c.wait_send()


def grid_sum(buf, spans, in_wide, in_thin, ssem, rsem, base, x, y, xs, ys, device):
    def route(h, n, lo, half):
        def wide(d, p):
            at = pl.ds(lo + p * half, half)
            return buf.at[d, :, at] if h == 0 else buf.at[:, d, at]

        def thin(d):
            at = pl.ds(lo, 2 * half)
            return buf.at[x, d, at] if h == 0 else buf.at[d, y, at]

        first = (x,) + xs if h == 0 else (y,) + ys
        yield from ring_sum(wide, lambda k: in_wide.at[n, k], ssem, rsem, base + n * 9, *first)
        i = y if h == 0 else x
        copies = []
        for k, step in enumerate((1, 3, 2)):
            copies.append(
                pltpu.make_async_remote_copy(
                    src_ref=thin(lax.rem(i + step, 4)),
                    dst_ref=in_thin.at[n, k],
                    send_sem=ssem.at[base + n * 9 + 6 + k],
                    recv_sem=rsem.at[base + n * 9 + 6 + k],
                    device_id=device(0, step) if h == 0 else device(step, 0),
                    device_id_type=MESH,
                )
            )
            copies[-1].start()
        yield
        for k, copy in enumerate(copies):
            copy.wait_recv()
            thin(i)[...] = thin(i)[...] + in_thin[n, k]
        for copy in copies:
            copy.wait_send()

    return [route(*span) for span in spans]


def together(routes):
    active = list(routes)
    while active:
        for route in list(active):
            try:
                next(route)
            except StopIteration:
                active.remove(route)
        yield


def grid_gather(buf, spans, ssem, rsem, base, x, y, device):
    def route(n, h, lo, rows):
        at = pl.ds(lo, rows)

        def near(dx, dy):
            return device(dx, dy) if h == 0 else device(dy, dx)

        def place(far, close):
            return buf.at[far, close, at] if h == 0 else buf.at[close, far, at]

        far, close = (x, y) if h == 0 else (y, x)
        started = []

        def send(ref, k, target):
            copy = pltpu.make_async_remote_copy(
                src_ref=ref,
                dst_ref=ref,
                send_sem=ssem.at[base + n * 15 + k],
                recv_sem=rsem.at[base + n * 15 + k],
                device_id=target,
                device_id_type=MESH,
            )
            copy.start()
            started.append(copy)

        for d in (1, 3, 2):
            send(place(far, close), d - 1, near(0, d))
        for d in (1, 3, 2):
            send(place(far, close), 2 + d, near(d, 0))
        firsts = list(started)
        for n2, d in enumerate((1, 3, 2)):
            yield
            firsts[n2].wait_recv()
            source = lax.rem(close + 4 - d, 4)
            for e in (1, 3, 2):
                send(place(far, source), 3 * d + 2 + e, near(e, 0))
        yield
        for copy in started[3:]:
            copy.wait_recv()
        for copy in started:
            copy.wait_send()

    return [route(n, *span) for n, span in enumerate(spans)]


def unpack(ref, x, y, row):
    lane = lax.broadcasted_iota(jnp.int32, (32, 128), 1)
    p = [ref[x, y, pl.ds(row + 32 * n, 32), :] for n in range(3)]
    b = jnp.where(lane < 32, pltpu.roll(p[0], 32, 1), pltpu.roll(p[1], 32, 1))
    c = jnp.where(lane < 64, pltpu.roll(p[1], 64, 1), pltpu.roll(p[2], 64, 1))
    d = pltpu.roll(p[2], 96, 1)
    out = [jnp.where(lane < 96, v, 0.0) for v in (p[0], b, c, d)]
    return jnp.concatenate(out, axis=0)


def split(v):
    hi = v.astype(jnp.bfloat16)
    return hi, (v - hi.astype(jnp.float32)).astype(jnp.bfloat16)


def dot(a, b):
    return jnp.dot(a, b, preferred_element_type=jnp.float32)


def high_dot(a, b, dims=((1,), (0,))):
    return lax.dot_general(a, b, (dims, ((), ())), precision=HIGH, preferred_element_type=jnp.float32)


def exchange_kernel(
    fan_one,
    fan_two,
    parts_ref,
    ws_ref,
    wn_ref,
    hb_ref,
    cs_ref,
    cn_ref,
    cb_ref,
    live_ref,
    links_ref,
    labels_ref,
    hidden_ref,
    sums_ref,
    parts,
    in_wide,
    in_thin,
    weights,
    pre_parts,
    in_core,
    in_z,
    classes_all,
    self_all,
    neigh_all,
    cb_pad,
    acts,
    label_rows,
    link_pad,
    logit_own,
    logit_core,
    logit_z,
    piece,
    terms,
    in_terms,
    extras,
    in_extras,
    local_sem,
    ssem,
    rsem,
):
    group = lax.axis_index("group")
    m = lax.axis_index("mp")
    x, y = lax.div(group, 4), lax.rem(group, 4)
    z, core = lax.div(m, 2), lax.rem(m, 2)
    groups = in_terms.shape[0]

    def up(i, n):
        return lax.rem(i + n, 4)

    def grid_device(dx, dy):
        return (up(x, dx) * 4 + up(y, dy), m)

    def z_device(dz):
        return (group, up(z, dz) * 2 + core)

    xs = (grid_device(1, 0), grid_device(3, 0))
    ys = (grid_device(0, 1), grid_device(0, 3))
    zs = (z_device(1), z_device(3))
    opposite = z_device(2)
    sibling = (group, z * 2 + 1 - core)
    others = [(lax.rem(group + r, groups), m) for r in range(1, groups)]

    load = pltpu.make_async_copy(parts_ref, parts, local_sem)
    load.start()
    barrier = pltpu.get_barrier_semaphore()
    nears = others + list(zs) + [opposite, sibling]
    for near in nears:
        pl.semaphore_signal(barrier, inc=1, device_id=near, device_id_type=MESH)
    pl.semaphore_wait(barrier, len(nears))
    load.wait()

    def core_copy(src, dst, k):
        return pltpu.make_async_remote_copy(
            src_ref=src,
            dst_ref=dst,
            send_sem=ssem.at[k],
            recv_sem=rsem.at[k],
            device_id=sibling,
            device_id_type=MESH,
        )

    def spread(ref_of, base):
        started = []
        for k, (slot, near) in enumerate(((1, zs[0]), (3, zs[1]), (2, opposite))):
            started.append(
                pltpu.make_async_remote_copy(
                    src_ref=ref_of(0, 0),
                    dst_ref=ref_of(slot, 0),
                    send_sem=ssem.at[base + k],
                    recv_sem=rsem.at[base + k],
                    device_id=near,
                    device_id_type=MESH,
                )
            )
        started.append(core_copy(ref_of(0, 0), ref_of(0, 1), base + 3))
        for k in (0, 1, 3):
            started[k].start()
        yield (0, 0)
        started[2].start()
        yield (0, 0)
        started[3].wait_recv()
        yield (0, 1)
        for k, slot in enumerate((1, 3)):
            started[k].wait_recv()
            started.append(core_copy(ref_of(slot, 0), ref_of(slot, 1), base + 3 + slot))
            started[-1].start()
            yield (slot, 0)
        for k, slot in enumerate((1, 3)):
            started[4 + k].wait_recv()
            yield (slot, 1)
        started[2].wait_recv()
        started.append(core_copy(ref_of(2, 0), ref_of(2, 1), base + 5))
        started[-1].start()
        yield (2, 0)
        started[6].wait_recv()
        yield (2, 1)
        for copy in started:
            copy.wait_send()

    used = 0
    width = ws_ref.shape[0]
    targets, hid = hidden_ref.shape
    half_rows = targets // 2
    seeds = labels_ref.shape[1]
    classes = cs_ref.shape[0]

    def half_route(n, base):
        spans = ((0, 2 * n, n * 96, 48), (1, 2 * n + 1, 192 + n * 96, 48))
        yield from together(grid_sum(parts, spans, in_wide, in_thin, ssem, rsem, 0, x, y, xs, ys, grid_device))
        at = pl.ds(n * half_rows, half_rows)
        own_self = unpack(parts, x, y, n * 96)
        own_neigh = unpack(parts, x, y, 192 + n * 96) / fan_one
        self_all[at, :] = own_self
        neigh_all[at, :] = own_neigh
        neigh_hi, neigh_lo = split(own_neigh)
        left_side = jnp.concatenate([own_self.astype(jnp.bfloat16), neigh_hi, neigh_lo], axis=1)

        def block_of(zz, cc):
            cols = pl.multiple_of((zz * 2 + cc) * hid, hid)
            pre_parts[zz, cc, at] = dot(left_side, weights[:, pl.ds(cols, hid)])

        for zz in range(4):
            block_of(zz, 1 - core)
        copy = core_copy(pre_parts.at[:, 1 - core, at], in_core.at[:, at], base)
        copy.start()
        for zz in range(4):
            block_of(zz, core)
        yield
        copy.wait()
        for zz in range(4):
            pre_parts[zz, core, at] = pre_parts[zz, core, at] + in_core[zz, at]
        copies = []
        for k, (step, near) in enumerate(((1, zs[0]), (3, zs[1]), (2, opposite))):
            copies.append(
                pltpu.make_async_remote_copy(
                    src_ref=pre_parts.at[lax.rem(z + step, 4), core, at],
                    dst_ref=in_z.at[n, k],
                    send_sem=ssem.at[base + 1 + k],
                    recv_sem=rsem.at[base + 1 + k],
                    device_id=near,
                    device_id_type=MESH,
                )
            )
            copies[-1].start()
        yield
        for k, copy in enumerate(copies):
            copy.wait_recv()
            pre_parts[z, core, at] = pre_parts[z, core, at] + in_z[n, k]
        for copy in copies:
            copy.wait_send()

    used += 36
    owners = [half_route(n, used + 7 * n) for n in range(2)]
    used += 14
    next(owners[0])
    next(owners[1])

    sent = 160
    classes_all[:, sent:256, :] = jnp.zeros((2, 256 - sent, 8 * hid), jnp.float32)
    classes_all[:, 0:sent, 0:hid] = jnp.zeros((2, sent, hid), jnp.float32)
    classes_all[0, 0:classes, 0:hid] = cs_ref[...].astype(jnp.float32)
    classes_all[1, 0:classes, 0:hid] = cn_ref[...].astype(jnp.float32)
    class_spread = spread(
        lambda n, a: classes_all.at[:, pl.ds(0, sent), pl.ds((n * 2 + a) * hid, hid)], used
    )
    used += 7
    next(class_spread)
    next(class_spread)
    weights[...] = jnp.zeros_like(weights)
    weights[0:width, :] = ws_ref[...]
    weights[128 : 128 + width, :] = wn_ref[...]
    weights[256 : 256 + width, :] = wn_ref[...]
    cb_pad[...] = jnp.zeros_like(cb_pad)
    cb_pad[:, 0:classes] = cb_ref[...]
    extras[...] = jnp.zeros_like(extras)
    for s in range(seeds):
        label_rows[s : s + 1, :] = jnp.full((1, 256), labels_ref[0, s], jnp.int32)
    seed_cols = lax.broadcasted_iota(jnp.int32, (targets, seeds), 0)
    counted = jnp.zeros((targets, seeds), jnp.float32)
    for k in range(fan_two):
        counted = counted + jnp.where(seed_cols == links_ref[k], 1.0, 0.0)
    link_pad[...] = jnp.zeros_like(link_pad)
    link_pad[:, 0:seeds] = counted
    links_t = link_pad[...]
    links_f = links_t.T[0:seeds].astype(jnp.bfloat16)
    links_b = links_t.astype(jnp.bfloat16)
    target_rows = lax.broadcasted_iota(jnp.int32, (targets, 128), 0)

    run_all(*owners)

    pre = pre_parts[z, core] + hb_ref[...]
    piece[0, 0] = pre
    pre_spread = spread(lambda n, a: piece.at[n, a], used)
    used += 7
    next(pre_spread)
    alive = (target_rows < live_ref[0]) & (pre > 0.0)
    hidden = jnp.where(alive, pre, 0.0).astype(jnp.bfloat16)
    hidden_ref[...] = hidden
    active = hidden.astype(jnp.float32)
    seed_self = active[0:seeds]
    seed_neigh = dot(links_f, hidden) / fan_two
    rows_cols = ((1,), (1,))
    own_self = high_dot(seed_self, classes_all[0, :, 0:hid], rows_cols)
    logit_own[...] = own_self + high_dot(seed_neigh, classes_all[1, :, 0:hid], rows_cols)
    to_core = core_copy(logit_own, logit_core, used)
    used += 1
    to_core.start()
    to_core.wait()
    logit_z[z] = logit_own[...] + logit_core[...]

    def z_sends(ref, base):
        copies = []
        for k, near in enumerate(zs + (opposite,)):
            copies.append(
                pltpu.make_async_remote_copy(
                    src_ref=ref,
                    dst_ref=ref,
                    send_sem=ssem.at[base + k],
                    recv_sem=rsem.at[base + k],
                    device_id=near,
                    device_id_type=MESH,
                )
            )
            copies[-1].start()
        return copies

    sends = z_sends(logit_z.at[z], used)
    used += 3
    next(pre_spread)
    run_all(class_spread)
    self_t = self_all[...].T[0:width].astype(jnp.bfloat16)
    neigh_t_hi, neigh_t_lo = split(neigh_all[...].T[0:width])
    rows_three = jnp.concatenate([self_t, neigh_t_hi, neigh_t_lo], axis=0)
    for c in sends:
        c.wait()
    logits = (logit_z[0] + logit_z[1]) + (logit_z[2] + logit_z[3]) + cb_pad[...]
    lanes = lax.broadcasted_iota(jnp.int32, logits.shape, 1)
    logits = jnp.where(lanes < classes, logits, -1e30)
    top = jnp.max(logits, axis=1, keepdims=True)
    log_total = jnp.log(jnp.sum(jnp.exp(logits - top), axis=1, keepdims=True)) + top
    onehot = jnp.where(lanes == label_rows[...], 1.0, 0.0)
    losses = log_total - jnp.sum(onehot * logits, axis=1, keepdims=True)
    dlogit = jnp.exp(logits - log_total) - onehot
    dlogit_two = jnp.concatenate(split(dlogit), axis=0)

    def back(kind):
        both = dot(dlogit_two, classes_all[kind].astype(jnp.bfloat16))
        return both[0:seeds] + both[seeds : 2 * seeds]

    back_neigh = jnp.concatenate(
        [back(1) / fan_two, jnp.zeros((128 - seeds, 8 * hid), jnp.float32)], axis=0
    )
    links_two = jnp.concatenate([links_b, links_b], axis=1)
    acts[...] = dot(links_two, jnp.concatenate(split(back_neigh), axis=0))
    acts[0:seeds, :] = acts[0:seeds, :] + back(0)
    live_rows = target_rows < live_ref[0]

    def grad_of(n, across):
        at = (n * 2 + across) * hid
        return jnp.where(live_rows & (piece[n, across] > 0.0), acts[:, at : at + hid], 0.0)

    term_base = used
    used += groups

    def term_copy(k, dest, k_recv):
        return pltpu.make_async_remote_copy(
            src_ref=terms.at[k],
            dst_ref=in_terms.at[group],
            send_sem=ssem.at[term_base + k],
            recv_sem=rsem.at[term_base + k_recv],
            device_id=(dest, m),
            device_id_type=MESH,
        )

    dests = {}

    hidden_line = []

    def block_terms(step, n, across):
        zz = lax.rem(z + 4 - n, 4)
        cc = 1 - core if across else core
        grad_pre = grad_of(n, across)
        if step == 0:
            hidden_line.append(jnp.sum(grad_pre, axis=0, keepdims=True))
        term = dot(rows_three, jnp.concatenate(split(grad_pre), axis=1))
        terms[2 * step] = term[0:width, 0:hid] + term[0:width, hid : 2 * hid]
        neigh_term = term[width : 2 * width, 0:hid] + term[width : 2 * width, hid : 2 * hid]
        terms[2 * step + 1] = neigh_term + term[2 * width : 3 * width, 0:hid]
        for s in range(2):
            k = 2 * step + s
            dests[k] = dest = zz * 4 + cc * 2 + s

            @pl.when(dest != group)
            def _():
                term_copy(k, dest, group).start()

            @pl.when(dest == group)
            def _():
                in_terms[group] = terms[k]

    block_terms(0, 0, 0)
    block_terms(1, *next(pre_spread))

    dlogit_t = dlogit.T[0:sent]
    class_grads = jnp.concatenate(
        [high_dot(dlogit_t, seed_self), high_dot(dlogit_t, seed_neigh)], axis=0
    )
    per = extras.shape[1]
    for n in range(0, 320, 8):
        extras[n // per, n % per : n % per + 8] = class_grads[n : n + 8]
    row_sum = jnp.sum(dlogit, axis=0, keepdims=True)
    lines = (
        hidden_line[0],
        row_sum[:, 0:128],
        row_sum[:, 128:256],
        jnp.broadcast_to(jnp.sum(losses, axis=0, keepdims=True), (1, 128)),
    )
    for n, line in enumerate(lines):
        extras[320 // per, 320 % per + n : 320 % per + n + 1] = line
    extra_sends = []
    for r in range(1, groups):
        copy = pltpu.make_async_remote_copy(
            src_ref=extras.at[lax.rem(group + r, groups)],
            dst_ref=in_extras.at[r],
            send_sem=ssem.at[used + r - 1],
            recv_sem=rsem.at[used + r - 1],
            device_id=others[r - 1],
            device_id_type=MESH,
        )
        copy.start()
        extra_sends.append(copy)
    used += groups - 1

    for step in range(2, groups // 2):
        block_terms(step, *next(pre_spread))
    run_all(pre_spread)

    for copy in extra_sends:
        copy.wait_recv()
    total = extras[group]
    for r in range(1, groups):
        total = total + in_extras[r]
    sums_ref[x, y, width : width + per] = total
    for source in range(groups):

        @pl.when(source != group)
        def _():
            pltpu.make_async_remote_copy(
                src_ref=terms.at[0],
                dst_ref=in_terms.at[source],
                send_sem=ssem.at[term_base],
                recv_sem=rsem.at[term_base + source],
                device_id=(source, m),
                device_id_type=MESH,
            ).wait_recv()

    total = in_terms[0]
    for source in range(1, groups):
        total = total + in_terms[source]
    sums_ref[x, y, 0:width] = total
    spans = ((0, 0, 56), (1, 56, 64))
    last = grid_gather(sums_ref, spans, ssem, rsem, used, x, y, grid_device)
    used += 30
    for route in last:
        next(route)
    for copy in extra_sends:
        copy.wait_send()
    for k in range(groups):
        dest = dests[k]

        @pl.when(dest != group)
        def _():
            term_copy(k, dest, group).wait_send()

    run_all(*last)
    assert used <= SEMS


SEMS = 160


def finish_kernel(scale, hidden_ref, sums_ref, *outs):
    hidden_out, self_out, neigh_out, hb_out, cs_out, cn_out, cb_out, loss_out, lines = outs
    width = self_out.shape[0]
    hid = hidden_ref.shape[1]
    groups, rows = sums_ref.shape[:2]
    per = rows - width
    hidden_out[...] = hidden_ref[...]
    for n in range(groups):
        out = neigh_out if n % 2 else self_out
        at = n // 2 * hid
        out[:, at : at + hid] = sums_ref[n, 0:width, :]
        lines[n * per : n * per + per, :] = sums_ref[n, width:rows, :]
    classes = cs_out.shape[0]
    cs_out[...] = lines[0:classes, :]
    cn_out[...] = lines[160 : 160 + classes, :]
    hb_out[...] = lines[320:321, :]
    cb_out[:, 0:128] = lines[321:322, :]
    cb_out[:, 128:classes] = lines[322:323, 0 : classes - 128]
    loss_out[...] = lines[323:324, :] * scale


def body(
    node_features,
    target_nodes,
    first_hop,
    live_counts,
    seed_links,
    seed_labels,
    self_weight,
    neigh_weight,
    hidden_bias,
    class_self,
    class_neigh,
    class_bias,
):
    node_rows = node_features.shape[1]
    batches, targets = target_nodes.shape
    fan_one = first_hop.shape[1]
    seeds, fan_two = seed_links.shape[1:]
    hid = hidden_bias.shape[0]
    width, hidden_all = self_weight.shape
    classes = class_bias.shape[0]
    offset = (lax.axis_index("group") * node_rows).astype(jnp.int32)[None]
    parts = gather_rows(node_features, target_nodes, first_hop, offset).reshape(4, 4, 384, 128)
    f32, vmem = jnp.float32, pl.BlockSpec(memory_space=pltpu.VMEM)
    smem = pl.BlockSpec(memory_space=pltpu.SMEM)
    shapes = [
        ((4, 4, 384, 128), f32),
        ((4, 6, 4, 48, 128), f32),
        ((4, 3, 96, 128), f32),
        ((384, hidden_all), jnp.bfloat16),
        ((4, 2, targets, hid), f32),
        ((4, targets, hid), f32),
        ((2, 3, targets // 2, hid), f32),
        ((2, 256, 8 * hid), f32),
        ((targets, 128), f32),
        ((targets, 128), f32),
        ((1, 256), f32),
        ((targets, 8 * hid), f32),
        ((seeds, 256), jnp.int32),
        ((targets, 128), f32),
        ((seeds, 256), f32),
        ((seeds, 256), f32),
        ((4, seeds, 256), f32),
        ((4, 2, targets, hid), f32),
        ((16, width, 128), f32),
        ((16, width, 128), f32),
        ((16, 24, 128), f32),
        ((16, 24, 128), f32),
    ]
    hidden_layer, sums = pl.pallas_call(
        functools.partial(exchange_kernel, fan_one, fan_two),
        out_shape=(
            jax.ShapeDtypeStruct((targets, hid), jnp.bfloat16),
            jax.ShapeDtypeStruct((4, 4, width + 24, 128), f32),
        ),
        in_specs=[pl.BlockSpec(memory_space=pl.ANY)] + [vmem] * 6 + [smem, vmem, smem],
        out_specs=(vmem, vmem),
        scratch_shapes=[pltpu.VMEM(shape, kind) for shape, kind in shapes]
        + [
            pltpu.SemaphoreType.DMA,
            pltpu.SemaphoreType.DMA((SEMS,)),
            pltpu.SemaphoreType.DMA((SEMS,)),
        ],
        compiler_params=pltpu.CompilerParams(
            collective_id=0, has_side_effects=True, vmem_limit_bytes=48 * 1024 * 1024
        ),
        name="exchange",
    )(
        parts,
        self_weight,
        neigh_weight,
        hidden_bias[None],
        class_self.T,
        class_neigh.T,
        class_bias[None],
        live_counts,
        jnp.transpose(seed_links, (2, 0, 1)),
        seed_labels,
    )
    outs = pl.pallas_call(
        functools.partial(finish_kernel, 1.0 / (batches * seeds)),
        out_shape=(
            jax.ShapeDtypeStruct((targets, hid), jnp.bfloat16),
            jax.ShapeDtypeStruct((width, hidden_all), f32),
            jax.ShapeDtypeStruct((width, hidden_all), f32),
            jax.ShapeDtypeStruct((1, hid), f32),
            jax.ShapeDtypeStruct((classes, hid), f32),
            jax.ShapeDtypeStruct((classes, hid), f32),
            jax.ShapeDtypeStruct((1, classes), f32),
            jax.ShapeDtypeStruct((1, 128), f32),
        ),
        in_specs=[vmem] * 2,
        out_specs=(vmem,) * 8,
        scratch_shapes=[pltpu.VMEM((16 * 24, 128), f32)],
        compiler_params=pltpu.CompilerParams(vmem_limit_bytes=8 * 1024 * 1024),
        name="finish",
    )(hidden_layer, sums.reshape(16, width + 24, 128))
    return (
        outs[0],
        outs[1],
        outs[2],
        outs[3][0],
        outs[4].T,
        outs[5].T,
        outs[6][0],
        outs[7][0, 0],
    )


def solution(mesh):
    in_specs = (
        P("mp", "group"),
        P(),
        P(),
        P("group"),
        P("group", None, None),
        P("group", None),
        P("mp", None),
        P("mp", None),
        P("mp"),
        P("mp", None),
        P("mp", None),
        P(),
    )
    out_specs = (
        P("group", "mp"),
        P("mp", None),
        P("mp", None),
        P("mp"),
        P("mp", None),
        P("mp", None),
        P(),
        P(),
    )
    return jax.shard_map(body, mesh=mesh, in_specs=in_specs, out_specs=out_specs, check_vma=False)
```

```python
import functools
import jax
import jax.numpy as jnp
from jax import lax
from jax.experimental import pallas as pl
from jax.experimental.pallas import tpu as pltpu
from jax.sharding import PartitionSpec as P

UNROLL = 16
TOP = 3
BLOCK = 14
TURNS = 64


def gather_kernel(offset_ref, feat_hbm, targets_hbm, hops_hbm, out_ref, feat_ref, targets_ref, hops_ref, table, acc, ids, codes, counts, first_s, counts_s, extra_s, sems, load_sems):
    loads = [
        pltpu.make_async_copy(src, dst, load_sems.at[n])
        for n, (src, dst) in enumerate(((hops_hbm, hops_ref), (targets_hbm, targets_ref), (feat_hbm, feat_ref)))
    ]
    for load in loads:
        load.start()
    width, nodes = feat_ref.shape
    lists, rows = ids.shape[:2]
    fan, batches, targets = hops_ref.shape
    used = fan + 1
    half = rows * 128
    slots = 2 * half
    cols = targets // 128
    loads[0].wait()
    loads[1].wait()
    for n in range(cols):
        at, wide = pl.ds(n * batches, batches), slice(n * 128, n * 128 + 128)
        ids[0:fan, at] = hops_ref[:, :, wide] - offset_ref[0]
        ids[fan, at] = targets_ref[:, wide] - offset_ref[0]
    ids[used:lists] = jnp.full((lists - used, rows, 128), -1, jnp.int32)
    lane = lax.broadcasted_iota(jnp.int32, (BLOCK, rows, 128), 2)
    sub = lax.broadcasted_iota(jnp.int32, (BLOCK, rows, 128), 1)
    outer = lax.broadcasted_iota(jnp.int32, (BLOCK, rows, 128), 0)
    row_i = lax.broadcasted_iota(jnp.int32, (128, 128), 0)
    col_i = lax.broadcasted_iota(jnp.int32, (128, 128), 1)
    before = jnp.where(row_i < col_i, 1.0, 0.0).astype(jnp.bfloat16)
    ones = jnp.ones((128, 128), jnp.bfloat16)
    row_r = lax.broadcasted_iota(jnp.int32, (BLOCK * rows, BLOCK * rows), 0)
    col_r = lax.broadcasted_iota(jnp.int32, (BLOCK * rows, BLOCK * rows), 1)
    same = (row_r // rows) == (col_r // rows)
    above = jnp.where(same & (col_r < row_r), 1.0, 0.0).astype(jnp.bfloat16)
    shift = (nodes - 1).bit_length()
    steps = (half - 1).bit_length()
    flag = 1 << (shift + steps)

    def turn(i):
        at = pl.multiple_of(i * 128, 128)
        part = feat_ref[:, pl.ds(at, 128)].astype(jnp.float32)
        part = jnp.concatenate([part, jnp.zeros((128 - width, 128), jnp.float32)], axis=0)
        table[pl.ds(at, 128), :] = part.T

    def compact(q, carry):
        local = ids[pl.ds(q * BLOCK, BLOCK)]
        inside = (local >= 0) & (local < nodes)
        out_b = jnp.where(inside, 0.0, 1.0).reshape(BLOCK * rows, 128).astype(jnp.bfloat16)
        pref = jnp.dot(out_b, before, preferred_element_type=jnp.float32)
        total = jnp.dot(out_b, ones, preferred_element_type=jnp.float32)
        scan = jnp.dot(above, total.astype(jnp.bfloat16), preferred_element_type=jnp.float32)
        moved = (pref + scan).reshape(BLOCK, rows, 128).astype(jnp.int32)
        total = total.reshape(BLOCK, rows, 128)
        for b in range(BLOCK):
            missing = jnp.sum(total[b], axis=0, keepdims=True)
            counts[pl.ds(q * BLOCK + b, 1), :] = (half - missing).astype(jnp.int32)
        x = jnp.where(inside, flag | (moved << shift) | local, 0)
        for j in range(steps):
            d = 1 << j
            if j < 7:
                y = pltpu.roll(x, 128 - d, 2)
                y = jnp.where(lane < 128 - d, y, pltpu.roll(y, rows - 1, 1))
            else:
                y = pltpu.roll(x, rows - d // 128, 1)
            bit = 1 << (shift + j)
            x = jnp.where((y & bit) != 0, y, jnp.where((x & bit) != 0, 0, x))
        place = sub * 128 + lane + ((x >> shift) & (half - 1))
        row = place >> 7
        slot = (row % batches) * targets + (row // batches) * 128 + (place & 127)
        slot = slot + jnp.where(q * BLOCK + outer == fan, half, 0)
        code = jnp.where(x != 0, (slot << 15) | (x & (nodes - 1)), (slots << 15) | nodes)
        codes[pl.ds(q * BLOCK, BLOCK)] = code
        for n in range(TURNS):
            turn(q * TURNS + n)
        return carry

    loads[2].wait()
    lax.fori_loop(0, lists // BLOCK, compact, 0)
    copy_counts = pltpu.make_async_copy(counts, counts_s, sems.at[0])
    copy_counts.start()
    copies = []
    for j in range(used):
        for r in range(TOP):
            n = j * TOP + r
            copy = pltpu.make_async_copy(codes.at[j, r], first_s.at[pl.ds(n * 128, 128)], sems.at[n + 2])
            copy.start()
            copies.append(copy)

    def turn_rest(i, carry):
        turn(i)
        return carry

    lax.fori_loop(lists // BLOCK * TURNS, nodes // 128, turn_rest, 0)
    table[pl.ds(nodes, 8), :] = jnp.zeros((8, 128), jnp.float32)

    def clear(i, carry):
        acc[pl.ds(pl.multiple_of(i * 128, 128), 128), :] = jnp.zeros((128, 128), jnp.float32)
        return carry

    lax.fori_loop(0, slots // 128, clear, 0)
    acc[pl.ds(slots, 8), :] = jnp.zeros((8, 128), jnp.float32)
    copy_counts.wait()
    for copy in copies:
        copy.wait()

    def add_group(ref, base):
        code = [ref[base + u] for u in range(UNROLL)]
        at = [c >> 15 for c in code]
        rows = [table[pl.ds(c & 32767, 1), :] for c in code]
        olds = [acc[pl.ds(a, 1), :] for a in at]
        for a, old, row in zip(at, olds, rows):
            acc[pl.ds(a, 1), :] = old + row

    span = TOP * 128

    def step(state):
        j, k = state
        add_group(first_s, j * span + k)
        k = k + UNROLL
        done = k >= jnp.minimum(counts_s[j, 0], span)
        return jnp.where(done, j + 1, j), jnp.where(done, 0, k)

    lax.while_loop(lambda state: state[0] < used, step, (0, 0))

    def rest(j, carry):
        n = counts_s[j, 0]

        @pl.when(n > span)
        def _():
            def one(r, inner):
                copy = pltpu.make_async_copy(codes.at[j, r], extra_s, sems.at[1])
                copy.start()
                copy.wait()

                def group(i, inner2):
                    add_group(extra_s, i * UNROLL)
                    return inner2

                return lax.fori_loop(0, 128 // UNROLL, group, inner)

            lax.fori_loop(TOP, (n + 127) // 128, one, 0)

        return carry

    lax.fori_loop(0, used, rest, 0)

    lanes = lax.broadcasted_iota(jnp.int32, (32, 128), 1)

    def pack(i, carry):
        for s in range(2):
            for n in range(2):
                base = (1 - s) * half + i * 256 + n * 128
                a, b, c, d = [acc[pl.ds(pl.multiple_of(base + k * 32, 32), 32), :] for k in range(4)]
                b, c, d = pltpu.roll(b, 96, 1), pltpu.roll(c, 64, 1), pltpu.roll(d, 32, 1)
                row = s * 192 + n * 96
                out_ref[i, pl.ds(row, 32), :] = jnp.where(lanes < 96, a, b)
                out_ref[i, pl.ds(row + 32, 32), :] = jnp.where(lanes < 64, b, c)
                out_ref[i, pl.ds(row + 64, 32), :] = jnp.where(lanes < 32, c, d)
        return carry

    lax.fori_loop(0, half // 256, pack, 0)


def gather_rows(features, target_nodes, first_hop, offset):
    nodes = features.shape[1]
    batches, targets = target_nodes.shape
    rows = batches * targets // 128
    lists = 28
    hbm = pl.BlockSpec(memory_space=pltpu.HBM)
    hops = jnp.moveaxis(first_hop, 1, 0)
    return pl.pallas_call(
        gather_kernel,
        out_shape=jax.ShapeDtypeStruct((batches, 384, 128), jnp.float32),
        in_specs=[pl.BlockSpec(memory_space=pltpu.SMEM)] + [hbm] * 3,
        out_specs=pl.BlockSpec(memory_space=pltpu.VMEM),
        scratch_shapes=[
            pltpu.VMEM(features.shape, features.dtype),
            pltpu.VMEM(target_nodes.shape, jnp.int32),
            pltpu.VMEM(hops.shape, jnp.int32),
            pltpu.VMEM((nodes + 8, 128), jnp.float32),
            pltpu.VMEM((batches * 512 + 8, 128), jnp.float32),
            pltpu.VMEM((lists, rows, 128), jnp.int32),
            pltpu.VMEM((lists, rows, 128), jnp.int32),
            pltpu.VMEM((lists + 4, 128), jnp.int32),
            pltpu.SMEM((lists * TOP * 128,), jnp.int32),
            pltpu.SMEM((lists + 4, 128), jnp.int32),
            pltpu.SMEM((128,), jnp.int32),
            pltpu.SemaphoreType.DMA((lists * TOP + 2,)),
            pltpu.SemaphoreType.DMA((3,)),
        ],
        compiler_params=pltpu.CompilerParams(vmem_limit_bytes=48 * 1024 * 1024),
        name="gather_rows",
    )(offset, features, target_nodes, hops)


MESH = pl.DeviceIdType.MESH


def run_all(*routes):
    active = list(routes)
    while active:
        for route in list(active):
            try:
                next(route)
            except StopIteration:
                active.remove(route)


def ring_sum(blk, inb, ssem, rsem, base, i, right, left):
    after, before, across = lax.rem(i + 1, 4), lax.rem(i + 3, 4), lax.rem(i + 2, 4)

    def copy(src, k, device):
        return pltpu.make_async_remote_copy(
            src_ref=src,
            dst_ref=inb(k),
            send_sem=ssem.at[base + k],
            recv_sem=rsem.at[base + k],
            device_id=device,
            device_id_type=MESH,
        )

    c0 = copy(blk(across, 0), 0, right)
    c1 = copy(blk(across, 1), 1, left)
    c2 = copy(blk(after, 1), 2, right)
    c3 = copy(blk(before, 0), 3, left)
    c4 = copy(blk(after, 0), 4, right)
    c5 = copy(blk(before, 1), 5, left)
    for c in (c0, c1, c2, c3):
        c.start()
    yield
    c0.wait_recv()
    blk(after, 0)[...] = blk(after, 0)[...] + inb(0)[...]
    c4.start()
    c1.wait_recv()
    blk(before, 1)[...] = blk(before, 1)[...] + inb(1)[...]
    c5.start()
    yield
    c3.wait_recv()
    c2.wait_recv()
    blk(i, 0)[...] = blk(i, 0)[...] + inb(3)[...]
    blk(i, 1)[...] = blk(i, 1)[...] + inb(2)[...]
    yield
    c4.wait_recv()
    blk(i, 0)[...] = blk(i, 0)[...] + inb(4)[...]
    c5.wait_recv()
    blk(i, 1)[...] = blk(i, 1)[...] + inb(5)[...]
    for c in (c0, c1, c2, c3, c4, c5):
        c.wait_send()


def grid_sum(buf, spans, in_wide, in_thin, ssem, rsem, base, x, y, xs, ys, device):
    def route(h, n, lo, half):
        def wide(d, p):
            at = pl.ds(lo + p * half, half)
            return buf.at[d, :, at] if h == 0 else buf.at[:, d, at]

        def thin(d):
            at = pl.ds(lo, 2 * half)
            return buf.at[x, d, at] if h == 0 else buf.at[d, y, at]

        first = (x,) + xs if h == 0 else (y,) + ys
        yield from ring_sum(wide, lambda k: in_wide.at[n, k], ssem, rsem, base + n * 9, *first)
        i = y if h == 0 else x
        copies = []
        for k, step in enumerate((1, 3, 2)):
            copies.append(
                pltpu.make_async_remote_copy(
                    src_ref=thin(lax.rem(i + step, 4)),
                    dst_ref=in_thin.at[n, k],
                    send_sem=ssem.at[base + n * 9 + 6 + k],
                    recv_sem=rsem.at[base + n * 9 + 6 + k],
                    device_id=device(0, step) if h == 0 else device(step, 0),
                    device_id_type=MESH,
                )
            )
            copies[-1].start()
        yield
        for k, copy in enumerate(copies):
            copy.wait_recv()
            thin(i)[...] = thin(i)[...] + in_thin[n, k]
        for copy in copies:
            copy.wait_send()

    return [route(*span) for span in spans]


def together(routes):
    active = list(routes)
    while active:
        for route in list(active):
            try:
                next(route)
            except StopIteration:
                active.remove(route)
        yield


def grid_gather(buf, spans, ssem, rsem, base, x, y, device):
    def route(n, h, lo, rows):
        at = pl.ds(lo, rows)

        def near(dx, dy):
            return device(dx, dy) if h == 0 else device(dy, dx)

        def place(far, close):
            return buf.at[far, close, at] if h == 0 else buf.at[close, far, at]

        far, close = (x, y) if h == 0 else (y, x)
        started = []

        def send(ref, k, target):
            copy = pltpu.make_async_remote_copy(
                src_ref=ref,
                dst_ref=ref,
                send_sem=ssem.at[base + n * 15 + k],
                recv_sem=rsem.at[base + n * 15 + k],
                device_id=target,
                device_id_type=MESH,
            )
            copy.start()
            started.append(copy)

        for d in (1, 3, 2):
            send(place(far, close), d - 1, near(0, d))
        for d in (1, 3, 2):
            send(place(far, close), 2 + d, near(d, 0))
        firsts = list(started)
        for n2, d in enumerate((1, 3, 2)):
            yield
            firsts[n2].wait_recv()
            source = lax.rem(close + 4 - d, 4)
            for e in (1, 3, 2):
                send(place(far, source), 3 * d + 2 + e, near(e, 0))
        yield
        for copy in started[3:]:
            copy.wait_recv()
        for copy in started:
            copy.wait_send()

    return [route(n, *span) for n, span in enumerate(spans)]


def unpack(ref, x, y, row):
    lane = lax.broadcasted_iota(jnp.int32, (32, 128), 1)
    p = [ref[x, y, pl.ds(row + 32 * n, 32), :] for n in range(3)]
    b = jnp.where(lane < 32, pltpu.roll(p[0], 32, 1), pltpu.roll(p[1], 32, 1))
    c = jnp.where(lane < 64, pltpu.roll(p[1], 64, 1), pltpu.roll(p[2], 64, 1))
    d = pltpu.roll(p[2], 96, 1)
    out = [jnp.where(lane < 96, v, 0.0) for v in (p[0], b, c, d)]
    return jnp.concatenate(out, axis=0)


def split(v):
    hi = v.astype(jnp.bfloat16)
    return hi, (v - hi.astype(jnp.float32)).astype(jnp.bfloat16)


def dot(a, b):
    return jnp.dot(a, b, preferred_element_type=jnp.float32)


def exchange_kernel(
    fan_one,
    fan_two,
    parts_ref,
    ws_ref,
    wn_ref,
    hb_ref,
    cs_ref,
    cn_ref,
    cb_ref,
    live_ref,
    links_ref,
    labels_ref,
    hidden_ref,
    sums_ref,
    parts,
    in_wide,
    in_thin,
    weights,
    pre_parts,
    in_core,
    in_z,
    classes_all,
    class_low,
    class_three,
    self_all,
    neigh_all,
    cb_pad,
    acts,
    label_rows,
    link_pad,
    logit_own,
    logit_core,
    logit_z,
    piece,
    terms,
    in_terms,
    extras,
    in_extras,
    local_sem,
    ssem,
    rsem,
):
    group = lax.axis_index("group")
    m = lax.axis_index("mp")
    x, y = lax.div(group, 4), lax.rem(group, 4)
    z, core = lax.div(m, 2), lax.rem(m, 2)
    groups = in_terms.shape[0]

    def up(i, n):
        return lax.rem(i + n, 4)

    def grid_device(dx, dy):
        return (up(x, dx) * 4 + up(y, dy), m)

    def z_device(dz):
        return (group, up(z, dz) * 2 + core)

    xs = (grid_device(1, 0), grid_device(3, 0))
    ys = (grid_device(0, 1), grid_device(0, 3))
    zs = (z_device(1), z_device(3))
    opposite = z_device(2)
    sibling = (group, z * 2 + 1 - core)
    others = [(lax.rem(group + r, groups), m) for r in range(1, groups)]

    load = pltpu.make_async_copy(parts_ref, parts, local_sem)
    load.start()
    barrier = pltpu.get_barrier_semaphore()
    axis_far = [grid_device(2, 0), grid_device(0, 2)]
    nears = list(xs + ys + zs) + axis_far + [opposite, sibling]
    for near in nears:
        pl.semaphore_signal(barrier, inc=1, device_id=near, device_id_type=MESH)
    pl.semaphore_wait(barrier, len(nears))
    load.wait()

    def core_copy(src, dst, k):
        return pltpu.make_async_remote_copy(
            src_ref=src,
            dst_ref=dst,
            send_sem=ssem.at[k],
            recv_sem=rsem.at[k],
            device_id=sibling,
            device_id_type=MESH,
        )

    def spread(ref_of, base):
        started = []
        for k, (slot, near) in enumerate(((1, zs[0]), (3, zs[1]), (2, opposite))):
            started.append(
                pltpu.make_async_remote_copy(
                    src_ref=ref_of(0, 0),
                    dst_ref=ref_of(slot, 0),
                    send_sem=ssem.at[base + k],
                    recv_sem=rsem.at[base + k],
                    device_id=near,
                    device_id_type=MESH,
                )
            )
        started.append(core_copy(ref_of(0, 0), ref_of(0, 1), base + 3))
        for k in (0, 1, 3):
            started[k].start()
        yield (0, 0)
        started[2].start()
        yield (0, 0)
        started[3].wait_recv()
        yield (0, 1)
        for k, slot in enumerate((1, 3)):
            started[k].wait_recv()
            started.append(core_copy(ref_of(slot, 0), ref_of(slot, 1), base + 3 + slot))
            started[-1].start()
            yield (slot, 0)
        for k, slot in enumerate((1, 3)):
            started[4 + k].wait_recv()
            yield (slot, 1)
        started[2].wait_recv()
        started.append(core_copy(ref_of(2, 0), ref_of(2, 1), base + 5))
        started[-1].start()
        yield (2, 0)
        started[6].wait_recv()
        yield (2, 1)
        for copy in started:
            copy.wait_send()

    used = 0
    width = ws_ref.shape[0]
    targets, hid = hidden_ref.shape
    half_rows = targets // 2
    seeds = labels_ref.shape[1]
    classes = cs_ref.shape[0]

    def half_route(n, base):
        spans = ((0, 2 * n, n * 96, 48), (1, 2 * n + 1, 192 + n * 96, 48))
        yield from together(grid_sum(parts, spans, in_wide, in_thin, ssem, rsem, 0, x, y, xs, ys, grid_device))
        at = pl.ds(n * half_rows, half_rows)
        own_self = unpack(parts, x, y, n * 96)
        own_neigh = unpack(parts, x, y, 192 + n * 96) / fan_one
        self_all[at, :] = own_self
        neigh_all[at, :] = own_neigh
        neigh_hi, neigh_lo = split(own_neigh)
        left_side = jnp.concatenate([own_self.astype(jnp.bfloat16), neigh_hi, neigh_lo], axis=1)

        def block_of(zz, cc):
            cols = pl.multiple_of((zz * 2 + cc) * hid, hid)
            pre_parts[zz, cc, at] = dot(left_side, weights[:, pl.ds(cols, hid)])

        for zz in range(4):
            block_of(zz, 1 - core)
        copy = core_copy(pre_parts.at[:, 1 - core, at], in_core.at[:, at], base)
        copy.start()
        for zz in range(4):
            block_of(zz, core)
        yield
        copy.wait()
        for zz in range(4):
            pre_parts[zz, core, at] = pre_parts[zz, core, at] + in_core[zz, at]
        copies = []
        for k, (step, near) in enumerate(((1, zs[0]), (3, zs[1]), (2, opposite))):
            copies.append(
                pltpu.make_async_remote_copy(
                    src_ref=pre_parts.at[lax.rem(z + step, 4), core, at],
                    dst_ref=in_z.at[n, k],
                    send_sem=ssem.at[base + 1 + k],
                    recv_sem=rsem.at[base + 1 + k],
                    device_id=near,
                    device_id_type=MESH,
                )
            )
            copies[-1].start()
        yield
        for k, copy in enumerate(copies):
            copy.wait_recv()
            pre_parts[z, core, at] = pre_parts[z, core, at] + in_z[n, k]
        for copy in copies:
            copy.wait_send()

    used += 36
    owners = [half_route(n, used + 7 * n) for n in range(2)]
    used += 14
    next(owners[0])
    next(owners[1])

    sent = 160
    classes_all[:, sent:256, :] = jnp.zeros((2, 256 - sent, 8 * hid), jnp.float32)
    classes_all[:, 0:sent, 0:hid] = jnp.zeros((2, sent, hid), jnp.float32)
    classes_all[0, 0:classes, 0:hid] = cs_ref[...].astype(jnp.float32)
    classes_all[1, 0:classes, 0:hid] = cn_ref[...].astype(jnp.float32)
    class_spread = spread(
        lambda n, a: classes_all.at[:, pl.ds(0, sent), pl.ds((n * 2 + a) * hid, hid)], used
    )
    used += 7
    next(class_spread)
    next(class_spread)
    weights[...] = jnp.zeros_like(weights)
    weights[0:width, :] = ws_ref[...]
    weights[128 : 128 + width, :] = wn_ref[...]
    weights[256 : 256 + width, :] = wn_ref[...]
    cb_pad[...] = jnp.zeros_like(cb_pad)
    cb_pad[:, 0:classes] = cb_ref[...]
    extras[...] = jnp.zeros_like(extras)
    for s in range(seeds):
        label_rows[s : s + 1, :] = jnp.full((1, 256), labels_ref[0, s], jnp.int32)
    seed_cols = lax.broadcasted_iota(jnp.int32, (targets, seeds), 0)
    counted = jnp.zeros((targets, seeds), jnp.float32)
    for k in range(fan_two):
        counted = counted + jnp.where(seed_cols == links_ref[k], 1.0, 0.0)
    link_pad[...] = jnp.zeros_like(link_pad)
    link_pad[:, 0:seeds] = counted
    links_t = link_pad[...]
    links_f = links_t.T[0:seeds].astype(jnp.bfloat16)
    links_b = links_t.astype(jnp.bfloat16)
    target_rows = lax.broadcasted_iota(jnp.int32, (targets, 128), 0)

    own_classes = [classes_all[kind, :, 0:hid].astype(jnp.bfloat16) for kind in range(2)]
    class_three[...] = jnp.concatenate([own_classes[0], own_classes[1], own_classes[1]], axis=1)
    run_all(*owners)

    pre = pre_parts[z, core] + hb_ref[...]
    piece[0, 0] = pre
    pre_spread = spread(lambda n, a: piece.at[n, a], used)
    used += 7
    next(pre_spread)
    alive = (target_rows < live_ref[0]) & (pre > 0.0)
    hidden = jnp.where(alive, pre, 0.0).astype(jnp.bfloat16)
    hidden_ref[...] = hidden
    seed_neigh = dot(links_f, hidden) / fan_two
    neigh_two = jnp.concatenate(split(seed_neigh), axis=1)
    seed_three = jnp.concatenate([hidden[0:seeds], neigh_two], axis=1)
    logit_own[...] = lax.dot_general(
        seed_three, class_three[...], (((1,), (1,)), ((), ())), preferred_element_type=jnp.float32
    )
    to_core = core_copy(logit_own, logit_core, used)
    used += 1
    to_core.start()
    to_core.wait()
    logit_z[z] = logit_own[...] + logit_core[...]

    def z_sends(ref, base):
        copies = []
        for k, near in enumerate(zs + (opposite,)):
            copies.append(
                pltpu.make_async_remote_copy(
                    src_ref=ref,
                    dst_ref=ref,
                    send_sem=ssem.at[base + k],
                    recv_sem=rsem.at[base + k],
                    device_id=near,
                    device_id_type=MESH,
                )
            )
            copies[-1].start()
        return copies

    sends = z_sends(logit_z.at[z], used)
    used += 3
    next(pre_spread)
    run_all(class_spread)
    for kind in range(2):
        class_low[kind] = classes_all[kind].astype(jnp.bfloat16)
    self_t = self_all[...].T[0:width].astype(jnp.bfloat16)
    neigh_t_hi, neigh_t_lo = split(neigh_all[...].T[0:width])
    rows_three = jnp.concatenate([self_t, neigh_t_hi, neigh_t_lo], axis=0)
    for c in sends:
        c.wait()
    logits = (logit_z[0] + logit_z[1]) + (logit_z[2] + logit_z[3]) + cb_pad[...]
    lanes = lax.broadcasted_iota(jnp.int32, logits.shape, 1)
    logits = jnp.where(lanes < classes, logits, -1e30)
    top = jnp.max(logits, axis=1, keepdims=True)
    log_total = jnp.log(jnp.sum(jnp.exp(logits - top), axis=1, keepdims=True)) + top
    onehot = jnp.where(lanes == label_rows[...], 1.0, 0.0)
    losses = log_total - jnp.sum(onehot * logits, axis=1, keepdims=True)
    dlogit = jnp.exp(logits - log_total) - onehot
    dlogit_two = jnp.concatenate(split(dlogit), axis=0)

    def back(kind):
        both = dot(dlogit_two, class_low[kind])
        return both[0:seeds] + both[seeds : 2 * seeds]

    back_neigh = jnp.concatenate(
        [back(1) / fan_two, jnp.zeros((128 - seeds, 8 * hid), jnp.float32)], axis=0
    )
    links_two = jnp.concatenate([links_b, links_b], axis=1)
    acts[...] = dot(links_two, jnp.concatenate(split(back_neigh), axis=0))
    acts[0:seeds, :] = acts[0:seeds, :] + back(0)
    live_rows = target_rows < live_ref[0]

    def grad_of(n, across):
        at = (n * 2 + across) * hid
        return jnp.where(live_rows & (piece[n, across] > 0.0), acts[:, at : at + hid], 0.0)

    term_base = used
    used += groups

    def term_copy(k, dest, k_recv):
        return pltpu.make_async_remote_copy(
            src_ref=terms.at[k],
            dst_ref=in_terms.at[group],
            send_sem=ssem.at[term_base + k],
            recv_sem=rsem.at[term_base + k_recv],
            device_id=(dest, m),
            device_id_type=MESH,
        )

    dests = {}

    hidden_line = []

    def block_terms(step, n, across):
        zz = lax.rem(z + 4 - n, 4)
        cc = 1 - core if across else core
        grad_pre = grad_of(n, across)
        if step == 0:
            hidden_line.append(jnp.sum(grad_pre, axis=0, keepdims=True))
        term = dot(rows_three, jnp.concatenate(split(grad_pre), axis=1))
        terms[2 * step] = term[0:width, 0:hid] + term[0:width, hid : 2 * hid]
        neigh_term = term[width : 2 * width, 0:hid] + term[width : 2 * width, hid : 2 * hid]
        terms[2 * step + 1] = neigh_term + term[2 * width : 3 * width, 0:hid]
        for s in range(2):
            k = 2 * step + s
            dests[k] = dest = zz * 4 + cc * 2 + s

            @pl.when(dest != group)
            def _():
                term_copy(k, dest, group).start()

            @pl.when(dest == group)
            def _():
                in_terms[group] = terms[k]

    block_terms(0, 0, 0)
    block_terms(1, *next(pre_spread))

    dlogit_t = jnp.concatenate(split(dlogit.T[0:sent]), axis=0)
    both = dot(dlogit_t, seed_three)
    both = [both[:, n * hid : n * hid + hid] for n in range(3)]
    class_grads = jnp.concatenate(
        [both[0][0:sent] + both[0][sent:], both[1][0:sent] + both[1][sent:] + both[2][0:sent]], axis=0
    )
    per = extras.shape[1]
    for n in range(0, 320, 8):
        extras[n // per, n % per : n % per + 8] = class_grads[n : n + 8]
    row_sum = jnp.sum(dlogit, axis=0, keepdims=True)
    lines = (
        hidden_line[0],
        row_sum[:, 0:128],
        row_sum[:, 128:256],
        jnp.broadcast_to(jnp.sum(losses, axis=0, keepdims=True), (1, 128)),
    )
    for n, line in enumerate(lines):
        extras[320 // per, 320 % per + n : 320 % per + n + 1] = line
    extra_sends = []
    for r in range(1, groups):
        copy = pltpu.make_async_remote_copy(
            src_ref=extras.at[lax.rem(group + r, groups)],
            dst_ref=in_extras.at[r],
            send_sem=ssem.at[used + r - 1],
            recv_sem=rsem.at[used + r - 1],
            device_id=others[r - 1],
            device_id_type=MESH,
        )
        copy.start()
        extra_sends.append(copy)
    used += groups - 1

    for step in range(2, groups // 2):
        block_terms(step, *next(pre_spread))
    run_all(pre_spread)

    for copy in extra_sends:
        copy.wait_recv()
    total = extras[group]
    for r in range(1, groups):
        total = total + in_extras[r]
    sums_ref[x, y, width : width + per] = total
    for source in range(groups):

        @pl.when(source != group)
        def _():
            pltpu.make_async_remote_copy(
                src_ref=terms.at[0],
                dst_ref=in_terms.at[source],
                send_sem=ssem.at[term_base],
                recv_sem=rsem.at[term_base + source],
                device_id=(source, m),
                device_id_type=MESH,
            ).wait_recv()

    total = in_terms[0]
    for source in range(1, groups):
        total = total + in_terms[source]
    sums_ref[x, y, 0:width] = total
    spans = ((0, 0, 56), (1, 56, 64))
    last = grid_gather(sums_ref, spans, ssem, rsem, used, x, y, grid_device)
    used += 30
    for route in last:
        next(route)
    for copy in extra_sends:
        copy.wait_send()
    for k in range(groups):
        dest = dests[k]

        @pl.when(dest != group)
        def _():
            term_copy(k, dest, group).wait_send()

    run_all(*last)
    assert used <= SEMS


SEMS = 160


def finish_kernel(scale, hidden_ref, sums_ref, *outs):
    hidden_out, self_out, neigh_out, hb_out, cs_out, cn_out, cb_out, loss_out, lines = outs
    width = self_out.shape[0]
    hid = hidden_ref.shape[1]
    groups, rows = sums_ref.shape[:2]
    per = rows - width
    hidden_out[...] = hidden_ref[...]
    for n in range(groups):
        out = neigh_out if n % 2 else self_out
        at = n // 2 * hid
        out[:, at : at + hid] = sums_ref[n, 0:width, :]
        lines[n * per : n * per + per, :] = sums_ref[n, width:rows, :]
    classes = cs_out.shape[0]
    cs_out[...] = lines[0:classes, :]
    cn_out[...] = lines[160 : 160 + classes, :]
    hb_out[...] = lines[320:321, :]
    cb_out[:, 0:128] = lines[321:322, :]
    cb_out[:, 128:classes] = lines[322:323, 0 : classes - 128]
    loss_out[...] = lines[323:324, :] * scale


def body(
    node_features,
    target_nodes,
    first_hop,
    live_counts,
    seed_links,
    seed_labels,
    self_weight,
    neigh_weight,
    hidden_bias,
    class_self,
    class_neigh,
    class_bias,
):
    node_rows = node_features.shape[1]
    batches, targets = target_nodes.shape
    fan_one = first_hop.shape[1]
    seeds, fan_two = seed_links.shape[1:]
    hid = hidden_bias.shape[0]
    width, hidden_all = self_weight.shape
    classes = class_bias.shape[0]
    offset = (lax.axis_index("group") * node_rows).astype(jnp.int32)[None]
    parts = gather_rows(node_features, target_nodes, first_hop, offset).reshape(4, 4, 384, 128)
    f32, vmem = jnp.float32, pl.BlockSpec(memory_space=pltpu.VMEM)
    smem = pl.BlockSpec(memory_space=pltpu.SMEM)
    shapes = [
        ((4, 4, 384, 128), f32),
        ((4, 6, 4, 48, 128), f32),
        ((4, 3, 96, 128), f32),
        ((384, hidden_all), jnp.bfloat16),
        ((4, 2, targets, hid), f32),
        ((4, targets, hid), f32),
        ((2, 3, targets // 2, hid), f32),
        ((2, 256, 8 * hid), f32),
        ((2, 256, 8 * hid), jnp.bfloat16),
        ((256, 3 * hid), jnp.bfloat16),
        ((targets, 128), f32),
        ((targets, 128), f32),
        ((1, 256), f32),
        ((targets, 8 * hid), f32),
        ((seeds, 256), jnp.int32),
        ((targets, 128), f32),
        ((seeds, 256), f32),
        ((seeds, 256), f32),
        ((4, seeds, 256), f32),
        ((4, 2, targets, hid), f32),
        ((16, width, 128), f32),
        ((16, width, 128), f32),
        ((16, 24, 128), f32),
        ((16, 24, 128), f32),
    ]
    hidden_layer, sums = pl.pallas_call(
        functools.partial(exchange_kernel, fan_one, fan_two),
        out_shape=(
            jax.ShapeDtypeStruct((targets, hid), jnp.bfloat16),
            jax.ShapeDtypeStruct((4, 4, width + 24, 128), f32),
        ),
        in_specs=[pl.BlockSpec(memory_space=pl.ANY)] + [vmem] * 6 + [smem, vmem, smem],
        out_specs=(vmem, vmem),
        scratch_shapes=[pltpu.VMEM(shape, kind) for shape, kind in shapes]
        + [
            pltpu.SemaphoreType.DMA,
            pltpu.SemaphoreType.DMA((SEMS,)),
            pltpu.SemaphoreType.DMA((SEMS,)),
        ],
        compiler_params=pltpu.CompilerParams(
            collective_id=0, has_side_effects=True, vmem_limit_bytes=48 * 1024 * 1024
        ),
        name="exchange",
    )(
        parts,
        self_weight,
        neigh_weight,
        hidden_bias[None],
        class_self.T,
        class_neigh.T,
        class_bias[None],
        live_counts,
        jnp.transpose(seed_links, (2, 0, 1)),
        seed_labels,
    )
    outs = pl.pallas_call(
        functools.partial(finish_kernel, 1.0 / (batches * seeds)),
        out_shape=(
            jax.ShapeDtypeStruct((targets, hid), jnp.bfloat16),
            jax.ShapeDtypeStruct((width, hidden_all), f32),
            jax.ShapeDtypeStruct((width, hidden_all), f32),
            jax.ShapeDtypeStruct((1, hid), f32),
            jax.ShapeDtypeStruct((classes, hid), f32),
            jax.ShapeDtypeStruct((classes, hid), f32),
            jax.ShapeDtypeStruct((1, classes), f32),
            jax.ShapeDtypeStruct((1, 128), f32),
        ),
        in_specs=[vmem] * 2,
        out_specs=(vmem,) * 8,
        scratch_shapes=[pltpu.VMEM((16 * 24, 128), f32)],
        compiler_params=pltpu.CompilerParams(vmem_limit_bytes=8 * 1024 * 1024),
        name="finish",
    )(hidden_layer, sums.reshape(16, width + 24, 128))
    return (
        outs[0],
        outs[1],
        outs[2],
        outs[3][0],
        outs[4].T,
        outs[5].T,
        outs[6][0],
        outs[7][0, 0],
    )


def solution(mesh):
    in_specs = (
        P("mp", "group"),
        P(),
        P(),
        P("group"),
        P("group", None, None),
        P("group", None),
        P("mp", None),
        P("mp", None),
        P("mp"),
        P("mp", None),
        P("mp", None),
        P(),
    )
    out_specs = (
        P("group", "mp"),
        P("mp", None),
        P("mp", None),
        P("mp"),
        P("mp", None),
        P("mp", None),
        P(),
        P(),
    )
    return jax.shard_map(body, mesh=mesh, in_specs=in_specs, out_specs=out_specs, check_vma=False)
```

```python
import functools
import jax
import jax.numpy as jnp
from jax import lax
from jax.experimental import pallas as pl
from jax.experimental.pallas import tpu as pltpu
from jax.sharding import PartitionSpec as P

UNROLL = 16
TOP = 3
BLOCK = 28
TURNS = 128


def gather_kernel(offset_ref, feat_hbm, targets_hbm, hops_hbm, out_ref, feat_ref, targets_ref, hops_ref, table, acc, ids, codes, counts, first_s, counts_s, extra_s, sems, load_sems):
    loads = [
        pltpu.make_async_copy(src, dst, load_sems.at[n])
        for n, (src, dst) in enumerate(((hops_hbm, hops_ref), (targets_hbm, targets_ref), (feat_hbm, feat_ref)))
    ]
    for load in loads:
        load.start()
    width, nodes = feat_ref.shape
    lists, rows = ids.shape[:2]
    fan, batches, targets = hops_ref.shape
    used = fan + 1
    half = rows * 128
    slots = 2 * half
    cols = targets // 128
    loads[0].wait()
    loads[1].wait()
    for n in range(cols):
        at, wide = pl.ds(n * batches, batches), slice(n * 128, n * 128 + 128)
        ids[0:fan, at] = hops_ref[:, :, wide] - offset_ref[0]
        ids[fan, at] = targets_ref[:, wide] - offset_ref[0]
    ids[used:lists] = jnp.full((lists - used, rows, 128), -1, jnp.int32)
    lane = lax.broadcasted_iota(jnp.int32, (BLOCK, rows, 128), 2)
    sub = lax.broadcasted_iota(jnp.int32, (BLOCK, rows, 128), 1)
    outer = lax.broadcasted_iota(jnp.int32, (BLOCK, rows, 128), 0)
    row_i = lax.broadcasted_iota(jnp.int32, (128, 128), 0)
    col_i = lax.broadcasted_iota(jnp.int32, (128, 128), 1)
    before = jnp.where(row_i < col_i, 1.0, 0.0).astype(jnp.bfloat16)
    ones = jnp.ones((128, 128), jnp.bfloat16)
    row_r = lax.broadcasted_iota(jnp.int32, (BLOCK * rows, BLOCK * rows), 0)
    col_r = lax.broadcasted_iota(jnp.int32, (BLOCK * rows, BLOCK * rows), 1)
    same = (row_r // rows) == (col_r // rows)
    above = jnp.where(same & (col_r < row_r), 1.0, 0.0).astype(jnp.bfloat16)
    shift = (nodes - 1).bit_length()
    steps = (half - 1).bit_length()
    flag = 1 << (shift + steps)

    def turn(i):
        at = pl.multiple_of(i * 128, 128)
        part = feat_ref[:, pl.ds(at, 128)].astype(jnp.float32)
        part = jnp.concatenate([part, jnp.zeros((128 - width, 128), jnp.float32)], axis=0)
        table[pl.ds(at, 128), :] = part.T

    def compact(q, carry):
        local = ids[pl.ds(q * BLOCK, BLOCK)]
        inside = (local >= 0) & (local < nodes)
        out_b = jnp.where(inside, 0.0, 1.0).reshape(BLOCK * rows, 128).astype(jnp.bfloat16)
        pref = jnp.dot(out_b, before, preferred_element_type=jnp.float32)
        total = jnp.dot(out_b, ones, preferred_element_type=jnp.float32)
        scan = jnp.dot(above, total.astype(jnp.bfloat16), preferred_element_type=jnp.float32)
        moved = (pref + scan).reshape(BLOCK, rows, 128).astype(jnp.int32)
        total = total.reshape(BLOCK, rows, 128)
        for b in range(BLOCK):
            missing = jnp.sum(total[b], axis=0, keepdims=True)
            counts[pl.ds(q * BLOCK + b, 1), :] = (half - missing).astype(jnp.int32)
        x = jnp.where(inside, flag | (moved << shift) | local, 0)
        for j in range(steps):
            d = 1 << j
            if j < 7:
                y = pltpu.roll(x, 128 - d, 2)
                y = jnp.where(lane < 128 - d, y, pltpu.roll(y, rows - 1, 1))
            else:
                y = pltpu.roll(x, rows - d // 128, 1)
            bit = 1 << (shift + j)
            x = jnp.where((y & bit) != 0, y, jnp.where((x & bit) != 0, 0, x))
        place = sub * 128 + lane + ((x >> shift) & (half - 1))
        row = place >> 7
        slot = (row % batches) * targets + (row // batches) * 128 + (place & 127)
        slot = slot + jnp.where(q * BLOCK + outer == fan, half, 0)
        code = jnp.where(x != 0, (slot << 15) | (x & (nodes - 1)), (slots << 15) | nodes)
        codes[pl.ds(q * BLOCK, BLOCK)] = code
        for n in range(TURNS):
            turn(q * TURNS + n)
        return carry

    loads[2].wait()
    lax.fori_loop(0, lists // BLOCK, compact, 0)
    copy_counts = pltpu.make_async_copy(counts, counts_s, sems.at[0])
    copy_counts.start()
    copies = []
    for j in range(used):
        for r in range(TOP):
            n = j * TOP + r
            copy = pltpu.make_async_copy(codes.at[j, r], first_s.at[pl.ds(n * 128, 128)], sems.at[n + 2])
            copy.start()
            copies.append(copy)

    def turn_rest(i, carry):
        turn(i)
        return carry

    lax.fori_loop(lists // BLOCK * TURNS, nodes // 128, turn_rest, 0)
    table[pl.ds(nodes, 8), :] = jnp.zeros((8, 128), jnp.float32)

    def clear(i, carry):
        acc[pl.ds(pl.multiple_of(i * 128, 128), 128), :] = jnp.zeros((128, 128), jnp.float32)
        return carry

    lax.fori_loop(0, slots // 128, clear, 0)
    acc[pl.ds(slots, 8), :] = jnp.zeros((8, 128), jnp.float32)
    copy_counts.wait()
    for copy in copies:
        copy.wait()

    def add_group(ref, base):
        code = [ref[base + u] for u in range(UNROLL)]
        at = [c >> 15 for c in code]
        rows = [table[pl.ds(c & 32767, 1), :] for c in code]
        olds = [acc[pl.ds(a, 1), :] for a in at]
        for a, old, row in zip(at, olds, rows):
            acc[pl.ds(a, 1), :] = old + row

    span = TOP * 128

    def step(state):
        j, k = state
        add_group(first_s, j * span + k)
        k = k + UNROLL
        done = k >= jnp.minimum(counts_s[j, 0], span)
        return jnp.where(done, j + 1, j), jnp.where(done, 0, k)

    lax.while_loop(lambda state: state[0] < used, step, (0, 0))

    def rest(j, carry):
        n = counts_s[j, 0]

        @pl.when(n > span)
        def _():
            def one(r, inner):
                copy = pltpu.make_async_copy(codes.at[j, r], extra_s, sems.at[1])
                copy.start()
                copy.wait()

                def group(i, inner2):
                    add_group(extra_s, i * UNROLL)
                    return inner2

                return lax.fori_loop(0, 128 // UNROLL, group, inner)

            lax.fori_loop(TOP, (n + 127) // 128, one, 0)

        return carry

    lax.fori_loop(0, used, rest, 0)

    lanes = lax.broadcasted_iota(jnp.int32, (32, 128), 1)

    def pack(i, carry):
        for s in range(2):
            for n in range(2):
                base = (1 - s) * half + i * 256 + n * 128
                a, b, c, d = [acc[pl.ds(pl.multiple_of(base + k * 32, 32), 32), :] for k in range(4)]
                b, c, d = pltpu.roll(b, 96, 1), pltpu.roll(c, 64, 1), pltpu.roll(d, 32, 1)
                row = s * 192 + n * 96
                out_ref[i, pl.ds(row, 32), :] = jnp.where(lanes < 96, a, b)
                out_ref[i, pl.ds(row + 32, 32), :] = jnp.where(lanes < 64, b, c)
                out_ref[i, pl.ds(row + 64, 32), :] = jnp.where(lanes < 32, c, d)
        return carry

    lax.fori_loop(0, half // 256, pack, 0)


def gather_rows(features, target_nodes, first_hop, offset):
    nodes = features.shape[1]
    batches, targets = target_nodes.shape
    rows = batches * targets // 128
    lists = 28
    hbm = pl.BlockSpec(memory_space=pltpu.HBM)
    hops = jnp.moveaxis(first_hop, 1, 0)
    return pl.pallas_call(
        gather_kernel,
        out_shape=jax.ShapeDtypeStruct((batches, 384, 128), jnp.float32),
        in_specs=[pl.BlockSpec(memory_space=pltpu.SMEM)] + [hbm] * 3,
        out_specs=pl.BlockSpec(memory_space=pltpu.VMEM),
        scratch_shapes=[
            pltpu.VMEM(features.shape, features.dtype),
            pltpu.VMEM(target_nodes.shape, jnp.int32),
            pltpu.VMEM(hops.shape, jnp.int32),
            pltpu.VMEM((nodes + 8, 128), jnp.float32),
            pltpu.VMEM((batches * 512 + 8, 128), jnp.float32),
            pltpu.VMEM((lists, rows, 128), jnp.int32),
            pltpu.VMEM((lists, rows, 128), jnp.int32),
            pltpu.VMEM((lists + 4, 128), jnp.int32),
            pltpu.SMEM((lists * TOP * 128,), jnp.int32),
            pltpu.SMEM((lists + 4, 128), jnp.int32),
            pltpu.SMEM((128,), jnp.int32),
            pltpu.SemaphoreType.DMA((lists * TOP + 2,)),
            pltpu.SemaphoreType.DMA((3,)),
        ],
        compiler_params=pltpu.CompilerParams(vmem_limit_bytes=48 * 1024 * 1024),
        name="gather_rows",
    )(offset, features, target_nodes, hops)


MESH = pl.DeviceIdType.MESH


def run_all(*routes):
    active = list(routes)
    while active:
        for route in list(active):
            try:
                next(route)
            except StopIteration:
                active.remove(route)


def ring_sum(blk, inb, ssem, rsem, base, i, right, left):
    after, before, across = lax.rem(i + 1, 4), lax.rem(i + 3, 4), lax.rem(i + 2, 4)

    def copy(src, k, device):
        return pltpu.make_async_remote_copy(
            src_ref=src,
            dst_ref=inb(k),
            send_sem=ssem.at[base + k],
            recv_sem=rsem.at[base + k],
            device_id=device,
            device_id_type=MESH,
        )

    c0 = copy(blk(across, 0), 0, right)
    c1 = copy(blk(across, 1), 1, left)
    c2 = copy(blk(after, 1), 2, right)
    c3 = copy(blk(before, 0), 3, left)
    c4 = copy(blk(after, 0), 4, right)
    c5 = copy(blk(before, 1), 5, left)
    for c in (c0, c1, c2, c3):
        c.start()
    yield
    c0.wait_recv()
    blk(after, 0)[...] = blk(after, 0)[...] + inb(0)[...]
    c4.start()
    c1.wait_recv()
    blk(before, 1)[...] = blk(before, 1)[...] + inb(1)[...]
    c5.start()
    yield
    c3.wait_recv()
    c2.wait_recv()
    blk(i, 0)[...] = blk(i, 0)[...] + inb(3)[...]
    blk(i, 1)[...] = blk(i, 1)[...] + inb(2)[...]
    yield
    c4.wait_recv()
    blk(i, 0)[...] = blk(i, 0)[...] + inb(4)[...]
    c5.wait_recv()
    blk(i, 1)[...] = blk(i, 1)[...] + inb(5)[...]
    for c in (c0, c1, c2, c3, c4, c5):
        c.wait_send()


def grid_sum(buf, spans, in_wide, in_thin, ssem, rsem, base, x, y, xs, ys, device):
    def route(h, n, lo, half):
        def wide(d, p):
            at = pl.ds(lo + p * half, half)
            return buf.at[d, :, at] if h == 0 else buf.at[:, d, at]

        def thin(d):
            at = pl.ds(lo, 2 * half)
            return buf.at[x, d, at] if h == 0 else buf.at[d, y, at]

        first = (x,) + xs if h == 0 else (y,) + ys
        yield from ring_sum(wide, lambda k: in_wide.at[n, k], ssem, rsem, base + n * 9, *first)
        i = y if h == 0 else x
        copies = []
        for k, step in enumerate((1, 3, 2)):
            copies.append(
                pltpu.make_async_remote_copy(
                    src_ref=thin(lax.rem(i + step, 4)),
                    dst_ref=in_thin.at[n, k],
                    send_sem=ssem.at[base + n * 9 + 6 + k],
                    recv_sem=rsem.at[base + n * 9 + 6 + k],
                    device_id=device(0, step) if h == 0 else device(step, 0),
                    device_id_type=MESH,
                )
            )
            copies[-1].start()
        yield
        for k, copy in enumerate(copies):
            copy.wait_recv()
            thin(i)[...] = thin(i)[...] + in_thin[n, k]
        for copy in copies:
            copy.wait_send()

    return [route(*span) for span in spans]


def together(routes):
    active = list(routes)
    while active:
        for route in list(active):
            try:
                next(route)
            except StopIteration:
                active.remove(route)
        yield


def grid_gather(buf, spans, ssem, rsem, base, x, y, device):
    def route(n, h, lo, rows):
        at = pl.ds(lo, rows)

        def near(dx, dy):
            return device(dx, dy) if h == 0 else device(dy, dx)

        def place(far, close):
            return buf.at[far, close, at] if h == 0 else buf.at[close, far, at]

        far, close = (x, y) if h == 0 else (y, x)
        started = []

        def send(ref, k, target):
            copy = pltpu.make_async_remote_copy(
                src_ref=ref,
                dst_ref=ref,
                send_sem=ssem.at[base + n * 15 + k],
                recv_sem=rsem.at[base + n * 15 + k],
                device_id=target,
                device_id_type=MESH,
            )
            copy.start()
            started.append(copy)

        for d in (1, 3, 2):
            send(place(far, close), d - 1, near(0, d))
        for d in (1, 3, 2):
            send(place(far, close), 2 + d, near(d, 0))
        firsts = list(started)
        for n2, d in enumerate((1, 3, 2)):
            yield
            firsts[n2].wait_recv()
            source = lax.rem(close + 4 - d, 4)
            for e in (1, 3, 2):
                send(place(far, source), 3 * d + 2 + e, near(e, 0))
        yield
        for copy in started[3:]:
            copy.wait_recv()
        for copy in started:
            copy.wait_send()

    return [route(n, *span) for n, span in enumerate(spans)]


def unpack(ref, x, y, row):
    lane = lax.broadcasted_iota(jnp.int32, (32, 128), 1)
    p = [ref[x, y, pl.ds(row + 32 * n, 32), :] for n in range(3)]
    b = jnp.where(lane < 32, pltpu.roll(p[0], 32, 1), pltpu.roll(p[1], 32, 1))
    c = jnp.where(lane < 64, pltpu.roll(p[1], 64, 1), pltpu.roll(p[2], 64, 1))
    d = pltpu.roll(p[2], 96, 1)
    out = [jnp.where(lane < 96, v, 0.0) for v in (p[0], b, c, d)]
    return jnp.concatenate(out, axis=0)


def split(v):
    hi = v.astype(jnp.bfloat16)
    return hi, (v - hi.astype(jnp.float32)).astype(jnp.bfloat16)


def dot(a, b):
    return jnp.dot(a, b, preferred_element_type=jnp.float32)


def exchange_kernel(
    fan_one,
    fan_two,
    parts_ref,
    ws_ref,
    wn_ref,
    hb_ref,
    cs_ref,
    cn_ref,
    cb_ref,
    live_ref,
    links_ref,
    labels_ref,
    hidden_ref,
    sums_ref,
    parts,
    in_wide,
    in_thin,
    weights,
    pre_parts,
    in_core,
    in_z,
    classes_all,
    class_low,
    class_three,
    self_all,
    neigh_all,
    cb_pad,
    acts,
    label_rows,
    link_pad,
    logit_own,
    logit_core,
    logit_z,
    piece,
    terms,
    in_terms,
    extras,
    in_extras,
    local_sem,
    ssem,
    rsem,
):
    group = lax.axis_index("group")
    m = lax.axis_index("mp")
    x, y = lax.div(group, 4), lax.rem(group, 4)
    z, core = lax.div(m, 2), lax.rem(m, 2)
    groups = in_terms.shape[0]

    def up(i, n):
        return lax.rem(i + n, 4)

    def grid_device(dx, dy):
        return (up(x, dx) * 4 + up(y, dy), m)

    def z_device(dz):
        return (group, up(z, dz) * 2 + core)

    xs = (grid_device(1, 0), grid_device(3, 0))
    ys = (grid_device(0, 1), grid_device(0, 3))
    zs = (z_device(1), z_device(3))
    opposite = z_device(2)
    sibling = (group, z * 2 + 1 - core)
    others = [(lax.rem(group + r, groups), m) for r in range(1, groups)]

    load = pltpu.make_async_copy(parts_ref, parts, local_sem)
    load.start()
    barrier = pltpu.get_barrier_semaphore()
    axis_far = [grid_device(2, 0), grid_device(0, 2)]
    nears = list(xs + ys + zs) + axis_far + [opposite, sibling]
    for near in nears:
        pl.semaphore_signal(barrier, inc=1, device_id=near, device_id_type=MESH)
    pl.semaphore_wait(barrier, len(nears))
    load.wait()

    def core_copy(src, dst, k):
        return pltpu.make_async_remote_copy(
            src_ref=src,
            dst_ref=dst,
            send_sem=ssem.at[k],
            recv_sem=rsem.at[k],
            device_id=sibling,
            device_id_type=MESH,
        )

    def spread(ref_of, base):
        started = []
        for k, (slot, near) in enumerate(((1, zs[0]), (3, zs[1]), (2, opposite))):
            started.append(
                pltpu.make_async_remote_copy(
                    src_ref=ref_of(0, 0),
                    dst_ref=ref_of(slot, 0),
                    send_sem=ssem.at[base + k],
                    recv_sem=rsem.at[base + k],
                    device_id=near,
                    device_id_type=MESH,
                )
            )
        started.append(core_copy(ref_of(0, 0), ref_of(0, 1), base + 3))
        for k in (0, 1, 3):
            started[k].start()
        yield (0, 0)
        started[2].start()
        yield (0, 0)
        started[3].wait_recv()
        yield (0, 1)
        for k, slot in enumerate((1, 3)):
            started[k].wait_recv()
            started.append(core_copy(ref_of(slot, 0), ref_of(slot, 1), base + 3 + slot))
            started[-1].start()
            yield (slot, 0)
        for k, slot in enumerate((1, 3)):
            started[4 + k].wait_recv()
            yield (slot, 1)
        started[2].wait_recv()
        started.append(core_copy(ref_of(2, 0), ref_of(2, 1), base + 5))
        started[-1].start()
        yield (2, 0)
        started[6].wait_recv()
        yield (2, 1)
        for copy in started:
            copy.wait_send()

    used = 0
    width = ws_ref.shape[0]
    targets, hid = hidden_ref.shape
    half_rows = targets // 2
    seeds = labels_ref.shape[1]
    classes = cs_ref.shape[0]

    def half_route(n, base):
        spans = ((0, 2 * n, n * 96, 48), (1, 2 * n + 1, 192 + n * 96, 48))
        yield from together(grid_sum(parts, spans, in_wide, in_thin, ssem, rsem, 0, x, y, xs, ys, grid_device))
        at = pl.ds(n * half_rows, half_rows)
        own_self = unpack(parts, x, y, n * 96)
        own_neigh = unpack(parts, x, y, 192 + n * 96) / fan_one
        self_all[at, :] = own_self
        neigh_all[at, :] = own_neigh
        neigh_hi, neigh_lo = split(own_neigh)
        left_side = jnp.concatenate([own_self.astype(jnp.bfloat16), neigh_hi, neigh_lo], axis=1)

        def block_of(zz, cc):
            cols = pl.multiple_of((zz * 2 + cc) * hid, hid)
            pre_parts[zz, cc, at] = dot(left_side, weights[:, pl.ds(cols, hid)])

        for zz in range(4):
            block_of(zz, 1 - core)
        copy = core_copy(pre_parts.at[:, 1 - core, at], in_core.at[:, at], base)
        copy.start()
        for zz in range(4):
            block_of(zz, core)
        yield
        copy.wait()
        for zz in range(4):
            pre_parts[zz, core, at] = pre_parts[zz, core, at] + in_core[zz, at]
        copies = []
        for k, (step, near) in enumerate(((1, zs[0]), (3, zs[1]), (2, opposite))):
            copies.append(
                pltpu.make_async_remote_copy(
                    src_ref=pre_parts.at[lax.rem(z + step, 4), core, at],
                    dst_ref=in_z.at[n, k],
                    send_sem=ssem.at[base + 1 + k],
                    recv_sem=rsem.at[base + 1 + k],
                    device_id=near,
                    device_id_type=MESH,
                )
            )
            copies[-1].start()
        yield
        for k, copy in enumerate(copies):
            copy.wait_recv()
            pre_parts[z, core, at] = pre_parts[z, core, at] + in_z[n, k]
        for copy in copies:
            copy.wait_send()

    used += 36
    owners = [half_route(n, used + 7 * n) for n in range(2)]
    used += 14
    next(owners[0])
    next(owners[1])

    sent = 160
    classes_all[:, sent:256, :] = jnp.zeros((2, 256 - sent, 8 * hid), jnp.float32)
    classes_all[:, 0:sent, 0:hid] = jnp.zeros((2, sent, hid), jnp.float32)
    classes_all[0, 0:classes, 0:hid] = cs_ref[...].astype(jnp.float32)
    classes_all[1, 0:classes, 0:hid] = cn_ref[...].astype(jnp.float32)
    class_spread = spread(
        lambda n, a: classes_all.at[:, pl.ds(0, sent), pl.ds((n * 2 + a) * hid, hid)], used
    )
    used += 7
    next(class_spread)
    next(class_spread)
    weights[...] = jnp.zeros_like(weights)
    weights[0:width, :] = ws_ref[...]
    weights[128 : 128 + width, :] = wn_ref[...]
    weights[256 : 256 + width, :] = wn_ref[...]
    cb_pad[...] = jnp.zeros_like(cb_pad)
    cb_pad[:, 0:classes] = cb_ref[...]
    extras[...] = jnp.zeros_like(extras)
    for s in range(seeds):
        label_rows[s : s + 1, :] = jnp.full((1, 256), labels_ref[0, s], jnp.int32)
    seed_cols = lax.broadcasted_iota(jnp.int32, (targets, seeds), 0)
    counted = jnp.zeros((targets, seeds), jnp.float32)
    for k in range(fan_two):
        counted = counted + jnp.where(seed_cols == links_ref[k], 1.0, 0.0)
    link_pad[...] = jnp.zeros_like(link_pad)
    link_pad[:, 0:seeds] = counted
    links_t = link_pad[...]
    links_f = links_t.T[0:seeds].astype(jnp.bfloat16)
    links_b = links_t.astype(jnp.bfloat16)
    target_rows = lax.broadcasted_iota(jnp.int32, (targets, 128), 0)

    own_classes = [classes_all[kind, :, 0:hid].astype(jnp.bfloat16) for kind in range(2)]
    class_three[...] = jnp.concatenate([own_classes[0], own_classes[1], own_classes[1]], axis=1)
    run_all(*owners)

    pre = pre_parts[z, core] + hb_ref[...]
    piece[0, 0] = pre
    pre_spread = spread(lambda n, a: piece.at[n, a], used)
    used += 7
    next(pre_spread)
    alive = (target_rows < live_ref[0]) & (pre > 0.0)
    hidden = jnp.where(alive, pre, 0.0).astype(jnp.bfloat16)
    hidden_ref[...] = hidden
    seed_neigh = dot(links_f, hidden) / fan_two
    neigh_two = jnp.concatenate(split(seed_neigh), axis=1)
    seed_three = jnp.concatenate([hidden[0:seeds], neigh_two], axis=1)
    logit_own[...] = lax.dot_general(
        seed_three, class_three[...], (((1,), (1,)), ((), ())), preferred_element_type=jnp.float32
    )
    to_core = core_copy(logit_own, logit_core, used)
    used += 1
    to_core.start()
    to_core.wait()
    logit_z[z] = logit_own[...] + logit_core[...]

    def z_sends(ref, base):
        copies = []
        for k, near in enumerate(zs + (opposite,)):
            copies.append(
                pltpu.make_async_remote_copy(
                    src_ref=ref,
                    dst_ref=ref,
                    send_sem=ssem.at[base + k],
                    recv_sem=rsem.at[base + k],
                    device_id=near,
                    device_id_type=MESH,
                )
            )
            copies[-1].start()
        return copies

    sends = z_sends(logit_z.at[z], used)
    used += 3
    next(pre_spread)
    run_all(class_spread)
    for kind in range(2):
        class_low[kind] = classes_all[kind].astype(jnp.bfloat16)
    self_t = self_all[...].T[0:width].astype(jnp.bfloat16)
    neigh_t_hi, neigh_t_lo = split(neigh_all[...].T[0:width])
    rows_three = jnp.concatenate([self_t, neigh_t_hi, neigh_t_lo], axis=0)
    for c in sends:
        c.wait()
    logits = (logit_z[0] + logit_z[1]) + (logit_z[2] + logit_z[3]) + cb_pad[...]
    lanes = lax.broadcasted_iota(jnp.int32, logits.shape, 1)
    logits = jnp.where(lanes < classes, logits, -1e30)
    top = jnp.max(logits, axis=1, keepdims=True)
    log_total = jnp.log(jnp.sum(jnp.exp(logits - top), axis=1, keepdims=True)) + top
    onehot = jnp.where(lanes == label_rows[...], 1.0, 0.0)
    losses = log_total - jnp.sum(onehot * logits, axis=1, keepdims=True)
    dlogit = jnp.exp(logits - log_total) - onehot
    dlogit_two = jnp.concatenate(split(dlogit), axis=0)

    def back(kind):
        both = dot(dlogit_two, class_low[kind])
        return both[0:seeds] + both[seeds : 2 * seeds]

    back_neigh = jnp.concatenate(
        [back(1) / fan_two, jnp.zeros((128 - seeds, 8 * hid), jnp.float32)], axis=0
    )
    links_two = jnp.concatenate([links_b, links_b], axis=1)
    acts[...] = dot(links_two, jnp.concatenate(split(back_neigh), axis=0))
    acts[0:seeds, :] = acts[0:seeds, :] + back(0)
    live_rows = target_rows < live_ref[0]

    def grad_of(n, across):
        at = (n * 2 + across) * hid
        return jnp.where(live_rows & (piece[n, across] > 0.0), acts[:, at : at + hid], 0.0)

    term_base = used
    used += groups

    def term_copy(k, dest, k_recv):
        return pltpu.make_async_remote_copy(
            src_ref=terms.at[k],
            dst_ref=in_terms.at[group],
            send_sem=ssem.at[term_base + k],
            recv_sem=rsem.at[term_base + k_recv],
            device_id=(dest, m),
            device_id_type=MESH,
        )

    dests = {}

    hidden_line = []

    def block_terms(step, n, across):
        zz = lax.rem(z + 4 - n, 4)
        cc = 1 - core if across else core
        grad_pre = grad_of(n, across)
        if step == 0:
            hidden_line.append(jnp.sum(grad_pre, axis=0, keepdims=True))
        term = dot(rows_three, jnp.concatenate(split(grad_pre), axis=1))
        terms[2 * step] = term[0:width, 0:hid] + term[0:width, hid : 2 * hid]
        neigh_term = term[width : 2 * width, 0:hid] + term[width : 2 * width, hid : 2 * hid]
        terms[2 * step + 1] = neigh_term + term[2 * width : 3 * width, 0:hid]
        for s in range(2):
            k = 2 * step + s
            dests[k] = dest = zz * 4 + cc * 2 + s

            @pl.when(dest != group)
            def _():
                term_copy(k, dest, group).start()

            @pl.when(dest == group)
            def _():
                in_terms[group] = terms[k]

    block_terms(0, 0, 0)
    block_terms(1, *next(pre_spread))

    dlogit_t = jnp.concatenate(split(dlogit.T[0:sent]), axis=0)
    both = dot(dlogit_t, seed_three)
    both = [both[:, n * hid : n * hid + hid] for n in range(3)]
    class_grads = jnp.concatenate(
        [both[0][0:sent] + both[0][sent:], both[1][0:sent] + both[1][sent:] + both[2][0:sent]], axis=0
    )
    per = extras.shape[1]
    for n in range(0, 320, 8):
        extras[n // per, n % per : n % per + 8] = class_grads[n : n + 8]
    row_sum = jnp.sum(dlogit, axis=0, keepdims=True)
    lines = (
        hidden_line[0],
        row_sum[:, 0:128],
        row_sum[:, 128:256],
        jnp.broadcast_to(jnp.sum(losses, axis=0, keepdims=True), (1, 128)),
    )
    for n, line in enumerate(lines):
        extras[320 // per, 320 % per + n : 320 % per + n + 1] = line
    extra_sends = []
    for r in range(1, groups):
        copy = pltpu.make_async_remote_copy(
            src_ref=extras.at[lax.rem(group + r, groups)],
            dst_ref=in_extras.at[r],
            send_sem=ssem.at[used + r - 1],
            recv_sem=rsem.at[used + r - 1],
            device_id=others[r - 1],
            device_id_type=MESH,
        )
        copy.start()
        extra_sends.append(copy)
    used += groups - 1

    for step in range(2, groups // 2):
        block_terms(step, *next(pre_spread))
    run_all(pre_spread)

    for copy in extra_sends:
        copy.wait_recv()
    total = extras[group]
    for r in range(1, groups):
        total = total + in_extras[r]
    sums_ref[x, y, width : width + per] = total
    for source in range(groups):

        @pl.when(source != group)
        def _():
            pltpu.make_async_remote_copy(
                src_ref=terms.at[0],
                dst_ref=in_terms.at[source],
                send_sem=ssem.at[term_base],
                recv_sem=rsem.at[term_base + source],
                device_id=(source, m),
                device_id_type=MESH,
            ).wait_recv()

    total = in_terms[0]
    for source in range(1, groups):
        total = total + in_terms[source]
    sums_ref[x, y, 0:width] = total
    spans = ((0, 0, 56), (1, 56, 64))
    last = grid_gather(sums_ref, spans, ssem, rsem, used, x, y, grid_device)
    used += 30
    for route in last:
        next(route)
    for copy in extra_sends:
        copy.wait_send()
    for k in range(groups):
        dest = dests[k]

        @pl.when(dest != group)
        def _():
            term_copy(k, dest, group).wait_send()

    run_all(*last)
    assert used <= SEMS


SEMS = 160


def finish_kernel(scale, hidden_ref, sums_ref, *outs):
    hidden_out, self_out, neigh_out, hb_out, cs_out, cn_out, cb_out, loss_out, lines = outs
    width = self_out.shape[0]
    hid = hidden_ref.shape[1]
    groups, rows = sums_ref.shape[:2]
    per = rows - width
    hidden_out[...] = hidden_ref[...]
    for n in range(groups):
        out = neigh_out if n % 2 else self_out
        at = n // 2 * hid
        out[:, at : at + hid] = sums_ref[n, 0:width, :]
        lines[n * per : n * per + per, :] = sums_ref[n, width:rows, :]
    classes = cs_out.shape[0]
    cs_out[...] = lines[0:classes, :]
    cn_out[...] = lines[160 : 160 + classes, :]
    hb_out[...] = lines[320:321, :]
    cb_out[:, 0:128] = lines[321:322, :]
    cb_out[:, 128:classes] = lines[322:323, 0 : classes - 128]
    loss_out[...] = lines[323:324, :] * scale


def body(
    node_features,
    target_nodes,
    first_hop,
    live_counts,
    seed_links,
    seed_labels,
    self_weight,
    neigh_weight,
    hidden_bias,
    class_self,
    class_neigh,
    class_bias,
):
    node_rows = node_features.shape[1]
    batches, targets = target_nodes.shape
    fan_one = first_hop.shape[1]
    seeds, fan_two = seed_links.shape[1:]
    hid = hidden_bias.shape[0]
    width, hidden_all = self_weight.shape
    classes = class_bias.shape[0]
    offset = (lax.axis_index("group") * node_rows).astype(jnp.int32)[None]
    parts = gather_rows(node_features, target_nodes, first_hop, offset).reshape(4, 4, 384, 128)
    f32, vmem = jnp.float32, pl.BlockSpec(memory_space=pltpu.VMEM)
    smem = pl.BlockSpec(memory_space=pltpu.SMEM)
    shapes = [
        ((4, 4, 384, 128), f32),
        ((4, 6, 4, 48, 128), f32),
        ((4, 3, 96, 128), f32),
        ((384, hidden_all), jnp.bfloat16),
        ((4, 2, targets, hid), f32),
        ((4, targets, hid), f32),
        ((2, 3, targets // 2, hid), f32),
        ((2, 256, 8 * hid), f32),
        ((2, 256, 8 * hid), jnp.bfloat16),
        ((256, 3 * hid), jnp.bfloat16),
        ((targets, 128), f32),
        ((targets, 128), f32),
        ((1, 256), f32),
        ((targets, 8 * hid), f32),
        ((seeds, 256), jnp.int32),
        ((targets, 128), f32),
        ((seeds, 256), f32),
        ((seeds, 256), f32),
        ((4, seeds, 256), f32),
        ((4, 2, targets, hid), f32),
        ((16, width, 128), f32),
        ((16, width, 128), f32),
        ((16, 24, 128), f32),
        ((16, 24, 128), f32),
    ]
    hidden_layer, sums = pl.pallas_call(
        functools.partial(exchange_kernel, fan_one, fan_two),
        out_shape=(
            jax.ShapeDtypeStruct((targets, hid), jnp.bfloat16),
            jax.ShapeDtypeStruct((4, 4, width + 24, 128), f32),
        ),
        in_specs=[pl.BlockSpec(memory_space=pl.ANY)] + [vmem] * 6 + [smem, vmem, smem],
        out_specs=(vmem, vmem),
        scratch_shapes=[pltpu.VMEM(shape, kind) for shape, kind in shapes]
        + [
            pltpu.SemaphoreType.DMA,
            pltpu.SemaphoreType.DMA((SEMS,)),
            pltpu.SemaphoreType.DMA((SEMS,)),
        ],
        compiler_params=pltpu.CompilerParams(
            collective_id=0, has_side_effects=True, vmem_limit_bytes=48 * 1024 * 1024
        ),
        name="exchange",
    )(
        parts,
        self_weight,
        neigh_weight,
        hidden_bias[None],
        class_self.T,
        class_neigh.T,
        class_bias[None],
        live_counts,
        jnp.transpose(seed_links, (2, 0, 1)),
        seed_labels,
    )
    outs = pl.pallas_call(
        functools.partial(finish_kernel, 1.0 / (batches * seeds)),
        out_shape=(
            jax.ShapeDtypeStruct((targets, hid), jnp.bfloat16),
            jax.ShapeDtypeStruct((width, hidden_all), f32),
            jax.ShapeDtypeStruct((width, hidden_all), f32),
            jax.ShapeDtypeStruct((1, hid), f32),
            jax.ShapeDtypeStruct((classes, hid), f32),
            jax.ShapeDtypeStruct((classes, hid), f32),
            jax.ShapeDtypeStruct((1, classes), f32),
            jax.ShapeDtypeStruct((1, 128), f32),
        ),
        in_specs=[vmem] * 2,
        out_specs=(vmem,) * 8,
        scratch_shapes=[pltpu.VMEM((16 * 24, 128), f32)],
        compiler_params=pltpu.CompilerParams(vmem_limit_bytes=8 * 1024 * 1024),
        name="finish",
    )(hidden_layer, sums.reshape(16, width + 24, 128))
    return (
        outs[0],
        outs[1],
        outs[2],
        outs[3][0],
        outs[4].T,
        outs[5].T,
        outs[6][0],
        outs[7][0, 0],
    )


def solution(mesh):
    in_specs = (
        P("mp", "group"),
        P(),
        P(),
        P("group"),
        P("group", None, None),
        P("group", None),
        P("mp", None),
        P("mp", None),
        P("mp"),
        P("mp", None),
        P("mp", None),
        P(),
    )
    out_specs = (
        P("group", "mp"),
        P("mp", None),
        P("mp", None),
        P("mp"),
        P("mp", None),
        P("mp", None),
        P(),
        P(),
    )
    return jax.shard_map(body, mesh=mesh, in_specs=in_specs, out_specs=out_specs, check_vma=False)
```
